256 devices in a mesh: dp: 32 (over y, x, core), tensor: 8 (over z).
Axes of the slice: x: 4, y: 4, z: 8, core: 2. Of those that a mesh axis runs over, the one named last changes fastest.
Arguments:
- patches: bfloat16 [49152, 1280], P('dp', 'tensor'), may hold values from -6 to 6
- gain: float32 [1280], replicated, may hold values from 0.25 to 1.75
- window_dest: int32 [768], P('dp'), may hold values from -1 to 31, as said below
- window_pos: int32 [768], P('dp'), may hold values from -1 to 16368, as said below
- fc1: bfloat16 [5120, 2560], P('dp', 'tensor'), may hold values from -0.078125 to 0.078125
- fc2: bfloat16 [2560, 8192], P('dp', 'tensor'), may hold values from -0.125 to 0.125
- text_embeds: bfloat16 [16384, 8192], P('dp', 'tensor'), may hold values from -6 to 6
- lm_grad: bfloat16 [16384, 8192], P('dp', 'tensor'), may hold values from -0.046875 to 0.046875
Outputs:
- lm_embeds: bfloat16 [16384, 8192], P('dp', 'tensor')
- grad_fc1: float32 [5120, 2560], P('dp', 'tensor')
- grad_fc2: float32 [2560, 8192], P('dp', 'tensor')
The draws below stay inside these ranges and needn't reach their ends.
Inputs may be any that keep to these rules, and one draw needn't show every extreme that they name: `window_dest`: live slots come first on each index of dp, which holds 8 or 24 of them. Every index of dp is named by exactly 16 live slots; the slots of one index of dp name one index at most 1 times, and some index of dp reaches that. `window_pos`: -1 exactly where window_dest is -1. The 16 rows from window_pos of a live slot lie in one block of 512 rows (one index of dp), never intersection another slot's rows, and every such block receives exactly 16 windows; at most 1 windows of one block share one value of window_dest, and some block reaches that.
All inputs are finite; a program needn't handle non-finite values.
Results may differ from the reference program's by a relative error of at most 0.029.
Values may be sent and summed in bfloat16 or wider, within the bound.
A program may use at most 128 MiB of HBM per device.

```python
import jax
import jax.numpy as jnp
from jax import lax

DM = 1280
DH = 5120
FFM = 2560
DOUT = 8192
WIN = 64
TOKW = 16
WORK_WIN = 16
SRC_WIN = 24
LM_DEV = 512
PATCHES = 49152
LM_TOKENS = 16384
N_DP = 32


def window_layout(key):
    key_order, key_turn, key_gaps = jax.random.split(key, 3)
    order = jax.random.permutation(key_order, N_DP)
    counts = jnp.where(order < N_DP // 2, 3 * WORK_WIN // 2, WORK_WIN // 2).astype(jnp.int32)
    firsts = (jnp.cumsum(counts) - counts).astype(jnp.int32)
    turn = jax.random.randint(key_turn, (), 0, N_DP).astype(jnp.int32)
    slot_ids = jnp.arange(SRC_WIN, dtype=jnp.int32)
    live = slot_ids[None, :] < counts[:, None]
    global_ids = jnp.where(live, firsts[:, None] + slot_ids[None, :], 0)
    dest = jnp.where(live, (global_ids + turn) % N_DP, -1)
    gaps = jax.random.randint(key_gaps, (N_DP, WORK_WIN), 0, TOKW + 1).astype(jnp.int32)
    starts = jnp.arange(WORK_WIN, dtype=jnp.int32)[None, :] * TOKW + jnp.cumsum(gaps, axis=1).astype(jnp.int32)
    starts = starts.at[:, WORK_WIN - 1].set(LM_DEV - TOKW)
    owner = global_ids // WORK_WIN
    within = global_ids % WORK_WIN
    rows = owner * LM_DEV + starts[owner, within]
    pos = jnp.where(live, rows, -1)
    return (dest.reshape(-1).astype(jnp.int32), pos.reshape(-1).astype(jnp.int32))


def draw_window_dest(key, part):
    return window_layout(key)[0]


def draw_window_pos(key, part):
    return window_layout(key)[1]


def steps_of(stream_key, dims, pieces, least, top_value):
    level, own = 1.0, jax.random.fold_in(stream_key, 6)
    for axis_at, parts in pieces:
        steps = jnp.exp(jax.random.uniform(jax.random.fold_in(own, axis_at), (parts,), jnp.float32, least / len(pieces), top_value / len(pieces)))
        level = level * jnp.repeat(steps, dims[axis_at] // parts).reshape([-1 if axis == axis_at else 1 for axis in range(len(dims))])
    return level


def scatter_about(own_key, dims, width, reach, shards=(), held_as=jnp.bfloat16):
    result = width * jax.random.normal(own_key, dims, jnp.float32)
    if shards:
        result = result * steps_of(own_key, dims, shards, -0.22, 0.18)
    return jnp.clip(result, -reach, reach).astype(held_as)


def setup_inputs(seed: int = 0) -> dict:
    arg_keys = jax.random.split(jax.random.key(seed), 9)
    return {
        "patches": scatter_about(arg_keys[0], (PATCHES, DM), 1.0, 6.0, ((0, 32), (1, 8))),
        "gain": jnp.clip(1.0 + 0.15 * jax.random.normal(arg_keys[1], (DM,), jnp.float32), 0.25, 1.75),
        "window_dest": draw_window_dest(jax.random.fold_in(arg_keys[8], 71), 0),
        "window_pos": draw_window_pos(jax.random.fold_in(arg_keys[8], 71), 0),
        "fc1": scatter_about(arg_keys[4], (DH, FFM), DH ** -0.5, 0.078125, ((0, 32), (1, 8))),
        "fc2": scatter_about(arg_keys[5], (FFM, DOUT), FFM ** -0.5, 0.125, ((0, 32), (1, 8))),
        "text_embeds": scatter_about(arg_keys[6], (LM_TOKENS, DOUT), 1.0, 6.0, ((0, 32), (1, 8))),
        "lm_grad": scatter_about(arg_keys[7], (LM_TOKENS, DOUT), (N_DP * LM_DEV) ** -0.5, 0.046875, ((0, 32), (1, 8))),
    }


def gelu_slope(z):
    cdf = 0.5 * (1.0 + lax.erf(z * 0.7071067811865476))
    pdf = jnp.exp(-0.5 * z * z) * 0.3989422804014327
    return cdf + z * pdf

def reference(patches, gain, window_dest, window_pos, fc1, fc2, text_embeds, lm_grad):
    slot_count = N_DP * SRC_WIN
    slot_ids = jnp.arange(slot_count, dtype=jnp.int32)
    sort_keys = jnp.where(window_dest >= 0, window_dest * slot_count + slot_ids, N_DP * slot_count + slot_ids)
    chosen = jnp.argsort(sort_keys)[:N_DP * WORK_WIN].astype(jnp.int32).reshape(N_DP, WORK_WIN)
    windows = patches.reshape(slot_count, WIN, DM)
    offsets = jnp.arange(TOKW, dtype=jnp.int32)

    def one_device(carry, picks):
        total_one, total_two = carry
        values = windows[picks].astype(jnp.float32)
        scale = lax.rsqrt(lax.optimization_barrier(jnp.mean(values * values, axis=-1, keepdims=True)) + 1e-06)
        normed = (values * scale * gain).astype(jnp.bfloat16).reshape(WORK_WIN * TOKW, DH)
        first = jnp.dot(normed, fc1, preferred_element_type=jnp.float32)
        hidden = jax.nn.gelu(first, approximate=False).astype(jnp.bfloat16)
        merged = jnp.dot(hidden, fc2, preferred_element_type=jnp.float32).astype(jnp.bfloat16)
        rows = (window_pos[picks][:, None] + offsets[None, :]).reshape(-1).astype(jnp.int32)
        upstream = lm_grad[rows]
        term_two = lax.dot_general(hidden, upstream, (((0,), (0,)), ((), ())), preferred_element_type=jnp.float32)
        term_two = lax.optimization_barrier(term_two.astype(jnp.bfloat16)).astype(jnp.float32)
        back = lax.dot_general(upstream, fc2, (((1,), (1,)), ((), ())), preferred_element_type=jnp.float32)
        slope = (back * gelu_slope(first)).astype(jnp.bfloat16)
        term_one = lax.dot_general(normed, slope, (((0,), (0,)), ((), ())), preferred_element_type=jnp.float32)
        term_one = lax.optimization_barrier(term_one.astype(jnp.bfloat16)).astype(jnp.float32)
        return ((total_one + term_one, total_two + term_two), (merged, rows))
    start = (jnp.zeros((DH, FFM), jnp.float32), jnp.zeros((FFM, DOUT), jnp.float32))
    (grad_fc1, grad_fc2), (merged_all, rows_all) = lax.scan(one_device, start, chosen)
    lm_embeds = text_embeds.at[rows_all.reshape(-1)].set(merged_all.reshape(-1, DOUT))
    return (lm_embeds, grad_fc1, grad_fc2)
```

```python
import functools

import jax
import jax.numpy as jnp
from jax import lax
from jax.experimental import pallas as pl
from jax.experimental.pallas import tpu as pltpu
from jax.sharding import PartitionSpec as P

MESH = pl.DeviceIdType.MESH
BF = jnp.bfloat16
F32 = jnp.float32
DM = 1280
NDP = 32
NZ = 8
SRC = 24
WORK = 16
TOK = 16
FEAT = 640
WIDE = 768
HID = 320
HPAD = 384
LM = 512
OUT = 1024
NTOK = WORK * TOK


def dot(a, b, da=1, db=0):
    return lax.dot_general(a, b, (((da,), (db,)), ((), ())), preferred_element_type=F32)


def iota(shape, axis):
    return lax.broadcasted_iota(jnp.int32, shape, axis)


def turn(v, k, n):
    return lax.rem(v + (k % n), n)


def add_into(target, *others):
    def body(i, carry):
        total = target[i].astype(F32)
        for o in others:
            total = total + o[i].astype(F32)
        target[i] = total.astype(BF)
        return carry

    lax.fori_loop(0, target.shape[0], body, 0)


class Half:
    def __init__(self, kind, h, y, x, c, t):
        self.kind, self.h, self.y, self.x, self.c, self.t = kind, h, y, x, c, t
        self.q = x if h == 0 else y
        self.r = y if h == 0 else x

    def dev(self, y, x, c):
        return (y * 8 + x * 2 + c, self.t)

    def first(self, k):
        if self.h == 0:
            return self.dev(self.y, turn(self.x, k, 4), self.c)
        return self.dev(turn(self.y, k, 4), self.x, self.c)

    def second(self, k):
        if self.h == 0:
            return self.dev(turn(self.y, k, 4), self.x, self.c)
        return self.dev(self.y, turn(self.x, k, 4), self.c)

    def sibling(self):
        return self.dev(self.y, self.x, 1 - self.c)

    def cut(self, s):
        if self.kind == 2:
            start = 512 * self.h + (256 if s == 1 else 0)
            return pl.ds(0, 80), pl.ds(start, 512 if s is None else 256)
        start = 80 * self.h + (48 if s == 1 else 0)
        return pl.ds(start, {None: 80, 0: 48, 1: 32}[s]), pl.ds(0, HID)

    def at(self, buf, y, x, c, s):
        rows, cols = self.cut(s)
        if self.kind == 2:
            return buf.at[y, x, c, rows, cols]
        return buf.at[x, c, y, rows, cols]

    def block(self, buf, k, s=None):
        p = turn(self.q, k, 4)
        if self.h == 0:
            return self.at(buf, self.y, p, self.c, s)
        return self.at(buf, p, self.x, self.c, s)

    def group(self, buf, k, s=None, other=False):
        p = turn(self.r, k, 4)
        c = 1 - self.c if other else self.c
        if self.h == 0:
            return self.at(buf, p, slice(None), c, s)
        return self.at(buf, slice(None), p, c, s)


class Mail:
    def __init__(self, send, recv):
        self.s, self.r, self.started = send, recv, []

    def make(self, src, dst, i, device):
        return pltpu.make_async_remote_copy(
            src_ref=src,
            dst_ref=dst,
            send_sem=self.s.at[i],
            recv_sem=self.r.at[i],
            device_id=device,
            device_id_type=MESH,
        )

    def send(self, src, dst, i, device):
        copy = self.make(src, dst, i, device)
        copy.start()
        self.started.append(copy)

    def wait(self, dst, i, device):
        self.make(dst, dst, i, device).wait_recv()

    def finish(self):
        for copy in self.started:
            copy.wait_send()
        self.started = []


def plane_gather(hf, buf, mail):
    def send(ref, i, device):
        mail.send(ref, ref, i, device)

    def wait(ref, i):
        mail.wait(ref, i, hf.sibling())

    send(hf.block(buf, 0), 0, hf.first(1))
    send(hf.block(buf, 0), 1, hf.first(-1))
    yield
    wait(hf.block(buf, -1), 0)
    send(hf.block(buf, -1, 0), 2, hf.first(1))
    wait(hf.block(buf, 1), 1)
    send(hf.block(buf, 1, 1), 3, hf.first(-1))
    yield
    wait(hf.block(buf, 2, 0), 2)
    wait(hf.block(buf, 2, 1), 3)
    send(hf.group(buf, 0), 4, hf.second(1))
    send(hf.group(buf, 0), 5, hf.second(-1))
    send(hf.group(buf, 0), 6, hf.sibling())
    yield
    wait(hf.group(buf, -1), 4)
    send(hf.group(buf, -1, 0), 7, hf.second(1))
    send(hf.group(buf, -1), 8, hf.sibling())
    wait(hf.group(buf, 1), 5)
    send(hf.group(buf, 1, 1), 9, hf.second(-1))
    send(hf.group(buf, 1), 10, hf.sibling())
    yield
    wait(hf.group(buf, 2, 0), 7)
    wait(hf.group(buf, 2, 1), 9)
    send(hf.group(buf, 2), 11, hf.sibling())
    yield
    for k, i in ((0, 6), (-1, 8), (1, 10), (2, 11)):
        wait(hf.group(buf, k, None, True), i)
    yield


def plane_scatter(hf, buf, room, mail, put):
    cores, sub0, sub1, full, last0, last1, last = room

    def wait(ref, i):
        mail.wait(ref, i, hf.sibling())

    for n, k in enumerate((2, 1, -1, 0)):
        mail.send(hf.group(buf, k, None, True), cores.at[n], n, hf.sibling())
    yield
    wait(cores.at[0], 0)
    add_into(hf.group(buf, 2), cores.at[0])
    mail.send(hf.group(buf, 2, 0), sub0, 4, hf.second(1))
    mail.send(hf.group(buf, 2, 1), sub1, 5, hf.second(-1))
    wait(cores.at[1], 1)
    add_into(hf.group(buf, 1), cores.at[1])
    wait(cores.at[2], 2)
    add_into(hf.group(buf, -1), cores.at[2])
    yield
    wait(sub0, 4)
    add_into(hf.group(buf, 1, 0), sub0)
    mail.send(hf.group(buf, 1), full.at[0], 6, hf.second(1))
    wait(sub1, 5)
    add_into(hf.group(buf, -1, 1), sub1)
    mail.send(hf.group(buf, -1), full.at[1], 7, hf.second(-1))
    wait(cores.at[3], 3)
    add_into(hf.group(buf, 0), cores.at[3])
    yield
    wait(full.at[0], 6)
    wait(full.at[1], 7)
    add_into(hf.group(buf, 0), full.at[0], full.at[1])
    mail.send(hf.block(buf, 2, 0), last0, 8, hf.first(1))
    mail.send(hf.block(buf, 2, 1), last1, 9, hf.first(-1))
    yield
    wait(last0, 8)
    near = hf.block(buf, 1, 0)
    near[...] = (near[...].astype(F32) + last0[...].astype(F32)).astype(BF)
    mail.send(hf.block(buf, 1), last.at[0], 10, hf.first(1))
    wait(last1, 9)
    near = hf.block(buf, -1, 1)
    near[...] = (near[...].astype(F32) + last1[...].astype(F32)).astype(BF)
    mail.send(hf.block(buf, -1), last.at[1], 11, hf.first(-1))
    yield
    wait(last.at[0], 10)
    wait(last.at[1], 11)
    put(
        hf.block(buf, 0)[...].astype(F32)
        + last[0].astype(F32)
        + last[1].astype(F32)
    )
    yield


def ring_gather(dp, t, buf, cuts, mail):
    up, down = (dp, turn(t, 1, NZ)), (dp, turn(t, -1, NZ))

    def view(k, cut):
        return buf.at[turn(t, k, NZ), cut, :]

    def send(k, cut, i, device):
        mail.send(view(k, cut), view(k, cut), i, device)

    def wait(k, cut, i):
        mail.wait(view(k, cut), i, up)

    for n, (whole, _, _) in enumerate(cuts):
        send(0, whole, (n, 0), up)
        send(0, whole, (n, 1), down)
    yield (0,)
    for k in (1, 2):
        for n, (whole, _, _) in enumerate(cuts):
            wait(-k, whole, (n, 2 * k - 2))
            send(-k, whole, (n, 2 * k), up)
            wait(k, whole, (n, 2 * k - 1))
            send(k, whole, (n, 2 * k + 1), down)
        yield (-k, k)
    for n, (whole, one, two) in enumerate(cuts):
        wait(-3, whole, (n, 4))
        send(-3, one, (n, 6), up)
        wait(3, whole, (n, 5))
        send(3, two, (n, 7), down)
    yield (-3, 3)
    for n, (_, one, two) in enumerate(cuts):
        wait(4, one, (n, 6))
        wait(4, two, (n, 7))
    yield (4,)


def ring_scatter(dp, t, buf, room, mail, put):
    up, down = (dp, turn(t, 1, NZ)), (dp, turn(t, -1, NZ))
    half = HID // 2
    low, high = pl.ds(0, half), pl.ds(half, half)

    def view(k, cut):
        return buf.at[turn(t, k, NZ), cut, :]

    def plus(k, cut, other):
        mine = view(k, cut)
        mine[...] = (mine[...].astype(F32) + other[...].astype(F32)).astype(BF)

    mail.send(view(4, low), room.at[0, low, :], 0, up)
    mail.send(view(4, high), room.at[1, high, :], 1, down)
    yield
    every = pl.ds(0, HID)
    for n, k in enumerate((3, 2, 1)):
        a, b = (low, high) if n == 0 else (every, every)
        mail.wait(room.at[2 * n, a, :], 2 * n, up)
        plus(k, a, room.at[2 * n, a, :])
        mail.send(view(k, every), room.at[2 * n + 2], 2 * n + 2, up)
        mail.wait(room.at[2 * n + 1, b, :], 2 * n + 1, up)
        plus(-k, b, room.at[2 * n + 1, b, :])
        mail.send(view(-k, every), room.at[2 * n + 3], 2 * n + 3, down)
        yield
    mail.wait(room.at[6], 6, up)
    mail.wait(room.at[7], 7, up)
    put(view(0, every)[...].astype(F32) + room[6].astype(F32) + room[7].astype(F32))
    yield


def body(
    win, gain, fc1, fc2, text, lmg,
    lm_out, g1_out, g2_out,
    sq, xn, st1, rv1, st2, rv2, xs, f1, f2, up_rows, place,
    acc, slope, hid, hb, hb_room, dz, mixed, p1, p2,
    a_cores, a_sub0, a_sub1, a_full, a_last0, a_last1, a_last,
    b_cores, b_sub, b_full, b_lasts, b_last,
    sq_s, sq_r, hop_s, hop_r, ag_s, ag_r, zx_s, zx_r, zh_s, zh_r, zb_s, zb_r, rs_s, rs_r,
):
    dp = lax.axis_index("dp")
    t = lax.axis_index("tensor")
    y, x, c = lax.div(dp, 8), lax.rem(lax.div(dp, 2), 4), lax.rem(dp, 2)

    barrier = pltpu.get_barrier_semaphore()

    def greet(k, carry):
        pl.semaphore_signal(
            barrier, inc=1, device_id=(lax.rem(dp + k, NDP), t), device_id_type=MESH
        )
        return carry

    lax.fori_loop(1, NDP, greet, 0)

    def greet_z(k, carry):
        pl.semaphore_signal(
            barrier, inc=1, device_id=(dp, lax.rem(t + k, NZ)), device_id_type=MESH
        )
        return carry

    lax.fori_loop(1, NZ, greet_z, 0)

    f2[y, x, c] = fc2[...]
    f1[x, c, y] = fc1[...]

    rows = SRC * TOK
    seg = iota((rows, FEAT), 1) // 160
    value = win[:, :FEAT].astype(F32)
    square = value * value
    lane = iota((rows, 128), 1)
    table = jnp.zeros((rows, 128), F32)
    for p in range(4):
        part = jnp.sum(jnp.where(seg == p, square, 0.0), axis=1, keepdims=True)
        table = jnp.where(lane == p, part, table)
    sq[t] = table.T[:8]

    pl.semaphore_wait(barrier, NDP - 1 + NZ - 1)

    def sq_copy(k, j):
        return pltpu.make_async_remote_copy(
            src_ref=sq.at[t], dst_ref=sq.at[t], send_sem=sq_s.at[k], recv_sem=sq_r.at[t],
            device_id=(dp, j), device_id_type=MESH,
        )

    def sq_wait(k):
        j = lax.rem(t + k, NZ)
        pltpu.make_async_remote_copy(
            src_ref=sq.at[j], dst_ref=sq.at[j], send_sem=sq_s.at[k], recv_sem=sq_r.at[j],
            device_id=(dp, j), device_id_type=MESH,
        ).wait_recv()

    for k in range(1, NZ):
        sq_copy(k, lax.rem(t + k, NZ)).start()

    halves = [Half(kind, h, y, x, c, t) for kind in (2, 1) for h in (0, 1)]
    ag_mail = [Mail(ag_s.at[n], ag_r.at[n]) for n in range(4)]
    gathers = [
        plane_gather(hf, f2 if hf.kind == 2 else f1, m) for hf, m in zip(halves, ag_mail)
    ]

    def step(generators):
        for g in generators:
            next(g)

    step(gathers)

    for k in range(1, NZ):
        sq_wait(k)
    total = jnp.sum(sq[...], axis=0)
    scale = lax.rsqrt(total * (1.0 / DM) + 1e-06)
    scale = jnp.concatenate([scale] * 16, axis=0).T
    spread = jnp.where(
        seg == 0,
        scale[:, 0:1],
        jnp.where(seg == 1, scale[:, 1:2], jnp.where(seg == 2, scale[:, 2:3], scale[:, 3:4])),
    )
    xn[:, :FEAT] = (win[:, :FEAT].astype(F32) * spread * gain[pl.ds(t, 1), :]).astype(BF)
    xn[:, FEAT:] = win[:, FEAT:]

    def facts(ref_rows):
        return ref_rows.astype(F32).T

    def pick(count, number, key, ok):
        n = key.shape[1]
        r, q = iota((count, n), 0), iota((count, n), 1)
        hit = (lax.div(r, TOK) == key) & (lax.rem(r, TOK) == lax.rem(q, TOK)) & (ok > 0.5)
        return jnp.where(hit, 1.0, 0.0).astype(BF)

    def hop_copy(n, src, dst, k):
        j = lax.rem(dp + k, NDP)
        return pltpu.make_async_remote_copy(
            src_ref=src.at[j], dst_ref=dst.at[dp], send_sem=hop_s.at[n, k], recv_sem=hop_r.at[n, dp],
            device_id=(j, t), device_id_type=MESH,
        )

    def hop_send(n, src, dst):
        def one(k, carry):
            hop_copy(n, src, dst, k).start()
            return carry

        lax.fori_loop(1, NDP, one, 0)
        dst[dp] = src[dp]

    def hop_wait(n, src, dst):
        def one(k, carry):
            j = lax.rem(dp + k, NDP)
            pltpu.make_async_remote_copy(
                src_ref=src.at[j], dst_ref=dst.at[j], send_sem=hop_s.at[n, k], recv_sem=hop_r.at[n, j],
                device_id=(j, t), device_id_type=MESH,
            ).wait_recv()
            return carry

        lax.fori_loop(1, NDP, one, 0)

    def hop_done(n, src, dst):
        def one(k, carry):
            hop_copy(n, src, dst, k).wait_send()
            return carry

        lax.fori_loop(1, NDP, one, 0)

    m = facts(xn[:, FEAT:])
    chosen = pick(NDP * TOK, None, m[3:4].astype(jnp.int32), m[0:1])
    st1[...] = dot(chosen, xn[...]).astype(BF).reshape(NDP, TOK, WIDE)
    hop_send(0, st1, rv1)
    step(gathers)

    hop_wait(0, st1, rv1)
    m = facts(rv1[:, :, FEAT:].reshape(NDP * TOK, 128))
    owner = lax.div(m[1:2].astype(jnp.int32), LM // 128)
    chosen = pick(NDP * TOK, None, owner, m[0:1])
    st2[...] = dot(chosen, rv1[...].reshape(NDP * TOK, WIDE)).astype(BF).reshape(NDP, TOK, WIDE)
    hop_send(1, st2, rv2)
    step(gathers)

    hop_wait(1, st2, rv2)
    m = facts(rv2[:, :, FEAT:].reshape(NDP * TOK, 128))
    n = NDP * TOK
    before = (lax.div(iota((n, n), 0), TOK) < lax.div(iota((n, n), 1), TOK)) & (
        lax.rem(iota((n, n), 0), TOK) == 0
    )
    live8 = jnp.broadcast_to(m[0:1], (16, n)).astype(BF)
    rank = dot(live8, jnp.where(before, 1.0, 0.0).astype(BF))[0:1]
    chosen = pick(NTOK, None, (rank + 0.5).astype(jnp.int32), m[0:1])
    work = dot(chosen, rv2[...].reshape(n, WIDE))
    xs[t] = work[:, :FEAT].astype(BF)

    zx_mail = Mail(zx_s, zx_r)
    zx = ring_gather(
        dp, t, xs,
        [(pl.ds(0, 128), pl.ds(0, 64), pl.ds(64, 64)), (pl.ds(128, 128), pl.ds(128, 64), pl.ds(192, 64))],
        zx_mail,
    )
    x_order = list(next(zx))

    base = dp * LM
    mcol = work[:, FEAT:]
    mrow = mcol.T
    tok_col = (mcol[:, 1:2] * 128.0 + mcol[:, 2:3] + 0.5).astype(jnp.int32) - base
    tok_row = (mrow[1:2] * 128.0 + mrow[2:3] + 0.5).astype(jnp.int32) - base
    fetch = jnp.where(iota((NTOK, LM), 1) == tok_col, 1.0, 0.0).astype(BF)
    place[...] = jnp.where(iota((LM, NTOK), 0) == tok_row, 1.0, 0.0).astype(BF)
    up_rows[...] = dot(fetch, lmg[...]).astype(BF)

    step(gathers)
    x_order += list(next(zx))
    step(gathers)
    x_order += list(next(zx))
    step(gathers)

    def second_rows(k):
        two = lax.rem(k, 2) * 2
        return f2[lax.div(k, 2), pl.ds(two, 2)].reshape(HID, OUT)

    def back(k, carry):
        hb[k] = dot(second_rows(k), up_rows[...], 1, 1).astype(BF)
        return carry

    lax.fori_loop(0, NZ, back, 0)

    zb_mail = Mail(zb_s, zb_r)

    def put_back(total):
        acc[:HID, :] = total

    zb = ring_scatter(dp, t, hb, hb_room, zb_mail, put_back)

    def first_part(k):
        j = turn(t, k, NZ)
        w = f1[lax.div(j, 2), lax.rem(j, 2)].reshape(FEAT, HID)
        return dot(xs[j], w)

    z1 = None
    for k in x_order:
        term = first_part(k)
        z1 = term if z1 is None else z1 + term
    for order in zx:
        for k in order:
            z1 = z1 + first_part(k)
    next(zb)
    z1 = jnp.concatenate([z1, jnp.zeros((NTOK, HPAD - HID), F32)], axis=1).T[:HID]
    cdf = 0.5 * (1.0 + lax.erf(z1 * 0.7071067811865476))
    hid[t] = (z1 * cdf).astype(BF)
    slope[...] = cdf + z1 * (jnp.exp(-0.5 * z1 * z1) * 0.3989422804014327)

    zh_mail = Mail(zh_s, zh_r)
    zh = ring_gather(dp, t, hid, [(pl.ds(0, 320), pl.ds(0, 160), pl.ds(160, 160))], zh_mail)
    mixed[...] = jnp.zeros_like(mixed)

    def use_hidden(k):
        j = turn(t, k, NZ)
        h = hid[j]
        mixed[...] += dot(h, second_rows(j), 0, 0)
        two = lax.rem(j, 2) * 2
        p2[lax.div(j, 2), pl.ds(two, 2)] = dot(h, up_rows[...]).astype(BF).reshape(2, 2, 80, OUT)

    for order in zh:
        for k in order:
            use_hidden(k)
        next(zb, None)

    rs_mail = [Mail(rs_s.at[n], rs_r.at[n]) for n in range(4)]

    def put2(h):
        def put(total):
            g2_out[:, 512 * h : 512 * h + 512] = total

        return put

    def put1(h):
        def put(total):
            g1_out[80 * h : 80 * h + 80, :] = total

        return put

    scatters = []
    for n, hf in enumerate(halves):
        h = hf.h
        if hf.kind == 2:
            room = (b_cores.at[h], b_sub.at[h, 0], b_sub.at[h, 1], b_full.at[h],
                    b_lasts.at[h, 0], b_lasts.at[h, 1], b_last.at[h])
            scatters.append(plane_scatter(hf, p2, room, rs_mail[n], put2(h)))
        else:
            room = (a_cores.at[h], a_sub0.at[h], a_sub1.at[h], a_full.at[h],
                    a_last0.at[h], a_last1.at[h], a_last.at[h])
            scatters.append(plane_scatter(hf, p1, room, rs_mail[n], put1(h)))
    step(scatters[:2])

    for _ in zb:
        pass
    dz_t = acc[:HID, :] * slope[...]
    dz[...] = jnp.concatenate([dz_t, jnp.zeros((HPAD - HID, NTOK), F32)], axis=0).T.astype(BF)

    def grad1(k, carry):
        term = dot(xs[k], dz[:, :HID], 0, 0).astype(BF)
        p1[lax.div(k, 2), lax.rem(k, 2)] = term.reshape(4, 160, HID)
        return carry

    lax.fori_loop(0, NZ, grad1, 0)
    step(scatters[2:])
    step(scatters[:2])

    merged = mixed[...].astype(BF)
    covered = jnp.max(place[...].astype(F32), axis=1, keepdims=True) > 0.5
    lm_out[...] = jnp.where(covered, dot(place[...], merged), text[...].astype(F32)).astype(BF)

    for _ in range(4):
        step(scatters[2:])
        step(scatters[:2])
    step(scatters[2:])

    for k in range(1, NZ):
        sq_copy(k, lax.rem(t + k, NZ)).wait_send()
    hop_done(0, st1, rv1)
    hop_done(1, st2, rv2)
    for m in ag_mail + rs_mail + [zx_mail, zh_mail, zb_mail]:
        m.finish()


def per_device(patches, gain, window_dest, window_pos, fc1, fc2, text_embeds, lm_grad):
    rows = SRC * TOK
    live = window_pos >= 0
    pos = jnp.where(live, window_pos, 0)[:, None] + jnp.arange(TOK, dtype=jnp.int32)[None, :]
    lane = jnp.arange(128, dtype=jnp.int32)[None, None, :]
    pos = pos[:, :, None]
    facts = jnp.where(
        lane == 0,
        live[:, None, None].astype(jnp.int32),
        jnp.where(
            lane == 1,
            pos // 128,
            jnp.where(lane == 2, pos % 128, jnp.where(lane == 3, window_dest[:, None, None], 0)),
        ),
    )
    win = jnp.concatenate(
        [patches.reshape(rows, FEAT), facts.astype(BF).reshape(rows, 128)], axis=1
    )
    gains = jnp.tile(gain.reshape(NZ, 160), (1, 4))
    vm = pl.BlockSpec(memory_space=pltpu.VMEM)
    V = pltpu.VMEM
    D = pltpu.SemaphoreType.DMA
    scratch = [
        V((NZ, 8, rows), F32),
        V((rows, WIDE), BF),
        V((NDP, TOK, WIDE), BF),
        V((NDP, TOK, WIDE), BF),
        V((NDP, TOK, WIDE), BF),
        V((NDP, TOK, WIDE), BF),
        V((NZ, NTOK, FEAT), BF),
        V((4, 2, 4, 160, HID), BF),
        V((4, 4, 2, 80, OUT), BF),
        V((NTOK, OUT), BF),
        V((LM, NTOK), BF),
        V((HID, NTOK), F32),
        V((HID, NTOK), F32),
        V((NZ, HID, NTOK), BF),
        V((NZ, HID, NTOK), BF),
        V((8, HID, NTOK), BF),
        V((NTOK, HPAD), BF),
        V((NTOK, OUT), F32),
        V((4, 2, 4, 160, HID), BF),
        V((4, 4, 2, 80, OUT), BF),
        V((2, 4, 4, 80, HID), BF),
        V((2, 4, 48, HID), BF),
        V((2, 4, 32, HID), BF),
        V((2, 2, 4, 80, HID), BF),
        V((2, 48, HID), BF),
        V((2, 32, HID), BF),
        V((2, 2, 80, HID), BF),
        V((2, 4, 4, 80, 512), BF),
        V((2, 2, 4, 80, 256), BF),
        V((2, 2, 4, 80, 512), BF),
        V((2, 2, 80, 256), BF),
        V((2, 2, 80, 512), BF),
        D((NZ,)), D((NZ,)),
        D((2, NDP)), D((2, NDP)),
        D((4, 12)), D((4, 12)),
        D((2, 8)), D((2, 8)),
        D((1, 8)), D((1, 8)),
        D((8,)), D((8,)),
        D((4, 12)), D((4, 12)),
    ]
    return pl.pallas_call(
        body,
        out_shape=(
            jax.ShapeDtypeStruct((LM, OUT), BF),
            jax.ShapeDtypeStruct((160, HID), F32),
            jax.ShapeDtypeStruct((80, OUT), F32),
        ),
        in_specs=[vm] * 6,
        out_specs=(vm, vm, vm),
        scratch_shapes=scratch,
        compiler_params=pltpu.CompilerParams(
            collective_id=0, has_side_effects=True, vmem_limit_bytes=60 * 1024 * 1024
        ),
        cost_estimate=pl.CostEstimate(
            flops=6_000_000_000, bytes_accessed=8_000_000, transcendentals=300_000
        ),
    )(win, gains, fc1, fc2, text_embeds, lm_grad)


def solution(mesh):
    both = P("dp", "tensor")
    return jax.shard_map(
        per_device,
        mesh=mesh,
        in_specs=(both, P(), P("dp"), P("dp"), both, both, both, both),
        out_specs=(both, both, both),
        check_vma=False,
    )
```

```python
import functools

import jax
import jax.numpy as jnp
from jax import lax
from jax.experimental import pallas as pl
from jax.experimental.pallas import tpu as pltpu
from jax.sharding import PartitionSpec as P

MESH = pl.DeviceIdType.MESH
BF = jnp.bfloat16
F32 = jnp.float32
DM = 1280
NDP = 32
NZ = 8
SRC = 24
WORK = 16
TOK = 16
FEAT = 640
WIN = 64
HID = 320
HPAD = 384
LM = 512
OUT = 1024
NTOK = WORK * TOK


def dot(a, b, da=1, db=0):
    return lax.dot_general(a, b, (((da,), (db,)), ((), ())), preferred_element_type=F32)


def iota(shape, axis):
    return lax.broadcasted_iota(jnp.int32, shape, axis)


def turn(v, k, n):
    return lax.rem(v + (k % n), n)


class Half:
    def __init__(self, kind, h, y, x, c, t):
        self.kind, self.h, self.y, self.x, self.c, self.t = kind, h, y, x, c, t
        self.q = x if h == 0 else y
        self.r = y if h == 0 else x

    def dev(self, y, x, c):
        return (y * 8 + x * 2 + c, self.t)

    def first(self, k):
        if self.h == 0:
            return self.dev(self.y, turn(self.x, k, 4), self.c)
        return self.dev(turn(self.y, k, 4), self.x, self.c)

    def second(self, k):
        if self.h == 0:
            return self.dev(turn(self.y, k, 4), self.x, self.c)
        return self.dev(self.y, turn(self.x, k, 4), self.c)

    def sibling(self):
        return self.dev(self.y, self.x, 1 - self.c)

    def cut(self, s):
        if self.kind == 2:
            start = 512 * self.h + (256 if s == 1 else 0)
            return pl.ds(0, 80), pl.ds(start, 512 if s is None else 256)
        start = 80 * self.h + (48 if s == 1 else 0)
        return pl.ds(start, {None: 80, 0: 48, 1: 32}[s]), pl.ds(0, HID)

    def at(self, buf, y, x, c, s):
        rows, cols = self.cut(s)
        if self.kind == 2:
            return buf.at[y, x, c, rows, cols]
        return buf.at[x, c, y, rows, cols]

    def block(self, buf, k, s=None):
        p = turn(self.q, k, 4)
        if self.h == 0:
            return self.at(buf, self.y, p, self.c, s)
        return self.at(buf, p, self.x, self.c, s)

    def cell(self, buf, g, b, s=None):
        p, q = turn(self.r, g, 4), turn(self.q, b, 4)
        if self.h == 0:
            return self.at(buf, p, q, self.c, s)
        return self.at(buf, q, p, self.c, s)

    def group(self, buf, k, s=None, other=False):
        p = turn(self.r, k, 4)
        c = 1 - self.c if other else self.c
        if self.h == 0:
            return self.at(buf, p, slice(None), c, s)
        return self.at(buf, slice(None), p, c, s)


class Mail:
    def __init__(self, send, recv):
        self.s, self.r, self.started = send, recv, []

    def make(self, src, dst, i, device):
        return pltpu.make_async_remote_copy(
            src_ref=src,
            dst_ref=dst,
            send_sem=self.s.at[i],
            recv_sem=self.r.at[i],
            device_id=device,
            device_id_type=MESH,
        )

    def send(self, src, dst, i, device):
        copy = self.make(src, dst, i, device)
        copy.start()
        self.started.append(copy)

    def wait(self, dst, i, device):
        self.make(dst, dst, i, device).wait_recv()

    def finish(self):
        for copy in self.started:
            copy.wait_send()
        self.started = []


def plane_gather(hf, buf, mail):
    def send(ref, i, device):
        mail.send(ref, ref, i, device)

    def wait(ref, i):
        mail.wait(ref, i, hf.sibling())

    send(hf.block(buf, 0), 0, hf.first(1))
    send(hf.block(buf, 0), 1, hf.first(-1))
    yield
    wait(hf.block(buf, -1), 0)
    send(hf.block(buf, -1, 0), 2, hf.first(1))
    wait(hf.block(buf, 1), 1)
    send(hf.block(buf, 1, 1), 3, hf.first(-1))
    yield
    wait(hf.block(buf, 2, 0), 2)
    wait(hf.block(buf, 2, 1), 3)
    send(hf.group(buf, 0), 4, hf.second(1))
    send(hf.group(buf, 0), 5, hf.second(-1))
    send(hf.group(buf, 0), 6, hf.sibling())
    yield
    wait(hf.group(buf, -1), 4)
    send(hf.group(buf, -1, 0), 7, hf.second(1))
    send(hf.group(buf, -1), 8, hf.sibling())
    wait(hf.group(buf, 1), 5)
    send(hf.group(buf, 1, 1), 9, hf.second(-1))
    send(hf.group(buf, 1), 10, hf.sibling())
    yield
    wait(hf.group(buf, 2, 0), 7)
    wait(hf.group(buf, 2, 1), 9)
    send(hf.group(buf, 2), 11, hf.sibling())
    yield
    for k, i in ((0, 6), (-1, 8), (1, 10), (2, 11)):
        wait(hf.group(buf, k, None, True), i)
    yield


def ring_sums(hf, buf, room, mail, put):
    sub0, sub1, full, last0, last1, last = room
    order = (2, 1, -1, 0)

    def wait(ref, i):
        mail.wait(ref, i, hf.sibling())

    def plus(mine, *others):
        total = mine[...].astype(F32)
        for o in others:
            total = total + o[...].astype(F32)
        mine[...] = total.astype(BF)

    for n, b in enumerate(order):
        mail.send(hf.cell(buf, 2, b, 0), sub0.at[n], n, hf.second(1))
        mail.send(hf.cell(buf, 2, b, 1), sub1.at[n], 4 + n, hf.second(-1))
    yield
    for n, b in enumerate(order):
        wait(sub0.at[n], n)
        plus(hf.cell(buf, 1, b, 0), sub0.at[n])
        mail.send(hf.cell(buf, 1, b), full.at[0, n], 8 + n, hf.second(1))
        wait(sub1.at[n], 4 + n)
        plus(hf.cell(buf, -1, b, 1), sub1.at[n])
        mail.send(hf.cell(buf, -1, b), full.at[1, n], 12 + n, hf.second(-1))
    yield
    for n in (0, 1, 2):
        wait(full.at[0, n], 8 + n)
        wait(full.at[1, n], 12 + n)
        plus(hf.cell(buf, 0, order[n]), full.at[0, n], full.at[1, n])
        if n == 0:
            mail.send(hf.block(buf, 2, 0), last0, 16, hf.first(1))
            mail.send(hf.block(buf, 2, 1), last1, 17, hf.first(-1))
    yield
    wait(last0, 16)
    plus(hf.block(buf, 1, 0), last0)
    mail.send(hf.block(buf, 1), last.at[0], 18, hf.first(1))
    wait(last1, 17)
    plus(hf.block(buf, -1, 1), last1)
    mail.send(hf.block(buf, -1), last.at[1], 19, hf.first(-1))
    yield
    wait(full.at[0, 3], 11)
    wait(full.at[1, 3], 15)
    wait(last.at[0], 18)
    wait(last.at[1], 19)
    total = hf.block(buf, 0)[...].astype(F32)
    for part in (full[0, 3], full[1, 3], last[0], last[1]):
        total = total + part.astype(F32)
    put(total)
    yield


def ring_gather(dp, t, buf, cuts, mail):
    up, down = (dp, turn(t, 1, NZ)), (dp, turn(t, -1, NZ))

    def view(k, cut):
        return buf.at[(turn(t, k, NZ),) + cut]

    def send(k, cut, i, device):
        mail.send(view(k, cut), view(k, cut), i, device)

    def wait(k, cut, i):
        mail.wait(view(k, cut), i, up)

    whole, one, two = cuts
    send(0, whole, 0, up)
    send(0, whole, 1, down)
    yield (0,)
    for k in (1, 2):
        wait(-k, whole, 2 * k - 2)
        send(-k, whole, 2 * k, up)
        wait(k, whole, 2 * k - 1)
        send(k, whole, 2 * k + 1, down)
        yield (-k, k)
    wait(-3, whole, 4)
    send(-3, one, 6, up)
    wait(3, whole, 5)
    send(3, two, 7, down)
    yield (-3, 3)
    wait(4, one, 6)
    wait(4, two, 7)
    yield (4,)


def ring_scatter(dp, t, buf, room, mail, put):
    up, down = (dp, turn(t, 1, NZ)), (dp, turn(t, -1, NZ))
    half = HID // 2
    low, high = pl.ds(0, half), pl.ds(half, half)

    def view(k, cut):
        return buf.at[turn(t, k, NZ), cut, :]

    def plus(k, cut, other):
        mine = view(k, cut)
        mine[...] = (mine[...].astype(F32) + other[...].astype(F32)).astype(BF)

    mail.send(view(4, low), room.at[0, low, :], 0, up)
    mail.send(view(4, high), room.at[1, high, :], 1, down)
    yield
    every = pl.ds(0, HID)
    for n, k in enumerate((3, 2, 1)):
        a, b = (low, high) if n == 0 else (every, every)
        mail.wait(room.at[2 * n, a, :], 2 * n, up)
        plus(k, a, room.at[2 * n, a, :])
        mail.send(view(k, every), room.at[2 * n + 2], 2 * n + 2, up)
        mail.wait(room.at[2 * n + 1, b, :], 2 * n + 1, up)
        plus(-k, b, room.at[2 * n + 1, b, :])
        mail.send(view(-k, every), room.at[2 * n + 3], 2 * n + 3, down)
        yield
    mail.wait(room.at[6], 6, up)
    mail.wait(room.at[7], 7, up)
    put(view(0, every)[...].astype(F32) + room[6].astype(F32) + room[7].astype(F32))
    yield


def body(
    patches_t, gain, dest, pos, fc1, fc2, text, lmg,
    lm_out, g1_out, g2_out,
    sq, meta, flat, st1, rv1, st2, rv2, xs, f1, f2, up_rows, place,
    acc, slope, hid, hb, hb_room, dz, mixed, p1, p2,
    a_cores, a_sub0, a_sub1, a_full, a_last0, a_last1, a_last,
    b_cores, b_sub, b_full, b_lasts, b_last,
    sq_s, sq_r, meta_s, meta_r, hop_s, hop_r, ag_s, ag_r, zx_s, zx_r, zh_s, zh_r, zb_s, zb_r,
    co_s, co_r, rs_s, rs_r,
):
    dp = lax.axis_index("dp")
    t = lax.axis_index("tensor")
    y, x, c = lax.div(dp, 8), lax.rem(lax.div(dp, 2), 4), lax.rem(dp, 2)
    sibling = (y * 8 + x * 2 + 1 - c, t)

    barrier = pltpu.get_barrier_semaphore()

    def greet(k, carry):
        pl.semaphore_signal(
            barrier, inc=1, device_id=(lax.rem(dp + k, NDP), t), device_id_type=MESH
        )
        return carry

    lax.fori_loop(1, NDP, greet, 0)

    def greet_z(k, carry):
        pl.semaphore_signal(
            barrier, inc=1, device_id=(dp, lax.rem(t + k, NZ)), device_id_type=MESH
        )
        return carry

    lax.fori_loop(1, NZ, greet_z, 0)

    r, q = iota((8, 128), 0), iota((8, 128), 1)
    table = jnp.full((8, 128), -1, jnp.int32)
    for s in range(SRC):
        table = jnp.where(q == s, jnp.where(r == 0, dest[s], pos[s]), table)
    meta[dp] = table

    value = patches_t[...].astype(F32)
    sq[t] = jnp.sum(value * value, axis=0, keepdims=True)
    f2[y, x, c] = fc2[...]
    f1[x, c, y] = fc1[...]

    pl.semaphore_wait(barrier, NDP - 1 + NZ - 1)

    def sq_copy(k, j, own):
        place_of = t if own else j
        return pltpu.make_async_remote_copy(
            src_ref=sq.at[place_of], dst_ref=sq.at[place_of], send_sem=sq_s.at[k], recv_sem=sq_r.at[place_of],
            device_id=(dp, j), device_id_type=MESH,
        )

    for k in range(1, NZ):
        sq_copy(k, lax.rem(t + k, NZ), True).start()

    def spread(copy):
        def start(k, carry):
            copy(k, lax.rem(dp + k, NDP), True).start()
            return carry

        def arrive(k, carry):
            copy(k, lax.rem(dp + k, NDP), False).wait_recv()
            return carry

        def sent(k, carry):
            copy(k, lax.rem(dp + k, NDP), True).wait_send()
            return carry

        return [functools.partial(lax.fori_loop, 1, NDP, f, 0) for f in (start, arrive, sent)]

    def meta_copy(k, j, own):
        place_of = dp if own else j
        return pltpu.make_async_remote_copy(
            src_ref=meta.at[place_of], dst_ref=meta.at[place_of], send_sem=meta_s.at[k], recv_sem=meta_r.at[place_of],
            device_id=(j, t), device_id_type=MESH,
        )

    meta_start, meta_arrive, meta_sent = spread(meta_copy)
    meta_start()

    halves = [Half(kind, h, y, x, c, t) for kind in (2, 1) for h in (0, 1)]
    ag_mail = [Mail(ag_s.at[n], ag_r.at[n]) for n in range(4)]
    gathers = [
        plane_gather(hf, f2 if hf.kind == 2 else f1, m) for hf, m in zip(halves, ag_mail)
    ]

    def step(generators):
        for g in generators:
            next(g)

    step(gathers)

    chunks = (pl.ds(0, 256), pl.ds(256, 384))

    def hop_copy(n, m, src, dst, k, j, own):
        cols = chunks[m]
        return pltpu.make_async_remote_copy(
            src_ref=src.at[j, :, cols],
            dst_ref=dst.at[dp if own else j, :, cols],
            send_sem=hop_s.at[n, m, k],
            recv_sem=hop_r.at[n, m, dp if own else j],
            device_id=(j, t),
            device_id_type=MESH,
        )

    hops = [
        [spread(functools.partial(hop_copy, n, m, src, dst)) for m in (0, 1)]
        for n, (src, dst) in enumerate(((st1, rv1), (st2, rv2)))
    ]

    def hop_send(n, m, value):
        src, dst = ((st1, rv1), (st2, rv2))[n]
        src[:, :, chunks[m]] = value.astype(BF).reshape(NDP, TOK, chunks[m].size)
        hops[n][m][0]()
        dst[dp, :, chunks[m]] = src[dp, :, chunks[m]]

    def selector(count, key):
        n = key.shape[1]
        r, q = iota((count, n), 0), iota((count, n), 1)
        hit = ((r >> 4).astype(F32) == key) & ((r & 15) == (q & 15))
        return jnp.where(hit, 1.0, 0.0).astype(BF)

    def widen(column, n):
        k = column.shape[0]
        return jnp.sum(
            jnp.where(iota((k, n), 0) == (iota((k, n), 1) >> 4), column, 0.0), axis=0, keepdims=True
        )

    slots = jnp.sum(
        jnp.where(iota((32, 128), 0) == iota((32, 128), 1), table[0:1].astype(F32), 0.0),
        axis=1,
        keepdims=True,
    )
    to_dest = selector(NDP * TOK, widen(slots, SRC * TOK))
    factor = jnp.sum(
        jnp.where(iota((160, DM), 1) == iota((160, DM), 0) + t * 160, gain[...], 0.0),
        axis=1,
        keepdims=True,
    )
    for k in range(1, NZ):
        sq_copy(k, lax.rem(t + k, NZ), False).wait_recv()
    scale = lax.rsqrt(jnp.sum(sq[...], axis=0) * (1.0 / DM) + 1e-06)
    normed = (patches_t[...].astype(F32) * scale * factor).astype(BF).astype(F32)
    flat[0] = normed[:128].T
    flat[1] = jnp.concatenate([normed[128:], jnp.zeros((96, SRC * WIN), F32)], axis=0).T
    pieces = []
    for p in range(4):
        pieces.append(flat[0, pl.ds(p, SRC * TOK, stride=4), :])
        pieces.append(flat[1, pl.ds(p, SRC * TOK, stride=4), :][:, :32])
    windows = jnp.concatenate(pieces, axis=1).astype(BF)
    hop_send(0, 0, dot(to_dest, windows[:, :256]))
    hop_send(0, 1, dot(to_dest, windows[:, 256:]))
    step(gathers)

    meta_arrive()
    dests, places = meta[:, 0, :], meta[:, 1, :]
    owners = places >> 9
    onward = (
        jnp.sum(jnp.where(dests == dp, (owners + 1).astype(F32), 0.0), axis=1, keepdims=True) - 1.0
    )
    to_owner = selector(NDP * TOK, widen(onward, NDP * TOK))
    via = jnp.where(owners == dp, dests, -1)
    next_place = (places + 1).astype(F32)
    r, q = iota((32, 128), 0), iota((32, 128), 1)
    found = jnp.zeros((32, 128), F32)
    for d in range(NDP):
        found = jnp.where(
            r == d, jnp.sum(jnp.where(via == d, next_place, 0.0), axis=0, keepdims=True), found
        )
    found = jnp.sum(found, axis=1, keepdims=True)
    live = jnp.where(found > 0.5, 1.0, 0.0)
    live_row = jnp.sum(jnp.where(r == q, live, 0.0), axis=0, keepdims=True)
    rank = jnp.sum(jnp.where(q < r, live_row, 0.0), axis=1, keepdims=True)
    rank = jnp.where(found > 0.5, rank, -1.0)
    rank_row = jnp.sum(jnp.where(r == q, rank, 0.0), axis=0, keepdims=True)
    rank_row = jnp.where(iota((1, 128), 1) < NDP, rank_row, -1.0)
    found_row = jnp.sum(jnp.where(r == q, found, 0.0), axis=0, keepdims=True)
    to_work = selector(NTOK, widen(rank, NDP * TOK))

    base = dp * LM + 1
    r, q = iota((32, NTOK), 0), iota((32, NTOK), 1)
    tok_row = jnp.sum(jnp.where(rank == (q >> 4).astype(F32), found, 0.0), axis=0, keepdims=True)
    tok_row = tok_row.astype(jnp.int32) + (iota((1, NTOK), 1) & 15) - base
    r = iota((NTOK, 128), 0)
    tok_col = jnp.sum(
        jnp.where(rank_row == (r >> 4).astype(F32), found_row, 0.0), axis=1, keepdims=True
    )
    tok_col = tok_col.astype(jnp.int32) + (iota((NTOK, 1), 0) & 15) - base
    fetch = jnp.where(iota((NTOK, LM), 1) == tok_col, 1.0, 0.0).astype(BF)
    place[...] = jnp.where(iota((LM, NTOK), 0) == tok_row, 1.0, 0.0).astype(BF)

    for m in (0, 1):
        hops[0][m][1]()
        part = rv1[:, :, chunks[m]].reshape(NDP * TOK, chunks[m].size)
        hop_send(1, m, dot(to_owner, part))
    step(gathers)
    up_rows[...] = dot(fetch, lmg[...]).astype(BF)

    low, high, every = pl.ds(0, 128), pl.ds(128, 128), pl.ds(0, 256)
    zx_mail = [Mail(zx_s.at[m], zx_r.at[m]) for m in (0, 1)]
    zx = []
    for m, cols in enumerate(chunks):
        hops[1][m][1]()
        part = rv2[:, :, cols].reshape(NDP * TOK, cols.size)
        xs[t, :, cols] = dot(to_work, part).astype(BF)
        zx.append(
            ring_gather(dp, t, xs, ((every, cols), (low, cols), (high, cols)), zx_mail[m])
        )
        next(zx[m])
    x_order = [0]
    for _ in range(3):
        step(zx[:1])
        x_order += list(next(zx[1]))
        step(gathers)

    def second_rows(k):
        two = lax.rem(k, 2) * 2
        return f2[lax.div(k, 2), pl.ds(two, 2)].reshape(HID, OUT)

    def back(k, carry):
        hb[k] = dot(second_rows(k), up_rows[...], 1, 1).astype(BF)
        return carry

    lax.fori_loop(0, NZ, back, 0)

    zb_mail = Mail(zb_s, zb_r)

    def put_back(total):
        acc[:HID, :] = total

    zb = ring_scatter(dp, t, hb, hb_room, zb_mail, put_back)
    next(zb)

    def first_part(k):
        j = turn(t, k, NZ)
        w = f1[lax.div(j, 2), lax.rem(j, 2)].reshape(FEAT, HID)
        return dot(xs[j], w)

    z1 = None
    for k in x_order:
        term = first_part(k)
        z1 = term if z1 is None else z1 + term
    step(zx)
    z1 = z1 + first_part(4)
    z1 = jnp.concatenate([z1, jnp.zeros((NTOK, HPAD - HID), F32)], axis=1).T[:HID]
    cdf = 0.5 * (1.0 + lax.erf(z1 * 0.7071067811865476))
    hid[t] = (z1 * cdf).astype(BF)

    zh_mail = Mail(zh_s, zh_r)
    zh = ring_gather(
        dp, t, hid, ((pl.ds(0, 320), every), (pl.ds(0, 160), every), (pl.ds(160, 160), every)), zh_mail
    )
    core_mail = Mail(co_s, co_r)
    sent = []

    def use_hidden(k):
        j = turn(t, k, NZ)
        h = hid[j]
        yy, two = lax.div(j, 2), pl.ds(lax.rem(j, 2) * 2, 2)
        p2[yy, two] = dot(h, up_rows[...]).astype(BF).reshape(2, 2, 80, OUT)
        core_mail.send(p2.at[yy, two, 1 - c], b_cores.at[yy, two], len(sent), sibling)
        sent.append((yy, two))
        term = dot(h, second_rows(j), 0, 0)
        if k == 0:
            mixed[...] = term
        else:
            mixed[...] += term

    summed = []

    def join_cores():
        while len(summed) < len(sent):
            yy, two = sent[len(summed)]
            core_mail.wait(b_cores.at[yy, two], len(summed), sibling)
            mine = p2.at[yy, two, c]
            mine[...] = (mine[...].astype(F32) + b_cores[yy, two].astype(F32)).astype(BF)
            summed.append(yy)

    order = next(zh)
    slope[...] = cdf + z1 * (jnp.exp(-0.5 * z1 * z1) * 0.3989422804014327)
    next(zb)
    for k in order:
        use_hidden(k)
    for order in zh:
        next(zb, None)
        join_cores()
        for k in order:
            use_hidden(k)

    rs_mail = [Mail(rs_s.at[n], rs_r.at[n]) for n in range(4)]

    def put2(h):
        def put(total):
            g2_out[:, 512 * h : 512 * h + 512] = total

        return put

    def put1(h):
        def put(total):
            g1_out[80 * h : 80 * h + 80, :] = total

        return put

    sums = []
    for n, hf in enumerate(halves):
        h = hf.h
        if hf.kind == 2:
            room = (b_sub.at[h, 0], b_sub.at[h, 1], b_full.at[h],
                    b_lasts.at[h, 0], b_lasts.at[h, 1], b_last.at[h])
            sums.append(ring_sums(hf, p2, room, rs_mail[n], put2(h)))
        else:
            room = (a_sub0.at[h], a_sub1.at[h], a_full.at[h],
                    a_last0.at[h], a_last1.at[h], a_last.at[h])
            sums.append(ring_sums(hf, p1, room, rs_mail[n], put1(h)))
    join_cores()
    step(sums[:2])

    for _ in zb:
        pass
    dz_t = acc[:HID, :] * slope[...]
    dz[...] = jnp.concatenate([dz_t, jnp.zeros((HPAD - HID, NTOK), F32)], axis=0).T.astype(BF)

    def grad1(xx, cc):
        term = dot(xs[xx * 2 + cc], dz[:, :HID], 0, 0).astype(BF)
        p1[xx, cc] = term.reshape(4, 160, HID)

    for xx in range(4):
        grad1(xx, 1 - c)
        core_mail.send(p1.at[xx, 1 - c], a_cores.at[xx], 8 + xx, sibling)
    for xx in range(4):
        grad1(xx, c)
        core_mail.wait(a_cores.at[xx], 8 + xx, sibling)
        mine = p1.at[xx, c]
        mine[...] = (mine[...].astype(F32) + a_cores[xx].astype(F32)).astype(BF)
    step(sums[2:])
    step(sums[:2])

    merged = mixed[...].astype(BF)
    covered = jnp.max(place[...].astype(F32), axis=1, keepdims=True) > 0.5
    lm_out[...] = jnp.where(covered, dot(place[...], merged), text[...].astype(F32)).astype(BF)

    for _ in range(3):
        step(sums[2:])
        step(sums[:2])
    step(sums[2:])

    for k in range(1, NZ):
        sq_copy(k, lax.rem(t + k, NZ), True).wait_send()
    meta_sent()
    for n in (0, 1):
        for m in (0, 1):
            hops[n][m][2]()
    for m in ag_mail + rs_mail + zx_mail + [zh_mail, zb_mail, core_mail]:
        m.finish()


def per_device(patches, gain, window_dest, window_pos, fc1, fc2, text_embeds, lm_grad):
    vm = pl.BlockSpec(memory_space=pltpu.VMEM)
    sm = pl.BlockSpec(memory_space=pltpu.SMEM)
    V = pltpu.VMEM
    D = pltpu.SemaphoreType.DMA
    scratch = [
        V((NZ, 1, SRC * WIN), F32),
        V((NDP, 8, 128), jnp.int32),
        V((2, SRC * WIN, 128), F32),
        V((NDP, TOK, FEAT), BF),
        V((NDP, TOK, FEAT), BF),
        V((NDP, TOK, FEAT), BF),
        V((NDP, TOK, FEAT), BF),
        V((NZ, NTOK, FEAT), BF),
        V((4, 2, 4, 160, HID), BF),
        V((4, 4, 2, 80, OUT), BF),
        V((NTOK, OUT), BF),
        V((LM, NTOK), BF),
        V((HID, NTOK), F32),
        V((HID, NTOK), F32),
        V((NZ, HID, NTOK), BF),
        V((NZ, HID, NTOK), BF),
        V((8, HID, NTOK), BF),
        V((NTOK, HPAD), BF),
        V((NTOK, OUT), F32),
        V((4, 2, 4, 160, HID), BF),
        V((4, 4, 2, 80, OUT), BF),
        V((4, 4, 160, HID), BF),
        V((2, 4, 48, HID), BF),
        V((2, 4, 32, HID), BF),
        V((2, 2, 4, 80, HID), BF),
        V((2, 48, HID), BF),
        V((2, 32, HID), BF),
        V((2, 2, 80, HID), BF),
        V((4, 4, 80, OUT), BF),
        V((2, 2, 4, 80, 256), BF),
        V((2, 2, 4, 80, 512), BF),
        V((2, 2, 80, 256), BF),
        V((2, 2, 80, 512), BF),
        D((NZ,)), D((NZ,)),
        D((NDP,)), D((NDP,)),
        D((2, 2, NDP)), D((2, 2, NDP)),
        D((4, 12)), D((4, 12)),
        D((2, 8)), D((2, 8)),
        D((8,)), D((8,)),
        D((8,)), D((8,)),
        D((12,)), D((12,)),
        D((4, 20)), D((4, 20)),
    ]
    return pl.pallas_call(
        body,
        out_shape=(
            jax.ShapeDtypeStruct((LM, OUT), BF),
            jax.ShapeDtypeStruct((160, HID), F32),
            jax.ShapeDtypeStruct((80, OUT), F32),
        ),
        in_specs=[vm, vm, sm, sm, vm, vm, vm, vm],
        out_specs=(vm, vm, vm),
        scratch_shapes=scratch,
        compiler_params=pltpu.CompilerParams(
            collective_id=0, has_side_effects=True, vmem_limit_bytes=60 * 1024 * 1024
        ),
        cost_estimate=pl.CostEstimate(
            flops=6_000_000_000, bytes_accessed=8_000_000, transcendentals=300_000
        ),
    )(patches.T, gain.reshape(1, DM), window_dest, window_pos, fc1, fc2, text_embeds, lm_grad)


def solution(mesh):
    both = P("dp", "tensor")
    return jax.shard_map(
        per_device,
        mesh=mesh,
        in_specs=(both, P(), P("dp"), P("dp"), both, both, both, both),
        out_specs=(both, both, both),
        check_vma=False,
    )
```

```python
import functools

import jax
import jax.numpy as jnp
from jax import lax
from jax.experimental import pallas as pl
from jax.experimental.pallas import tpu as pltpu
from jax.sharding import PartitionSpec as P

MESH = pl.DeviceIdType.MESH
BF = jnp.bfloat16
F32 = jnp.float32
DM = 1280
NDP = 32
NZ = 8
SRC = 24
WORK = 16
TOK = 16
FEAT = 640
WIN = 64
HID = 320
HPAD = 384
LM = 512
OUT = 1024
NTOK = WORK * TOK


def dot(a, b, da=1, db=0):
    return lax.dot_general(a, b, (((da,), (db,)), ((), ())), preferred_element_type=F32)


def iota(shape, axis):
    return lax.broadcasted_iota(jnp.int32, shape, axis)


def turn(v, k, n):
    return lax.rem(v + (k % n), n)


class Half:
    def __init__(self, kind, h, y, x, c, t):
        self.kind, self.h, self.y, self.x, self.c, self.t = kind, h, y, x, c, t
        self.q = x if h == 0 else y
        self.r = y if h == 0 else x

    def dev(self, y, x, c):
        return (y * 8 + x * 2 + c, self.t)

    def first(self, k):
        if self.h == 0:
            return self.dev(self.y, turn(self.x, k, 4), self.c)
        return self.dev(turn(self.y, k, 4), self.x, self.c)

    def second(self, k):
        if self.h == 0:
            return self.dev(turn(self.y, k, 4), self.x, self.c)
        return self.dev(self.y, turn(self.x, k, 4), self.c)

    def sibling(self):
        return self.dev(self.y, self.x, 1 - self.c)

    def cut(self, s):
        if self.kind == 2:
            start = 512 * self.h + (256 if s == 1 else 0)
            return pl.ds(0, 80), pl.ds(start, 512 if s is None else 256)
        start = 80 * self.h + (48 if s == 1 else 0)
        return pl.ds(start, {None: 80, 0: 48, 1: 32}[s]), pl.ds(0, HID)

    def at(self, buf, y, x, c, s):
        rows, cols = self.cut(s)
        if self.kind == 2:
            return buf.at[y, x, c, rows, cols]
        return buf.at[x, c, y, rows, cols]

    def block(self, buf, k, s=None):
        p = turn(self.q, k, 4)
        if self.h == 0:
            return self.at(buf, self.y, p, self.c, s)
        return self.at(buf, p, self.x, self.c, s)

    def cell(self, buf, g, b, s=None):
        p, q = turn(self.r, g, 4), turn(self.q, b, 4)
        if self.h == 0:
            return self.at(buf, p, q, self.c, s)
        return self.at(buf, q, p, self.c, s)

    def group(self, buf, k, s=None, other=False):
        p = turn(self.r, k, 4)
        c = 1 - self.c if other else self.c
        if self.h == 0:
            return self.at(buf, p, slice(None), c, s)
        return self.at(buf, slice(None), p, c, s)


class Mail:
    def __init__(self, pool, first, recv):
        self.pool, self.next, self.r, self.started = pool, first, recv, []

    def make(self, src, dst, send, i, device):
        return pltpu.make_async_remote_copy(
            src_ref=src,
            dst_ref=dst,
            send_sem=self.pool.at[send],
            recv_sem=self.r.at[i],
            device_id=device,
            device_id_type=MESH,
        )

    def send(self, src, dst, i, device):
        copy = self.make(src, dst, self.next, i, device)
        copy.start()
        self.next += 1
        self.started.append(copy)

    def wait(self, dst, i, device):
        self.make(dst, dst, 0, i, device).wait_recv()

    def finish(self):
        for copy in self.started:
            copy.wait_send()
        self.started = []


def plane_gather(hf, buf, mail):
    def send(ref, i, device):
        mail.send(ref, ref, i, device)

    def wait(ref, i):
        mail.wait(ref, i, hf.sibling())

    send(hf.block(buf, 0), 0, hf.first(1))
    send(hf.block(buf, 0), 1, hf.first(-1))
    yield
    wait(hf.block(buf, -1), 0)
    send(hf.block(buf, -1, 0), 2, hf.first(1))
    wait(hf.block(buf, 1), 1)
    send(hf.block(buf, 1, 1), 3, hf.first(-1))
    yield
    wait(hf.block(buf, 2, 0), 2)
    wait(hf.block(buf, 2, 1), 3)
    send(hf.group(buf, 0), 4, hf.second(1))
    send(hf.group(buf, 0), 5, hf.second(-1))
    send(hf.group(buf, 0), 6, hf.sibling())
    yield
    wait(hf.group(buf, -1), 4)
    send(hf.group(buf, -1, 0), 7, hf.second(1))
    send(hf.group(buf, -1), 6, hf.sibling())
    wait(hf.group(buf, 1), 5)
    send(hf.group(buf, 1, 1), 8, hf.second(-1))
    send(hf.group(buf, 1), 6, hf.sibling())
    yield
    wait(hf.group(buf, 2, 0), 7)
    wait(hf.group(buf, 2, 1), 8)
    send(hf.group(buf, 2), 6, hf.sibling())
    yield
    wait(hf.at(buf, slice(None), slice(None), 1 - hf.c, None), 6)
    yield


def ring_sums(hf, buf, room, mail, put):
    sub0, sub1, full, last0, last1, last = room
    order = (2, 1, -1, 0)

    def wait(ref, i):
        mail.wait(ref, i, hf.sibling())

    def plus(mine, *others):
        total = mine[...].astype(F32)
        for o in others:
            total = total + o[...].astype(F32)
        mine[...] = total.astype(BF)

    for n, b in enumerate(order):
        mail.send(hf.cell(buf, 2, b, 0), sub0.at[n], n, hf.second(1))
        mail.send(hf.cell(buf, 2, b, 1), sub1.at[n], 4 + n, hf.second(-1))
    yield
    for n, b in enumerate(order):
        wait(sub0.at[n], n)
        plus(hf.cell(buf, 1, b, 0), sub0.at[n])
        mail.send(hf.cell(buf, 1, b), full.at[0, n], 8 + n, hf.second(1))
        wait(sub1.at[n], 4 + n)
        plus(hf.cell(buf, -1, b, 1), sub1.at[n])
        mail.send(hf.cell(buf, -1, b), full.at[1, n], 12 + n, hf.second(-1))
    yield
    for n in (0, 1, 2):
        wait(full.at[0, n], 8 + n)
        wait(full.at[1, n], 12 + n)
        plus(hf.cell(buf, 0, order[n]), full.at[0, n], full.at[1, n])
        if n == 0:
            mail.send(hf.block(buf, 2, 0), last0, 16, hf.first(1))
            mail.send(hf.block(buf, 2, 1), last1, 17, hf.first(-1))
    yield
    wait(last0, 16)
    plus(hf.block(buf, 1, 0), last0)
    mail.send(hf.block(buf, 1), last.at[0], 18, hf.first(1))
    wait(last1, 17)
    plus(hf.block(buf, -1, 1), last1)
    mail.send(hf.block(buf, -1), last.at[1], 19, hf.first(-1))
    yield
    wait(full.at[0, 3], 11)
    wait(full.at[1, 3], 15)
    wait(last.at[0], 18)
    wait(last.at[1], 19)
    total = hf.block(buf, 0)[...].astype(F32)
    for part in (full[0, 3], full[1, 3], last[0], last[1]):
        total = total + part.astype(F32)
    put(total)
    yield


def ring_gather(dp, t, buf, cuts, mail):
    up, down = (dp, turn(t, 1, NZ)), (dp, turn(t, -1, NZ))

    def view(k, cut):
        return buf.at[(turn(t, k, NZ),) + cut]

    def send(k, cut, i, device):
        mail.send(view(k, cut), view(k, cut), i, device)

    def wait(k, cut, i):
        mail.wait(view(k, cut), i, up)

    whole, one, two = cuts
    send(0, whole, 0, up)
    send(0, whole, 1, down)
    yield (0,)
    for k in (1, 2):
        wait(-k, whole, 2 * k - 2)
        send(-k, whole, 2 * k, up)
        wait(k, whole, 2 * k - 1)
        send(k, whole, 2 * k + 1, down)
        yield (-k, k)
    wait(-3, whole, 4)
    send(-3, one, 6, up)
    wait(3, whole, 5)
    send(3, two, 7, down)
    yield (-3, 3)
    wait(4, one, 6)
    wait(4, two, 7)
    yield (4,)


def ring_scatter(dp, t, buf, room, cols, mail, put):
    up, down = (dp, turn(t, 1, NZ)), (dp, turn(t, -1, NZ))
    half = HID // 2
    low, high, every = pl.ds(0, half), pl.ds(half, half), pl.ds(0, HID)

    def view(k, cut):
        return buf.at[turn(t, k, NZ), cut, cols]

    def plus(k, cut, other):
        mine = view(k, cut)
        mine[...] = (mine[...].astype(F32) + other[...].astype(F32)).astype(BF)

    mail.send(view(4, low), room.at[0, low, cols], 0, up)
    mail.send(view(4, high), room.at[1, high, cols], 1, down)
    yield
    for n, k in enumerate((3, 2, 1)):
        a, b = (low, high) if n == 0 else (every, every)
        mail.wait(room.at[2 * n, a, cols], 2 * n, up)
        plus(k, a, room.at[2 * n, a, cols])
        mail.send(view(k, every), room.at[2 * n + 2, every, cols], 2 * n + 2, up)
        mail.wait(room.at[2 * n + 1, b, cols], 2 * n + 1, up)
        plus(-k, b, room.at[2 * n + 1, b, cols])
        mail.send(view(-k, every), room.at[2 * n + 3, every, cols], 2 * n + 3, down)
        yield
    mail.wait(room.at[6, every, cols], 6, up)
    mail.wait(room.at[7, every, cols], 7, up)
    put(
        view(0, every)[...].astype(F32)
        + room[6, :, cols].astype(F32)
        + room[7, :, cols].astype(F32)
    )
    yield


def body(
    patches_t, gain, dest, pos, fc1, fc2, text_hbm, lmg_hbm,
    lm_hbm, g1_out, g2_out,
    text, lmg, lm_out, io_s,
    sq, meta, gains, factor, xn, flat, st1, rv1, st2, rv2, xs, f1, f2, up_rows, place,
    acc, hid, hb, hb_room, dz, mixed, p1, p2,
    a_cores, a_sub0, a_sub1, a_full, a_last0, a_last1, a_last,
    b_cores, b_sub, b_full, b_lasts, b_last,
    pool, sq_s, meta_s, hop_s, ag_r, zx_r, zh_r, zb_r, co_r, rs_r,
):
    dp = lax.axis_index("dp")
    t = lax.axis_index("tensor")
    y, x, c = lax.div(dp, 8), lax.rem(lax.div(dp, 2), 4), lax.rem(dp, 2)
    sibling = (y * 8 + x * 2 + 1 - c, t)

    text_in = pltpu.make_async_copy(text_hbm, text, io_s.at[0])
    lmg_in = pltpu.make_async_copy(lmg_hbm, lmg, io_s.at[1])
    lm_done = pltpu.make_async_copy(lm_out, lm_hbm, io_s.at[2])

    barrier = pltpu.get_barrier_semaphore()

    def greet(k, carry):
        pl.semaphore_signal(
            barrier, inc=1, device_id=(lax.rem(dp + k, NDP), t), device_id_type=MESH
        )
        return carry

    lax.fori_loop(1, NDP, greet, 0)

    def greet_z(k, carry):
        pl.semaphore_signal(
            barrier, inc=1, device_id=(dp, lax.rem(t + k, NZ)), device_id_type=MESH
        )
        return carry

    lax.fori_loop(1, NZ, greet_z, 0)

    lmg_in.start()
    text_in.start()

    q = iota((1, 128), 1)
    table = jnp.full((1, 128), -1, jnp.int32)
    for s in range(SRC):
        table = jnp.where(q == s, jnp.where(dest[s] >= 0, (dest[s] << 14) + pos[s], -1), table)
    meta[dp] = table
    f2[y, x, c] = fc2[...]
    f1[x, c, y] = fc1[...]

    def selector(count, key):
        n = key.shape[1]
        r, q = iota((count, n), 0), iota((count, n), 1)
        hit = ((r >> 4).astype(F32) == key) & ((r & 15) == (q & 15))
        return jnp.where(hit, 1.0, 0.0).astype(BF)

    def widen(column, n):
        k = column.shape[0]
        return jnp.sum(
            jnp.where(iota((k, n), 0) == (iota((k, n), 1) >> 4), column, 0.0), axis=0, keepdims=True
        )

    value = patches_t[...].astype(F32)
    flat[0] = value[:128].T
    flat[1] = jnp.concatenate([value[128:], jnp.zeros((96, SRC * WIN), F32)], axis=0).T
    pieces = []
    for p in range(4):
        pieces.append(flat[0, pl.ds(p, SRC * TOK, stride=4), :])
        pieces.append(flat[1, pl.ds(p, SRC * TOK, stride=4), :][:, :32])
    windows = jnp.concatenate(pieces, axis=1).astype(BF)
    slots = jnp.sum(
        jnp.where(iota((32, 128), 0) == iota((32, 128), 1), (table >> 14).astype(F32), 0.0),
        axis=1,
        keepdims=True,
    )
    to_dest = selector(NDP * TOK, widen(slots, SRC * TOK))
    st1[...] = dot(to_dest, windows).astype(BF).reshape(NDP, TOK, FEAT)
    rv1[dp] = st1[dp]

    pl.semaphore_wait(barrier, NDP - 1 + NZ - 1)

    def spread(copy, many):
        def start(k, carry):
            copy(k, lax.rem(dp + k, NDP)).start()
            return carry

        return (
            functools.partial(lax.fori_loop, 1, NDP, start, 0),
            lambda: many().wait_recv(),
            lambda: many().wait_send(),
        )

    def push(src, dst, sems, device):
        return pltpu.make_async_remote_copy(
            src_ref=src, dst_ref=dst, send_sem=sems.at[0], recv_sem=sems.at[1],
            device_id=device, device_id_type=MESH,
        )

    others = pl.ds(0, NDP - 1)
    meta_start, meta_arrive, meta_sent = spread(
        lambda k, j: push(meta.at[dp], meta.at[dp], meta_s, (j, t)),
        lambda: push(meta.at[others], meta.at[others], meta_s, sibling),
    )

    chunks = (pl.ds(0, 256), pl.ds(256, 384))

    def hop(n, m, src, dst):
        cols, sems = chunks[m], hop_s.at[2 * n + m]
        return spread(
            lambda k, j: push(src.at[j, :, cols], dst.at[dp, :, cols], sems, (j, t)),
            lambda: push(src.at[others, :, cols], dst.at[others, :, cols], sems, sibling),
        )

    hops = [
        [hop(n, m, src, dst) for m in (0, 1)]
        for n, (src, dst) in enumerate(((st1, rv1), (st2, rv2)))
    ]

    meta_start()
    hops[0][0][0]()
    hops[0][1][0]()

    halves = [Half(kind, h, y, x, c, t) for kind in (2, 1) for h in (0, 1)]
    ag_mail = [Mail(pool, 12 * n, ag_r.at[n]) for n in range(4)]
    gathers = [
        plane_gather(hf, f2 if hf.kind == 2 else f1, m) for hf, m in zip(halves, ag_mail)
    ]

    def step(generators):
        for g in generators:
            next(g)

    step(gathers)

    meta_arrive()
    tables = meta[:, 0, :]
    dests, places = tables >> 14, tables & 16383
    owners = jnp.where(tables >= 0, places >> 9, -1)
    onward = (
        jnp.sum(jnp.where(dests == dp, (owners + 1).astype(F32), 0.0), axis=1, keepdims=True) - 1.0
    )
    to_owner = selector(NDP * TOK, widen(onward, NDP * TOK))
    via = jnp.where(owners == dp, dests, -1)
    next_place = (places + 1).astype(F32)
    r, q = iota((32, 128), 0), iota((32, 128), 1)
    found = jnp.zeros((32, 128), F32)
    for d in range(NDP):
        found = jnp.where(
            r == d, jnp.sum(jnp.where(via == d, next_place, 0.0), axis=0, keepdims=True), found
        )
    found = jnp.sum(found, axis=1, keepdims=True)
    live = jnp.where(found > 0.5, 1.0, 0.0)
    live_row = jnp.sum(jnp.where(r == q, live, 0.0), axis=0, keepdims=True)
    rank = jnp.sum(jnp.where(q < r, live_row, 0.0), axis=1, keepdims=True)
    rank = jnp.where(found > 0.5, rank, -1.0)
    rank_row = jnp.sum(jnp.where(r == q, rank, 0.0), axis=0, keepdims=True)
    rank_row = jnp.where(iota((1, 128), 1) < NDP, rank_row, -1.0)
    found_row = jnp.sum(jnp.where(r == q, found, 0.0), axis=0, keepdims=True)
    to_work = selector(NTOK, widen(rank, NDP * TOK))

    base = dp * LM + 1
    r, q = iota((32, NTOK), 0), iota((32, NTOK), 1)
    tok_row = jnp.sum(jnp.where(rank == (q >> 4).astype(F32), found, 0.0), axis=0, keepdims=True)
    tok_row = tok_row.astype(jnp.int32) + (iota((1, NTOK), 1) & 15) - base
    r = iota((NTOK, 128), 0)
    tok_col = jnp.sum(
        jnp.where(rank_row == (r >> 4).astype(F32), found_row, 0.0), axis=1, keepdims=True
    )
    tok_col = tok_col.astype(jnp.int32) + (iota((NTOK, 1), 0) & 15) - base
    fetch = jnp.where(iota((NTOK, LM), 1) == tok_col, 1.0, 0.0).astype(BF)
    place[...] = jnp.where(iota((LM, NTOK), 0) == tok_row, 1.0, 0.0).astype(BF)


    for m, cols in enumerate(chunks):
        hops[0][m][1]()
        part = rv1[:, :, cols].reshape(NDP * TOK, cols.size)
        st2[:, :, cols] = dot(to_owner, part).astype(BF).reshape(NDP, TOK, cols.size)
        hops[1][m][0]()
        rv2[dp, :, cols] = st2[dp, :, cols]
    lmg_in.wait()
    up_rows[...] = dot(fetch, lmg[...]).astype(BF)

    low, high, every = pl.ds(0, 128), pl.ds(128, 128), pl.ds(0, 256)
    zx_mail = [Mail(pool, 48 + 8 * m, zx_r.at[m]) for m in (0, 1)]
    zx = []
    for m, cols in enumerate(chunks):
        hops[1][m][1]()
        part = rv2[:, :, cols].reshape(NDP * TOK, cols.size)
        xs[t, :, cols] = dot(to_work, part).astype(BF)
        zx.append(
            ring_gather(dp, t, xs, ((every, cols), (low, cols), (high, cols)), zx_mail[m])
        )
        next(zx[m])

    seg = iota((NTOK, FEAT), 1) // 160
    square = xs[t].astype(F32)
    square = square * square
    lane = iota((NTOK, 128), 1)
    sums_of = jnp.zeros((NTOK, 128), F32)
    for p in range(4):
        part = jnp.sum(jnp.where(seg == p, square, 0.0), axis=1, keepdims=True)
        sums_of = jnp.where(lane == p, part, sums_of)
    sq[t] = sums_of.T[:8]

    for k in range(1, NZ):
        push(sq.at[t], sq.at[t], sq_s, (dp, lax.rem(t + k, NZ))).start()
    seven = push(sq.at[pl.ds(0, NZ - 1)], sq.at[pl.ds(0, NZ - 1)], sq_s, sibling)
    step(gathers)
    step(gathers)
    all_gain = gain[...].reshape(1, DM)
    for k in range(NZ):
        gains[k] = jnp.concatenate([all_gain[:, 160 * k : 160 * k + 160]] * 4, axis=1)
    seven.wait_recv()
    scale = lax.rsqrt(jnp.sum(sq[...], axis=0) * (1.0 / DM) + 1e-06)
    scale = jnp.concatenate([scale] * 16, axis=0).T
    factor[...] = jnp.where(
        seg == 0,
        scale[:, 0:1],
        jnp.where(seg == 1, scale[:, 1:2], jnp.where(seg == 2, scale[:, 2:3], scale[:, 3:4])),
    )

    def normalise(k):
        j = turn(t, k, NZ)
        xn[j] = (xs[j].astype(F32) * factor[...] * gains[j]).astype(BF)

    normalise(0)
    step(zx)
    step(gathers)
    normalise(-1)
    normalise(1)
    step(zx)
    step(gathers)
    normalise(-2)
    normalise(2)
    step(gathers)

    def second_rows(k):
        two = lax.rem(k, 2) * 2
        return f2[lax.div(k, 2), pl.ds(two, 2)].reshape(HID, OUT)

    def back(k, carry):
        hb[k] = dot(second_rows(k), up_rows[...], 1, 1).astype(BF)
        return carry

    lax.fori_loop(0, NZ, back, 0)

    tokens = (low, high)
    zb_mail = [Mail(pool, 64 + 8 * m, zb_r.at[m]) for m in (0, 1)]

    def put_back(m):
        def put(total):
            acc[:, 128 * m : 128 * m + 128] = total

        return put

    zb = [
        ring_scatter(dp, t, hb, hb_room, tokens[m], zb_mail[m], put_back(m)) for m in (0, 1)
    ]
    step(zb)

    def first_part(k):
        j = turn(t, k, NZ)
        w = f1[lax.div(j, 2), lax.rem(j, 2)].reshape(FEAT, HID)
        return dot(xn[j], w)

    step(zx)
    normalise(-3)
    normalise(3)
    meta_sent()
    seven.wait_send()
    for n in (0, 1):
        for m in (0, 1):
            hops[n][m][2]()
    step(zb)
    z1 = first_part(0) + first_part(-1) + first_part(1) + first_part(-2)
    step(zb)
    for m in ag_mail:
        m.finish()
    z1 = z1 + first_part(2) + first_part(-3) + first_part(3)
    step(zx)
    normalise(4)
    z1 = z1 + first_part(4)
    z1 = jnp.concatenate([z1, jnp.zeros((NTOK, HPAD - HID), F32)], axis=1).T[:HID]
    cdf = 0.5 * (1.0 + lax.erf(z1 * 0.7071067811865476))
    hid[t] = (z1 * cdf).astype(BF)

    zh_mail = [Mail(pool, 8 * m, zh_r.at[m]) for m in (0, 1)]
    zh = [
        ring_gather(
            dp, t, hid,
            ((pl.ds(0, 320), cut), (pl.ds(0, 160), cut), (pl.ds(160, 160), cut)),
            zh_mail[m],
        )
        for m, cut in enumerate(tokens)
    ]
    core_mail = Mail(pool, 96, co_r)
    sent = []

    def use_hidden(k):
        j = turn(t, k, NZ)
        yy, two = lax.div(j, 2), pl.ds(lax.rem(j, 2) * 2, 2)
        p2[yy, two] = dot(hid[j], up_rows[...]).astype(BF).reshape(2, 2, 80, OUT)
        core_mail.send(p2.at[yy, two, 1 - c], b_cores.at[yy, two], len(sent), sibling)
        sent.append((yy, two))

    summed = []

    def join_cores():
        while len(summed) < len(sent):
            yy, two = sent[len(summed)]
            core_mail.wait(b_cores.at[yy, two], len(summed), sibling)
            mine = p2.at[yy, two, c]
            mine[...] = (mine[...].astype(F32) + b_cores[yy, two].astype(F32)).astype(BF)
            summed.append(yy)

    def grad1(xx, cc):
        term = dot(xn[xx * 2 + cc], dz[:, :HID], 0, 0).astype(BF)
        p1[xx, cc] = term.reshape(4, 160, HID)

    step(zh)
    step(zb)
    slope = cdf + z1 * (jnp.exp(-0.5 * z1 * z1) * 0.3989422804014327)
    step(zb)
    dz_t = acc[...] * slope
    dz[...] = jnp.concatenate([dz_t, jnp.zeros((HPAD - HID, NTOK), F32)], axis=0).T.astype(BF)
    for xx in range(4):
        grad1(xx, 1 - c)
        core_mail.send(p1.at[xx, 1 - c], a_cores.at[xx], 8 + xx, sibling)
    use_hidden(0)
    for m in zx_mail:
        m.finish()
    rs_mail = [Mail(pool, (56, 76, 16, 36)[n], rs_r.at[n]) for n in range(4)]

    def put2(h):
        def put(total):
            g2_out[:, 512 * h : 512 * h + 512] = total

        return put

    def put1(h):
        def put(total):
            g1_out[80 * h : 80 * h + 80, :] = total

        return put

    sums = []
    for n, hf in enumerate(halves):
        h = hf.h
        if hf.kind == 2:
            room = (b_sub.at[h, 0], b_sub.at[h, 1], b_full.at[h],
                    b_lasts.at[h, 0], b_lasts.at[h, 1], b_last.at[h])
            sums.append(ring_sums(hf, p2, room, rs_mail[n], put2(h)))
        else:
            room = (a_sub0.at[h], a_sub1.at[h], a_full.at[h],
                    a_last0.at[h], a_last1.at[h], a_last.at[h])
            sums.append(ring_sums(hf, p1, room, rs_mail[n], put1(h)))
    step(zh)
    for xx in range(4):
        grad1(xx, c)
        core_mail.wait(a_cores.at[xx], 8 + xx, sibling)
        mine = p1.at[xx, c]
        mine[...] = (mine[...].astype(F32) + a_cores[xx].astype(F32)).astype(BF)
    step(sums[2:])
    use_hidden(-1)
    use_hidden(1)
    step(zh)
    use_hidden(-2)
    use_hidden(2)
    join_cores()
    step(sums[2:])
    step(zh)
    use_hidden(-3)
    use_hidden(3)
    join_cores()
    for m in zb_mail:
        m.finish()
    step(sums[2:])
    step(zh)
    use_hidden(4)
    join_cores()
    step(sums[:2])
    step(sums[2:])

    def forward(k):
        return dot(hid[k], second_rows(k), 0, 0)

    mixed[...] = forward(0) + forward(1) + forward(2) + forward(3)
    step(sums[:2])
    step(sums[2:])
    merged = (mixed[...] + forward(4) + forward(5) + forward(6) + forward(7)).astype(BF)
    step(sums[:2])
    text_in.wait()
    covered = jnp.max(place[...].astype(F32), axis=1, keepdims=True) > 0.5
    lm_out[...] = jnp.where(covered, dot(place[...], merged), text[...].astype(F32)).astype(BF)
    lm_done.start()
    step(sums[:2])
    for m in zh_mail + [core_mail]:
        m.finish()
    step(sums[:2])

    lm_done.wait()
    for m in rs_mail:
        m.finish()


def per_device(patches, gain, window_dest, window_pos, fc1, fc2, text_embeds, lm_grad):
    vm = pl.BlockSpec(memory_space=pltpu.VMEM)
    anywhere = pl.BlockSpec(memory_space=pl.ANY)
    sm = pl.BlockSpec(memory_space=pltpu.SMEM)
    V = pltpu.VMEM
    D = pltpu.SemaphoreType.DMA
    scratch = [
        V((LM, OUT), BF),
        V((LM, OUT), BF),
        V((LM, OUT), BF),
        D((3,)),
        V((NZ, 8, NTOK), F32),
        V((NDP, 1, 128), jnp.int32),
        V((NZ, 1, FEAT), F32),
        V((NTOK, FEAT), F32),
        V((NZ, NTOK, FEAT), BF),
        V((2, SRC * WIN, 128), F32),
        V((NDP, TOK, FEAT), BF),
        V((NDP, TOK, FEAT), BF),
        V((NDP, TOK, FEAT), BF),
        V((NDP, TOK, FEAT), BF),
        V((NZ, NTOK, FEAT), BF),
        V((4, 2, 4, 160, HID), BF),
        V((4, 4, 2, 80, OUT), BF),
        V((NTOK, OUT), BF),
        V((LM, NTOK), BF),
        V((HID, NTOK), F32),
        V((NZ, HID, NTOK), BF),
        V((NZ, HID, NTOK), BF),
        V((8, HID, NTOK), BF),
        V((NTOK, HPAD), BF),
        V((NTOK, OUT), F32),
        V((4, 2, 4, 160, HID), BF),
        V((4, 4, 2, 80, OUT), BF),
        V((4, 4, 160, HID), BF),
        V((2, 4, 48, HID), BF),
        V((2, 4, 32, HID), BF),
        V((2, 2, 4, 80, HID), BF),
        V((2, 48, HID), BF),
        V((2, 32, HID), BF),
        V((2, 2, 80, HID), BF),
        V((4, 4, 80, OUT), BF),
        V((2, 2, 4, 80, 256), BF),
        V((2, 2, 4, 80, 512), BF),
        V((2, 2, 80, 256), BF),
        V((2, 2, 80, 512), BF),
        D((108,)), D((2,)), D((2,)), D((4, 2)),
        D((4, 9)), D((2, 8)), D((2, 8)), D((2, 8)), D((12,)), D((4, 20)),
    ]
    return pl.pallas_call(
        body,
        out_shape=(
            pltpu.VMEM((LM, OUT), BF),
            pltpu.VMEM((160, HID), F32),
            pltpu.VMEM((80, OUT), F32),
        ),
        in_specs=[vm, vm, sm, sm, vm, vm, anywhere, anywhere],
        out_specs=(anywhere, vm, vm),
        scratch_shapes=scratch,
        compiler_params=pltpu.CompilerParams(
            collective_id=0, has_side_effects=True, vmem_limit_bytes=60 * 1024 * 1024
        ),
        cost_estimate=pl.CostEstimate(
            flops=6_000_000_000, bytes_accessed=8_000_000, transcendentals=300_000
        ),
    )(patches.T, gain, window_dest, window_pos, fc1, fc2, text_embeds, lm_grad)


def solution(mesh):
    both = P("dp", "tensor")
    return jax.shard_map(
        per_device,
        mesh=mesh,
        in_specs=(both, P(), P("dp"), P("dp"), both, both, both, both),
        out_specs=(both, both, both),
        check_vma=False,
    )
```

```python
import functools

import jax
import jax.numpy as jnp
from jax import lax
from jax.experimental import pallas as pl
from jax.experimental.pallas import tpu as pltpu
from jax.sharding import PartitionSpec as P

MESH = pl.DeviceIdType.MESH
BF = jnp.bfloat16
F32 = jnp.float32
DM = 1280
NDP = 32
NZ = 8
SRC = 24
WORK = 16
TOK = 16
FEAT = 640
WIN = 64
HID = 320
HPAD = 384
LM = 512
OUT = 1024
NTOK = WORK * TOK


def dot(a, b, da=1, db=0):
    return lax.dot_general(a, b, (((da,), (db,)), ((), ())), preferred_element_type=F32)


def iota(shape, axis):
    return lax.broadcasted_iota(jnp.int32, shape, axis)


def turn(v, k, n):
    return lax.rem(v + (k % n), n)


class Half:
    def __init__(self, kind, h, y, x, c, t):
        self.kind, self.h, self.y, self.x, self.c, self.t = kind, h, y, x, c, t
        self.q = x if h == 0 else y
        self.r = y if h == 0 else x

    def dev(self, y, x, c):
        return (y * 8 + x * 2 + c, self.t)

    def first(self, k):
        if self.h == 0:
            return self.dev(self.y, turn(self.x, k, 4), self.c)
        return self.dev(turn(self.y, k, 4), self.x, self.c)

    def second(self, k):
        if self.h == 0:
            return self.dev(turn(self.y, k, 4), self.x, self.c)
        return self.dev(self.y, turn(self.x, k, 4), self.c)

    def sibling(self):
        return self.dev(self.y, self.x, 1 - self.c)

    def cut(self, s):
        if self.kind == 2:
            start = 512 * self.h + (256 if s == 1 else 0)
            return pl.ds(0, 80), pl.ds(start, 512 if s is None else 256)
        start = 80 * self.h + (48 if s == 1 else 0)
        return pl.ds(start, {None: 80, 0: 48, 1: 32}[s]), pl.ds(0, HID)

    def at(self, buf, y, x, c, s):
        rows, cols = self.cut(s)
        if self.kind == 2:
            return buf.at[y, x, c, rows, cols]
        return buf.at[x, c, y, rows, cols]

    def block(self, buf, k, s=None):
        p = turn(self.q, k, 4)
        if self.h == 0:
            return self.at(buf, self.y, p, self.c, s)
        return self.at(buf, p, self.x, self.c, s)

    def cell(self, buf, g, b, s=None):
        y, x = turn(self.r, g, 4), turn(self.q, b, 4)
        if self.h == 1:
            y, x = x, y
        rows, cols = self.cut(s)
        if self.kind == 2:
            return buf.at[y, x, rows, cols]
        return buf.at[x, y, rows, cols]

    def group(self, buf, k, s=None, other=False):
        p = turn(self.r, k, 4)
        c = 1 - self.c if other else self.c
        if self.h == 0:
            return self.at(buf, p, slice(None), c, s)
        return self.at(buf, slice(None), p, c, s)


class Mail:
    def __init__(self, pool, first, recv):
        self.pool, self.next, self.r, self.started = pool, first, recv, []

    def make(self, src, dst, send, i, device):
        return pltpu.make_async_remote_copy(
            src_ref=src,
            dst_ref=dst,
            send_sem=self.pool.at[send],
            recv_sem=self.r.at[i],
            device_id=device,
            device_id_type=MESH,
        )

    def send(self, src, dst, i, device):
        copy = self.make(src, dst, self.next, i, device)
        copy.start()
        self.next += 1
        self.started.append(copy)

    def wait(self, dst, i, device):
        self.make(dst, dst, 0, i, device).wait_recv()

    def finish(self):
        for copy in self.started:
            copy.wait_send()
        self.started = []


def plane_gather(hf, buf, mail):
    def send(ref, i, device):
        mail.send(ref, ref, i, device)

    def wait(ref, i):
        mail.wait(ref, i, hf.sibling())

    send(hf.block(buf, 0), 0, hf.first(1))
    send(hf.block(buf, 0), 1, hf.first(-1))
    yield
    wait(hf.block(buf, -1), 0)
    send(hf.block(buf, -1, 0), 2, hf.first(1))
    wait(hf.block(buf, 1), 1)
    send(hf.block(buf, 1, 1), 3, hf.first(-1))
    yield
    wait(hf.block(buf, 2, 0), 2)
    wait(hf.block(buf, 2, 1), 3)
    send(hf.group(buf, 0), 4, hf.second(1))
    send(hf.group(buf, 0), 5, hf.second(-1))
    send(hf.group(buf, 0), 6, hf.sibling())
    yield
    wait(hf.group(buf, -1), 4)
    send(hf.group(buf, -1, 0), 7, hf.second(1))
    send(hf.group(buf, -1), 6, hf.sibling())
    wait(hf.group(buf, 1), 5)
    send(hf.group(buf, 1, 1), 8, hf.second(-1))
    send(hf.group(buf, 1), 6, hf.sibling())
    yield
    wait(hf.group(buf, 2, 0), 7)
    wait(hf.group(buf, 2, 1), 8)
    send(hf.group(buf, 2), 6, hf.sibling())
    yield
    wait(hf.at(buf, slice(None), slice(None), 1 - hf.c, None), 6)
    yield


def ring_sums(hf, buf, room, mail, put):
    sub0, sub1, full, last0, last1, last = room
    order = (2, 1, -1, 0)

    def wait(ref, i):
        mail.wait(ref, i, hf.sibling())

    def plus(mine, *others):
        total = mine[...].astype(F32)
        for o in others:
            total = total + o[...].astype(F32)
        mine[...] = total.astype(BF)

    for n, b in enumerate(order):
        mail.send(hf.cell(buf, 2, b, 0), sub0.at[n], n, hf.second(1))
        mail.send(hf.cell(buf, 2, b, 1), sub1.at[n], 4 + n, hf.second(-1))
    yield
    for n, b in enumerate(order):
        wait(sub0.at[n], n)
        plus(hf.cell(buf, 1, b, 0), sub0.at[n])
        mail.send(hf.cell(buf, 1, b), full.at[0, n], 8 + n, hf.second(1))
        wait(sub1.at[n], 4 + n)
        plus(hf.cell(buf, -1, b, 1), sub1.at[n])
        mail.send(hf.cell(buf, -1, b), full.at[1, n], 12 + n, hf.second(-1))
    yield
    for n in (0, 1, 2):
        wait(full.at[0, n], 8 + n)
        wait(full.at[1, n], 12 + n)
        plus(hf.cell(buf, 0, order[n]), full.at[0, n], full.at[1, n])
        if n == 0:
            mail.send(hf.cell(buf, 0, 2, 0), last0, 16, hf.first(1))
            mail.send(hf.cell(buf, 0, 2, 1), last1, 17, hf.first(-1))
    yield
    wait(last0, 16)
    plus(hf.cell(buf, 0, 1, 0), last0)
    mail.send(hf.cell(buf, 0, 1), last.at[0], 18, hf.first(1))
    wait(last1, 17)
    plus(hf.cell(buf, 0, -1, 1), last1)
    mail.send(hf.cell(buf, 0, -1), last.at[1], 19, hf.first(-1))
    yield
    wait(full.at[0, 3], 11)
    wait(full.at[1, 3], 15)
    wait(last.at[0], 18)
    wait(last.at[1], 19)
    total = hf.cell(buf, 0, 0)[...].astype(F32)
    for part in (full[0, 3], full[1, 3], last[0], last[1]):
        total = total + part.astype(F32)
    put(total)
    yield


def ring_gather(dp, t, buf, cuts, mail):
    up, down = (dp, turn(t, 1, NZ)), (dp, turn(t, -1, NZ))

    def view(k, cut):
        return buf.at[(turn(t, k, NZ),) + cut]

    def send(k, cut, i, device):
        mail.send(view(k, cut), view(k, cut), i, device)

    def wait(k, cut, i):
        mail.wait(view(k, cut), i, up)

    whole, one, two = cuts
    send(0, whole, 0, up)
    send(0, whole, 1, down)
    yield (0,)
    for k in (1, 2):
        wait(-k, whole, 2 * k - 2)
        send(-k, whole, 2 * k, up)
        wait(k, whole, 2 * k - 1)
        send(k, whole, 2 * k + 1, down)
        yield (-k, k)
    wait(-3, whole, 4)
    send(-3, one, 6, up)
    wait(3, whole, 5)
    send(3, two, 7, down)
    yield (-3, 3)
    wait(4, one, 6)
    wait(4, two, 7)
    yield (4,)


def ring_scatter(dp, t, buf, room, cols, mail, put):
    up, down = (dp, turn(t, 1, NZ)), (dp, turn(t, -1, NZ))
    half = HID // 2
    low, high, every = pl.ds(0, half), pl.ds(half, half), pl.ds(0, HID)

    def view(k, cut):
        return buf.at[turn(t, k, NZ), cut, cols]

    def plus(k, cut, other):
        mine = view(k, cut)
        mine[...] = (mine[...].astype(F32) + other[...].astype(F32)).astype(BF)

    mail.send(view(4, low), room.at[0, low, cols], 0, up)
    mail.send(view(4, high), room.at[1, high, cols], 1, down)
    yield
    for n, k in enumerate((3, 2, 1)):
        a, b = (low, high) if n == 0 else (every, every)
        mail.wait(room.at[2 * n, a, cols], 2 * n, up)
        plus(k, a, room.at[2 * n, a, cols])
        mail.send(view(k, every), room.at[2 * n + 2, every, cols], 2 * n + 2, up)
        mail.wait(room.at[2 * n + 1, b, cols], 2 * n + 1, up)
        plus(-k, b, room.at[2 * n + 1, b, cols])
        mail.send(view(-k, every), room.at[2 * n + 3, every, cols], 2 * n + 3, down)
        yield
    mail.wait(room.at[6, every, cols], 6, up)
    mail.wait(room.at[7, every, cols], 7, up)
    put(
        view(0, every)[...].astype(F32)
        + room[6, :, cols].astype(F32)
        + room[7, :, cols].astype(F32)
    )
    yield


def body(
    patches_t, gain, dest, pos, fc1, fc2, text_hbm, lmg_hbm,
    lm_hbm, g1_out, g2_out,
    text, lmg, lm_out, io_s,
    sq, meta, gains, factor, xn, flat, st1, rv1, st2, rv2, xs, f1, f2, up_rows, place,
    acc, hid, hb, hb_room, dz, mixed, p1, p2, hid2, up2, dz2, x2,
    a_sub0, a_sub1, a_full, a_last0, a_last1, a_last,
    b_sub, b_full, b_lasts, b_last,
    pool, sq_s, meta_s, hop_s, ag_r, zx_r, zh_r, zb_r, co_r, rs_r,
):
    dp = lax.axis_index("dp")
    t = lax.axis_index("tensor")
    y, x, c = lax.div(dp, 8), lax.rem(lax.div(dp, 2), 4), lax.rem(dp, 2)
    sibling = (y * 8 + x * 2 + 1 - c, t)

    text_in = pltpu.make_async_copy(text_hbm, text, io_s.at[0])
    lmg_in = pltpu.make_async_copy(lmg_hbm, lmg, io_s.at[1])
    lm_done = pltpu.make_async_copy(lm_out, lm_hbm, io_s.at[2])

    barrier = pltpu.get_barrier_semaphore()

    def greet(k, carry):
        pl.semaphore_signal(
            barrier, inc=1, device_id=(lax.rem(dp + k, NDP), t), device_id_type=MESH
        )
        return carry

    lax.fori_loop(1, NDP, greet, 0)

    def greet_z(k, carry):
        pl.semaphore_signal(
            barrier, inc=1, device_id=(dp, lax.rem(t + k, NZ)), device_id_type=MESH
        )
        return carry

    lax.fori_loop(1, NZ, greet_z, 0)

    lmg_in.start()
    text_in.start()

    q = iota((1, 128), 1)
    table = jnp.full((1, 128), -1, jnp.int32)
    for s in range(SRC):
        table = jnp.where(q == s, jnp.where(dest[s] >= 0, (dest[s] << 14) + pos[s], -1), table)
    meta[dp] = table
    f2[y, x, c] = fc2[...]
    f1[x, c, y] = fc1[...]

    def selector(count, key):
        n = key.shape[1]
        r, q = iota((count, n), 0), iota((count, n), 1)
        hit = ((r >> 4).astype(F32) == key) & ((r & 15) == (q & 15))
        return jnp.where(hit, 1.0, 0.0).astype(BF)

    def widen(column, n):
        k = column.shape[0]
        return jnp.sum(
            jnp.where(iota((k, n), 0) == (iota((k, n), 1) >> 4), column, 0.0), axis=0, keepdims=True
        )

    value = patches_t[...].astype(F32)
    flat[0] = value[:128].T
    flat[1] = jnp.concatenate([value[128:], jnp.zeros((96, SRC * WIN), F32)], axis=0).T
    pieces = []
    for p in range(4):
        pieces.append(flat[0, pl.ds(p, SRC * TOK, stride=4), :])
        pieces.append(flat[1, pl.ds(p, SRC * TOK, stride=4), :][:, :32])
    windows = jnp.concatenate(pieces, axis=1).astype(BF)
    slots = jnp.sum(
        jnp.where(iota((32, 128), 0) == iota((32, 128), 1), (table >> 14).astype(F32), 0.0),
        axis=1,
        keepdims=True,
    )
    to_dest = selector(NDP * TOK, widen(slots, SRC * TOK))
    st1[...] = dot(to_dest, windows).astype(BF).reshape(NDP, TOK, FEAT)
    rv1[dp] = st1[dp]

    pl.semaphore_wait(barrier, NDP - 1 + NZ - 1)

    def spread(copy, many):
        def start(k, carry):
            copy(k, lax.rem(dp + k, NDP)).start()
            return carry

        return (
            functools.partial(lax.fori_loop, 1, NDP, start, 0),
            lambda: many().wait_recv(),
            lambda: many().wait_send(),
        )

    def push(src, dst, sems, device):
        return pltpu.make_async_remote_copy(
            src_ref=src, dst_ref=dst, send_sem=sems.at[0], recv_sem=sems.at[1],
            device_id=device, device_id_type=MESH,
        )

    others = pl.ds(0, NDP - 1)
    meta_start, meta_arrive, meta_sent = spread(
        lambda k, j: push(meta.at[dp], meta.at[dp], meta_s, (j, t)),
        lambda: push(meta.at[others], meta.at[others], meta_s, sibling),
    )

    chunks = (pl.ds(0, 256), pl.ds(256, 384))

    def hop(n, m, src, dst):
        cols, sems = chunks[m], hop_s.at[2 * n + m]
        return spread(
            lambda k, j: push(src.at[j, :, cols], dst.at[dp, :, cols], sems, (j, t)),
            lambda: push(src.at[others, :, cols], dst.at[others, :, cols], sems, sibling),
        )

    hops = [
        [hop(n, m, src, dst) for m in (0, 1)]
        for n, (src, dst) in enumerate(((st1, rv1), (st2, rv2)))
    ]

    meta_start()
    hops[0][0][0]()
    hops[0][1][0]()

    halves = [Half(kind, h, y, x, c, t) for kind in (2, 1) for h in (0, 1)]
    ag_mail = [Mail(pool, 12 * n, ag_r.at[n]) for n in range(4)]
    gathers = [
        plane_gather(hf, f2 if hf.kind == 2 else f1, m) for hf, m in zip(halves, ag_mail)
    ]

    def step(generators):
        for g in generators:
            next(g)

    step(gathers)

    meta_arrive()
    tables = meta[:, 0, :]
    dests, places = tables >> 14, tables & 16383
    owners = jnp.where(tables >= 0, places >> 9, -1)
    onward = (
        jnp.sum(jnp.where(dests == dp, (owners + 1).astype(F32), 0.0), axis=1, keepdims=True) - 1.0
    )
    to_owner = selector(NDP * TOK, widen(onward, NDP * TOK))
    via = jnp.where(owners == dp, dests, -1)
    next_place = (places + 1).astype(F32)
    r, q = iota((32, 128), 0), iota((32, 128), 1)
    found = jnp.zeros((32, 128), F32)
    for d in range(NDP):
        found = jnp.where(
            r == d, jnp.sum(jnp.where(via == d, next_place, 0.0), axis=0, keepdims=True), found
        )
    found = jnp.sum(found, axis=1, keepdims=True)
    live = jnp.where(found > 0.5, 1.0, 0.0)
    live_row = jnp.sum(jnp.where(r == q, live, 0.0), axis=0, keepdims=True)
    rank = jnp.sum(jnp.where(q < r, live_row, 0.0), axis=1, keepdims=True)
    rank = jnp.where(found > 0.5, rank, -1.0)
    rank_row = jnp.sum(jnp.where(r == q, rank, 0.0), axis=0, keepdims=True)
    rank_row = jnp.where(iota((1, 128), 1) < NDP, rank_row, -1.0)
    found_row = jnp.sum(jnp.where(r == q, found, 0.0), axis=0, keepdims=True)
    to_work = selector(NTOK, widen(rank, NDP * TOK))

    base = dp * LM + 1
    r, q = iota((32, NTOK), 0), iota((32, NTOK), 1)
    tok_row = jnp.sum(jnp.where(rank == (q >> 4).astype(F32), found, 0.0), axis=0, keepdims=True)
    tok_row = tok_row.astype(jnp.int32) + (iota((1, NTOK), 1) & 15) - base
    r = iota((NTOK, 128), 0)
    tok_col = jnp.sum(
        jnp.where(rank_row == (r >> 4).astype(F32), found_row, 0.0), axis=1, keepdims=True
    )
    tok_col = tok_col.astype(jnp.int32) + (iota((NTOK, 1), 0) & 15) - base
    fetch = jnp.where(iota((NTOK, LM), 1) == tok_col, 1.0, 0.0).astype(BF)
    place[...] = jnp.where(iota((LM, NTOK), 0) == tok_row, 1.0, 0.0).astype(BF)


    for m, cols in enumerate(chunks):
        hops[0][m][1]()
        part = rv1[:, :, cols].reshape(NDP * TOK, cols.size)
        st2[:, :, cols] = dot(to_owner, part).astype(BF).reshape(NDP, TOK, cols.size)
        hops[1][m][0]()
        rv2[dp, :, cols] = st2[dp, :, cols]
    step(gathers)
    lmg_in.wait()
    up_rows[...] = dot(fetch, lmg[...]).astype(BF)
    core_mail = Mail(pool, 96, co_r)
    core_mail.send(up_rows, up2, 8, sibling)
    all_gain = gain[...].reshape(1, DM)
    for k in range(NZ):
        gains[k] = jnp.concatenate([all_gain[:, 160 * k : 160 * k + 160]] * 4, axis=1)

    low, high, every = pl.ds(0, 128), pl.ds(128, 128), pl.ds(0, 256)
    zx_mail = [Mail(pool, 48 + 8 * m, zx_r.at[m]) for m in (0, 1)]
    zx = [
        ring_gather(dp, t, xs, ((every, cols), (low, cols), (high, cols)), zx_mail[m])
        for m, cols in enumerate(chunks)
    ]

    def arrive(m):
        cols = chunks[m]
        hops[1][m][1]()
        part = rv2[:, :, cols].reshape(NDP * TOK, cols.size)
        xs[t, :, cols] = dot(to_work, part).astype(BF)

    arrive(0)
    step(zx[:1])
    step(gathers[:2])
    arrive(1)

    seg = iota((NTOK, FEAT), 1) // 160
    square = xs[t].astype(F32)
    square = square * square
    lane = iota((NTOK, 128), 1)
    sums_of = jnp.zeros((NTOK, 128), F32)
    for p in range(4):
        part = jnp.sum(jnp.where(seg == p, square, 0.0), axis=1, keepdims=True)
        sums_of = jnp.where(lane == p, part, sums_of)
    sq[t] = sums_of.T[:8]
    for k in range(1, NZ):
        push(sq.at[t], sq.at[t], sq_s, (dp, lax.rem(t + k, NZ))).start()
    seven = push(sq.at[pl.ds(0, NZ - 1)], sq.at[pl.ds(0, NZ - 1)], sq_s, sibling)
    step(zx[1:])

    step(zx)
    step(gathers[:2])
    step(gathers[2:])
    seven.wait_recv()
    scale = lax.rsqrt(jnp.sum(sq[...], axis=0) * (1.0 / DM) + 1e-06)
    scale = jnp.concatenate([scale] * 16, axis=0).T
    factor[...] = jnp.where(
        seg == 0,
        scale[:, 0:1],
        jnp.where(seg == 1, scale[:, 1:2], jnp.where(seg == 2, scale[:, 2:3], scale[:, 3:4])),
    )

    def normalise(k):
        j = turn(t, k, NZ)
        xn[j] = (xs[j].astype(F32) * factor[...] * gains[j]).astype(BF)

    normalise(0)
    step(zx)
    step(gathers[:2])
    normalise(-1)
    normalise(1)
    step(gathers[:2])

    def second_rows(k):
        two = lax.rem(k, 2) * 2
        return f2[lax.div(k, 2), pl.ds(two, 2)].reshape(HID, OUT)

    def back(k, carry):
        hb[k] = dot(second_rows(k), up_rows[...], 1, 1).astype(BF)
        return carry

    lax.fori_loop(0, NZ, back, 0)

    tokens = (low, high)
    zb_mail = [Mail(pool, 64 + 8 * m, zb_r.at[m]) for m in (0, 1)]

    def put_back(m):
        def put(total):
            acc[:, 128 * m : 128 * m + 128] = total

        return put

    zb = [
        ring_scatter(dp, t, hb, hb_room, tokens[m], zb_mail[m], put_back(m)) for m in (0, 1)
    ]
    step(zb)

    def first_part(k):
        j = turn(t, k, NZ)
        w = f1[lax.div(j, 2), lax.rem(j, 2)].reshape(FEAT, HID)
        return dot(xn[j], w)

    step(gathers[2:])
    step(zx)
    normalise(-2)
    normalise(2)
    step(gathers[2:])
    step(zb)
    normalise(-3)
    normalise(3)
    meta_sent()
    seven.wait_send()
    for n in (0, 1):
        for m in (0, 1):
            hops[n][m][2]()
    step(gathers[2:])
    for m in ag_mail:
        m.finish()
    z1 = first_part(0) + first_part(-1) + first_part(1) + first_part(-2)
    z1 = z1 + first_part(2) + first_part(-3) + first_part(3)
    step(zx)
    normalise(4)
    for xx in range(4):
        core_mail.send(xn.at[xx * 2 + 1 - c], x2.at[xx], 10 + xx, sibling)
    z1 = z1 + first_part(4)
    z1 = jnp.concatenate([z1, jnp.zeros((NTOK, HPAD - HID), F32)], axis=1).T[:HID]
    cdf = 0.5 * (1.0 + lax.erf(z1 * 0.7071067811865476))
    hid[t] = (z1 * cdf).astype(BF).reshape(2, 2, 80, NTOK)

    zh_mail = [Mail(pool, 8 * m, zh_r.at[m]) for m in (0, 1)]
    full = slice(None)
    zh = [
        ring_gather(
            dp, t, hid,
            ((full, full, full, cut), (pl.ds(0, 1), full, full, cut), (pl.ds(1, 1), full, full, cut)),
            zh_mail[m],
        )
        for m, cut in enumerate(tokens)
    ]
    order = (0, -1, 1, -2, 2, -3, 3, 4)

    def share(*ks):
        for k in ks:
            j = turn(t, k, NZ)
            core_mail.send(hid.at[j, :, 1 - c], hid2.at[j], order.index(k), sibling)

    def use_hidden(*ks):
        for k in ks:
            j = turn(t, k, NZ)
            mine = dot(hid[j, :, c].reshape(160, NTOK), up_rows[...])
            core_mail.wait(hid2.at[j], order.index(k), sibling)
            term = mine + dot(hid2[j].reshape(160, NTOK), up2[...])
            p2[lax.div(j, 2), pl.ds(lax.rem(j, 2) * 2, 2)] = term.astype(BF).reshape(2, 80, OUT)

    def grad1(xx):
        mine = dot(xn[xx * 2 + c], dz[:, :HID], 0, 0)
        if xx == 0:
            core_mail.wait(dz2, 9, sibling)
        core_mail.wait(x2.at[xx], 10 + xx, sibling)
        p1[xx] = (mine + dot(x2[xx], dz2[:, :HID], 0, 0)).astype(BF).reshape(4, 160, HID)

    rs_mail = [Mail(pool, (56, 76, 16, 36)[n], rs_r.at[n]) for n in range(4)]

    def put2(h):
        def put(total):
            g2_out[:, 512 * h : 512 * h + 512] = total

        return put

    def put1(h):
        def put(total):
            g1_out[80 * h : 80 * h + 80, :] = total

        return put

    sums = []
    for n, hf in enumerate(halves):
        h = hf.h
        if hf.kind == 2:
            room = (b_sub.at[h, 0], b_sub.at[h, 1], b_full.at[h],
                    b_lasts.at[h, 0], b_lasts.at[h, 1], b_last.at[h])
            sums.append(ring_sums(hf, p2, room, rs_mail[n], put2(h)))
        else:
            room = (a_sub0.at[h], a_sub1.at[h], a_full.at[h],
                    a_last0.at[h], a_last1.at[h], a_last.at[h])
            sums.append(ring_sums(hf, p1, room, rs_mail[n], put1(h)))
    def forward(k):
        return dot(hid[k].reshape(HID, NTOK), second_rows(k), 0, 0)

    step(zh)
    share(0)
    step(zb)
    slope = cdf + z1 * (jnp.exp(-0.5 * z1 * z1) * 0.3989422804014327)
    core_mail.wait(up2, 8, sibling)
    use_hidden(0)
    step(zh)
    share(-1, 1)
    step(zb)
    use_hidden(-1, 1)
    step(zh)
    share(-2, 2)
    step(zb)
    dz_t = acc[...] * slope
    dz[...] = jnp.concatenate([dz_t, jnp.zeros((HPAD - HID, NTOK), F32)], axis=0).T.astype(BF)
    core_mail.send(dz, dz2, 9, sibling)
    use_hidden(-2, 2)
    for m in zx_mail:
        m.finish()
    step(zh)
    share(-3, 3)
    for xx in range(4):
        grad1(xx)
    step(sums[2:])
    use_hidden(-3, 3)
    for m in zb_mail:
        m.finish()
    step(zh)
    share(4)
    step(sums[2:])
    use_hidden(4)
    step(sums[:2])
    step(sums[2:])
    mixed[...] = forward(0) + forward(1) + forward(2) + forward(3)
    step(sums[:2])
    step(sums[2:])
    merged = (mixed[...] + forward(4) + forward(5) + forward(6) + forward(7)).astype(BF)
    step(sums[:2])
    step(sums[2:])
    text_in.wait()
    covered = jnp.max(place[...].astype(F32), axis=1, keepdims=True) > 0.5
    lm_out[...] = jnp.where(covered, dot(place[...], merged), text[...].astype(F32)).astype(BF)
    lm_done.start()
    step(sums[:2])
    for m in zh_mail + [core_mail]:
        m.finish()
    step(sums[:2])

    lm_done.wait()
    for m in rs_mail:
        m.finish()


def per_device(patches, gain, window_dest, window_pos, fc1, fc2, text_embeds, lm_grad):
    vm = pl.BlockSpec(memory_space=pltpu.VMEM)
    anywhere = pl.BlockSpec(memory_space=pl.ANY)
    sm = pl.BlockSpec(memory_space=pltpu.SMEM)
    V = pltpu.VMEM
    D = pltpu.SemaphoreType.DMA
    scratch = [
        V((LM, OUT), BF),
        V((LM, OUT), BF),
        V((LM, OUT), BF),
        D((3,)),
        V((NZ, 8, NTOK), F32),
        V((NDP, 1, 128), jnp.int32),
        V((NZ, 1, FEAT), F32),
        V((NTOK, FEAT), F32),
        V((NZ, NTOK, FEAT), BF),
        V((2, SRC * WIN, 128), F32),
        V((NDP, TOK, FEAT), BF),
        V((NDP, TOK, FEAT), BF),
        V((NDP, TOK, FEAT), BF),
        V((NDP, TOK, FEAT), BF),
        V((NZ, NTOK, FEAT), BF),
        V((4, 2, 4, 160, HID), BF),
        V((4, 4, 2, 80, OUT), BF),
        V((NTOK, OUT), BF),
        V((LM, NTOK), BF),
        V((HID, NTOK), F32),
        V((NZ, 2, 2, 80, NTOK), BF),
        V((NZ, HID, NTOK), BF),
        V((8, HID, NTOK), BF),
        V((NTOK, HPAD), BF),
        V((NTOK, OUT), F32),
        V((4, 4, 160, HID), BF),
        V((4, 4, 80, OUT), BF),
        V((NZ, 2, 80, NTOK), BF),
        V((NTOK, OUT), BF),
        V((NTOK, HPAD), BF),
        V((4, NTOK, FEAT), BF),
        V((2, 4, 48, HID), BF),
        V((2, 4, 32, HID), BF),
        V((2, 2, 4, 80, HID), BF),
        V((2, 48, HID), BF),
        V((2, 32, HID), BF),
        V((2, 2, 80, HID), BF),
        V((2, 2, 4, 80, 256), BF),
        V((2, 2, 4, 80, 512), BF),
        V((2, 2, 80, 256), BF),
        V((2, 2, 80, 512), BF),
        D((110,)), D((2,)), D((2,)), D((4, 2)),
        D((4, 9)), D((2, 8)), D((2, 8)), D((2, 8)), D((14,)), D((4, 20)),
    ]
    return pl.pallas_call(
        body,
        out_shape=(
            pltpu.VMEM((LM, OUT), BF),
            pltpu.VMEM((160, HID), F32),
            pltpu.VMEM((80, OUT), F32),
        ),
        in_specs=[vm, vm, sm, sm, vm, vm, anywhere, anywhere],
        out_specs=(anywhere, vm, vm),
        scratch_shapes=scratch,
        compiler_params=pltpu.CompilerParams(
            collective_id=0, has_side_effects=True, vmem_limit_bytes=60 * 1024 * 1024
        ),
        cost_estimate=pl.CostEstimate(
            flops=6_000_000_000, bytes_accessed=8_000_000, transcendentals=300_000
        ),
    )(patches.T, gain, window_dest, window_pos, fc1, fc2, text_embeds, lm_grad)


def solution(mesh):
    both = P("dp", "tensor")
    return jax.shard_map(
        per_device,
        mesh=mesh,
        in_specs=(both, P(), P("dp"), P("dp"), both, both, both, both),
        out_specs=(both, both, both),
        check_vma=False,
    )
```

```python
import functools

import jax
import jax.numpy as jnp
from jax import lax
from jax.experimental import pallas as pl
from jax.experimental.pallas import tpu as pltpu
from jax.sharding import PartitionSpec as P

MESH = pl.DeviceIdType.MESH
BF = jnp.bfloat16
F32 = jnp.float32
DM = 1280
NDP = 32
NZ = 8
SRC = 24
WORK = 16
TOK = 16
FEAT = 640
WIN = 64
HID = 320
HPAD = 384
LM = 512
OUT = 1024
NTOK = WORK * TOK


def dot(a, b, da=1, db=0):
    return lax.dot_general(a, b, (((da,), (db,)), ((), ())), preferred_element_type=F32)


def iota(shape, axis):
    return lax.broadcasted_iota(jnp.int32, shape, axis)


def turn(v, k, n):
    return lax.rem(v + (k % n), n)


class Half:
    def __init__(self, kind, h, y, x, c, t):
        self.kind, self.h, self.y, self.x, self.c, self.t = kind, h, y, x, c, t
        self.q = x if h == 0 else y
        self.r = y if h == 0 else x

    def dev(self, y, x, c):
        return (y * 8 + x * 2 + c, self.t)

    def first(self, k):
        if self.h == 0:
            return self.dev(self.y, turn(self.x, k, 4), self.c)
        return self.dev(turn(self.y, k, 4), self.x, self.c)

    def second(self, k):
        if self.h == 0:
            return self.dev(turn(self.y, k, 4), self.x, self.c)
        return self.dev(self.y, turn(self.x, k, 4), self.c)

    def sibling(self):
        return self.dev(self.y, self.x, 1 - self.c)

    def cut(self, s):
        if self.kind == 2:
            start = 512 * self.h + (256 if s == 1 else 0)
            return pl.ds(0, 80), pl.ds(start, 512 if s is None else 256)
        start = 80 * self.h + (48 if s == 1 else 0)
        return pl.ds(start, {None: 80, 0: 48, 1: 32}[s]), pl.ds(0, HID)

    def at(self, buf, y, x, c, s):
        rows, cols = self.cut(s)
        if self.kind == 2:
            return buf.at[y, x, c, rows, cols]
        return buf.at[x, c, y, rows, cols]

    def block(self, buf, k, s=None):
        p = turn(self.q, k, 4)
        if self.h == 0:
            return self.at(buf, self.y, p, self.c, s)
        return self.at(buf, p, self.x, self.c, s)

    def cell(self, buf, g, b, s=None):
        y, x = turn(self.r, g, 4), turn(self.q, b, 4)
        if self.h == 1:
            y, x = x, y
        rows, cols = self.cut(s)
        if self.kind == 2:
            return buf.at[y, x, rows, cols]
        return buf.at[x, y, rows, cols]

    def group(self, buf, k, s=None, other=False):
        p = turn(self.r, k, 4)
        c = 1 - self.c if other else self.c
        if self.h == 0:
            return self.at(buf, p, slice(None), c, s)
        return self.at(buf, slice(None), p, c, s)


class Mail:
    def __init__(self, pool, first, recv, *totals):
        self.pool, self.first, self.r, self.totals = pool, first, recv, totals

    def make(self, src, dst, lot, i, device):
        return pltpu.make_async_remote_copy(
            src_ref=src,
            dst_ref=dst,
            send_sem=self.pool.at[self.first + lot],
            recv_sem=self.r.at[i],
            device_id=device,
            device_id_type=MESH,
        )

    def send(self, src, dst, i, device, lot=0):
        self.make(src, dst, lot, i, device).start()

    def wait(self, dst, i, device):
        self.make(dst, dst, 0, i, device).wait_recv()

    def finish(self, device):
        for lot, view in enumerate(self.totals):
            self.make(view, view, lot, 0, device).wait_send()


def plane_gather(hf, buf, mail):
    def send(ref, i, device, lot=0):
        mail.send(ref, ref, i, device, lot)

    def wait(ref, i):
        mail.wait(ref, i, hf.sibling())

    send(hf.block(buf, 0), 0, hf.first(1), 0)
    send(hf.block(buf, 0), 1, hf.first(-1), 0)
    yield
    wait(hf.block(buf, -1), 0)
    send(hf.block(buf, -1, 0), 2, hf.first(1), 0)
    wait(hf.block(buf, 1), 1)
    send(hf.block(buf, 1, 1), 3, hf.first(-1), 0)
    yield
    wait(hf.block(buf, 2, 0), 2)
    wait(hf.block(buf, 2, 1), 3)
    send(hf.group(buf, 0), 4, hf.second(1), 2)
    send(hf.group(buf, 0), 5, hf.second(-1), 2)
    send(hf.group(buf, 0), 6, hf.sibling(), 2)
    yield
    wait(hf.group(buf, -1), 4)
    send(hf.group(buf, -1, 0), 7, hf.second(1), 1)
    send(hf.group(buf, -1), 6, hf.sibling(), 2)
    wait(hf.group(buf, 1), 5)
    send(hf.group(buf, 1, 1), 8, hf.second(-1), 1)
    send(hf.group(buf, 1), 6, hf.sibling(), 2)
    yield
    wait(hf.group(buf, 2, 0), 7)
    wait(hf.group(buf, 2, 1), 8)
    send(hf.group(buf, 2), 6, hf.sibling(), 2)
    yield
    wait(hf.at(buf, slice(None), slice(None), 1 - hf.c, None), 6)
    yield


def ring_sums(hf, buf, room, mail, put):
    sub0, sub1, full, last0, last1, last = room
    order = (2, 1, -1, 0)

    def wait(ref, i):
        mail.wait(ref, i, hf.sibling())

    def plus(mine, *others):
        total = mine[...].astype(F32)
        for o in others:
            total = total + o[...].astype(F32)
        mine[...] = total.astype(BF)

    for n, b in enumerate(order):
        mail.send(hf.cell(buf, 2, b, 0), sub0.at[n], n, hf.second(1))
        mail.send(hf.cell(buf, 2, b, 1), sub1.at[n], 4 + n, hf.second(-1))
    yield
    for n, b in enumerate(order):
        wait(sub0.at[n], n)
        plus(hf.cell(buf, 1, b, 0), sub0.at[n])
        mail.send(hf.cell(buf, 1, b), full.at[0, n], 8 + n, hf.second(1))
        wait(sub1.at[n], 4 + n)
        plus(hf.cell(buf, -1, b, 1), sub1.at[n])
        mail.send(hf.cell(buf, -1, b), full.at[1, n], 12 + n, hf.second(-1))
    yield
    for n in (0, 1, 2):
        wait(full.at[0, n], 8 + n)
        wait(full.at[1, n], 12 + n)
        plus(hf.cell(buf, 0, order[n]), full.at[0, n], full.at[1, n])
        if n == 0:
            mail.send(hf.cell(buf, 0, 2, 0), last0, 16, hf.first(1), 1)
            mail.send(hf.cell(buf, 0, 2, 1), last1, 17, hf.first(-1), 1)
    yield
    wait(last0, 16)
    plus(hf.cell(buf, 0, 1, 0), last0)
    mail.send(hf.cell(buf, 0, 1), last.at[0], 18, hf.first(1), 1)
    wait(last1, 17)
    plus(hf.cell(buf, 0, -1, 1), last1)
    mail.send(hf.cell(buf, 0, -1), last.at[1], 19, hf.first(-1), 1)
    yield
    wait(full.at[0, 3], 11)
    wait(full.at[1, 3], 15)
    wait(last.at[0], 18)
    wait(last.at[1], 19)
    total = hf.cell(buf, 0, 0)[...].astype(F32)
    for part in (full[0, 3], full[1, 3], last[0], last[1]):
        total = total + part.astype(F32)
    put(total)
    yield


def group_sums(hf, buf, room, mail, put):
    sub0, sub1, full, last0, last1, last = room

    def wait(ref, i):
        mail.wait(ref, i, hf.sibling())

    def row(g, s=None):
        rows, cols = hf.cut(s)
        p = turn(hf.r, g, 4)
        if hf.h == 0:
            return buf.at[:, p, rows, cols]
        return buf.at[p, :, rows, cols]

    def plus(mine, *others):
        total = mine[...].astype(F32)
        for o in others:
            total = total + o[...].astype(F32)
        mine[...] = total.astype(BF)

    mail.send(row(2, 0), sub0, 0, hf.second(1))
    mail.send(row(2, 1), sub1, 1, hf.second(-1))
    yield
    wait(sub0, 0)
    plus(row(1, 0), sub0)
    mail.send(row(1), full.at[0], 2, hf.second(1))
    wait(sub1, 1)
    plus(row(-1, 1), sub1)
    mail.send(row(-1), full.at[1], 3, hf.second(-1))
    yield
    wait(full.at[0], 2)
    wait(full.at[1], 3)
    for b in (2, 1, -1):
        q = turn(hf.q, b, 4)
        plus(hf.cell(buf, 0, b), full.at[0, q], full.at[1, q])
        if b == 2:
            mail.send(hf.cell(buf, 0, 2, 0), last0, 4, hf.first(1), 1)
            mail.send(hf.cell(buf, 0, 2, 1), last1, 5, hf.first(-1), 1)
    yield
    wait(last0, 4)
    plus(hf.cell(buf, 0, 1, 0), last0)
    mail.send(hf.cell(buf, 0, 1), last.at[0], 6, hf.first(1), 1)
    wait(last1, 5)
    plus(hf.cell(buf, 0, -1, 1), last1)
    mail.send(hf.cell(buf, 0, -1), last.at[1], 7, hf.first(-1), 1)
    yield
    wait(last.at[0], 6)
    wait(last.at[1], 7)
    total = hf.cell(buf, 0, 0)[...].astype(F32)
    for part in (full[0, hf.q], full[1, hf.q], last[0], last[1]):
        total = total + part.astype(F32)
    put(total)
    yield


def ring_gather(dp, t, buf, cuts, mail):
    up, down = (dp, turn(t, 1, NZ)), (dp, turn(t, -1, NZ))

    def view(k, cut):
        return buf.at[(turn(t, k, NZ),) + cut]

    def send(k, cut, i, device):
        mail.send(view(k, cut), view(k, cut), i, device)

    def wait(k, cut, i):
        mail.wait(view(k, cut), i, up)

    whole, one, two = cuts
    send(0, whole, 0, up)
    send(0, whole, 1, down)
    yield (0,)
    for k in (1, 2):
        wait(-k, whole, 2 * k - 2)
        send(-k, whole, 2 * k, up)
        wait(k, whole, 2 * k - 1)
        send(k, whole, 2 * k + 1, down)
        yield (-k, k)
    wait(-3, whole, 4)
    send(-3, one, 6, up)
    wait(3, whole, 5)
    send(3, two, 7, down)
    yield (-3, 3)
    wait(4, one, 6)
    wait(4, two, 7)
    yield (4,)


def ring_scatter(dp, t, buf, room, cols, mail, put):
    up, down = (dp, turn(t, 1, NZ)), (dp, turn(t, -1, NZ))
    half = HID // 2
    low, high, every = pl.ds(0, half), pl.ds(half, half), pl.ds(0, HID)

    def view(k, cut):
        return buf.at[turn(t, k, NZ), cut, cols]

    def plus(k, cut, other):
        mine = view(k, cut)
        mine[...] = (mine[...].astype(F32) + other[...].astype(F32)).astype(BF)

    mail.send(view(4, low), room.at[0, low, cols], 0, up)
    mail.send(view(4, high), room.at[1, high, cols], 1, down)
    yield
    for n, k in enumerate((3, 2, 1)):
        a, b = (low, high) if n == 0 else (every, every)
        mail.wait(room.at[2 * n, a, cols], 2 * n, up)
        plus(k, a, room.at[2 * n, a, cols])
        mail.send(view(k, every), room.at[2 * n + 2, every, cols], 2 * n + 2, up)
        mail.wait(room.at[2 * n + 1, b, cols], 2 * n + 1, up)
        plus(-k, b, room.at[2 * n + 1, b, cols])
        mail.send(view(-k, every), room.at[2 * n + 3, every, cols], 2 * n + 3, down)
        yield
    mail.wait(room.at[6, every, cols], 6, up)
    mail.wait(room.at[7, every, cols], 7, up)
    put(
        view(0, every)[...].astype(F32)
        + room[6, :, cols].astype(F32)
        + room[7, :, cols].astype(F32)
    )
    yield


def body(
    patches_t, gain, dest, pos, fc1, fc2, text_hbm, lmg_hbm,
    lm_hbm, g1_out, g2_out,
    text, lmg, lm_out, io_s,
    sq, meta, gains, factor, xn, flat, st1, rv1, st2, rv2, xs, f1, f2, up_rows, place,
    acc, hid, hb, hb_room, dz, mixed, p1, p2, hid2, up2, dz2, x2,
    a_sub0, a_sub1, a_full, a_last0, a_last1, a_last,
    b_sub, b_full, b_lasts, b_last,
    pool, sq_s, meta_s, hop_s, ag_r, zx_r, zh_r, zb_r, co_r, rs_r, rs_q,
):
    dp = lax.axis_index("dp")
    t = lax.axis_index("tensor")
    y, x, c = lax.div(dp, 8), lax.rem(lax.div(dp, 2), 4), lax.rem(dp, 2)
    sibling = (y * 8 + x * 2 + 1 - c, t)

    text_in = pltpu.make_async_copy(text_hbm, text, io_s.at[0])
    lmg_in = pltpu.make_async_copy(lmg_hbm, lmg, io_s.at[1])
    lm_done = pltpu.make_async_copy(lm_out, lm_hbm, io_s.at[2])

    barrier = pltpu.get_barrier_semaphore()

    def greet(k, carry):
        pl.semaphore_signal(
            barrier, inc=1, device_id=(lax.rem(dp + k, NDP), t), device_id_type=MESH
        )
        return carry

    lax.fori_loop(1, NDP, greet, 0)

    def greet_z(k, carry):
        pl.semaphore_signal(
            barrier, inc=1, device_id=(dp, lax.rem(t + k, NZ)), device_id_type=MESH
        )
        return carry

    lax.fori_loop(1, NZ, greet_z, 0)

    lmg_in.start()
    text_in.start()

    q = iota((1, 128), 1)
    table = jnp.full((1, 128), -1, jnp.int32)
    for s in range(SRC):
        table = jnp.where(q == s, jnp.where(dest[s] >= 0, (dest[s] << 14) + pos[s], -1), table)
    meta[dp] = table
    f2[y, x, c] = fc2[...]
    f1[x, c, y] = fc1[...]

    def selector(count, key):
        n = key.shape[1]
        r, q = iota((count, n), 0), iota((count, n), 1)
        hit = ((r >> 4).astype(F32) == key) & ((r & 15) == (q & 15))
        return jnp.where(hit, 1.0, 0.0).astype(BF)

    def widen(column, n):
        k = column.shape[0]
        return jnp.sum(
            jnp.where(iota((k, n), 0) == (iota((k, n), 1) >> 4), column, 0.0), axis=0, keepdims=True
        )

    value = patches_t[...].astype(F32)
    flat[0] = value[:128].T
    flat[1] = jnp.concatenate([value[128:], jnp.zeros((96, SRC * WIN), F32)], axis=0).T
    pieces = []
    for p in range(4):
        pieces.append(flat[0, pl.ds(p, SRC * TOK, stride=4), :])
        pieces.append(flat[1, pl.ds(p, SRC * TOK, stride=4), :][:, :32])
    windows = jnp.concatenate(pieces, axis=1).astype(BF)
    slots = jnp.sum(
        jnp.where(iota((32, 128), 0) == iota((32, 128), 1), (table >> 14).astype(F32), 0.0),
        axis=1,
        keepdims=True,
    )
    to_dest = selector(NDP * TOK, widen(slots, SRC * TOK))
    st1[...] = dot(to_dest, windows).astype(BF).reshape(NDP, TOK, FEAT)
    rv1[dp] = st1[dp]

    pl.semaphore_wait(barrier, NDP - 1 + NZ - 1)

    def spread(copy, many):
        def start(k, carry):
            copy(k, lax.rem(dp + k, NDP)).start()
            return carry

        return (
            functools.partial(lax.fori_loop, 1, NDP, start, 0),
            lambda: many().wait_recv(),
            lambda: many().wait_send(),
        )

    def push(src, dst, sems, device):
        return pltpu.make_async_remote_copy(
            src_ref=src, dst_ref=dst, send_sem=sems.at[0], recv_sem=sems.at[1],
            device_id=device, device_id_type=MESH,
        )

    others = pl.ds(0, NDP - 1)
    meta_start, meta_arrive, meta_sent = spread(
        lambda k, j: push(meta.at[dp], meta.at[dp], meta_s, (j, t)),
        lambda: push(meta.at[others], meta.at[others], meta_s, sibling),
    )

    chunks = (pl.ds(0, 256), pl.ds(256, 384))

    def hop(n, m, src, dst):
        cols, sems = chunks[m], hop_s.at[2 * n + m]
        return spread(
            lambda k, j: push(src.at[j, :, cols], dst.at[dp, :, cols], sems, (j, t)),
            lambda: push(src.at[others, :, cols], dst.at[others, :, cols], sems, sibling),
        )

    hops = [
        [hop(n, m, src, dst) for m in (0, 1)]
        for n, (src, dst) in enumerate(((st1, rv1), (st2, rv2)))
    ]

    meta_start()
    hops[0][0][0]()
    hops[0][1][0]()

    halves = [Half(kind, h, y, x, c, t) for kind in (2, 1) for h in (0, 1)]
    ag_mail = []
    for n, hf in enumerate(halves):
        buf = f2 if hf.kind == 2 else f1
        three, all4 = pl.ds(0, 3), slice(None)
        ag_mail.append(
            Mail(
                pool, 3 * n, ag_r.at[n],
                hf.at(buf, 0, three, 0, None), hf.at(buf, 0, all4, 0, None), hf.at(buf, all4, three, all4, None),
            )
        )
    gathers = [
        plane_gather(hf, f2 if hf.kind == 2 else f1, m) for hf, m in zip(halves, ag_mail)
    ]

    def step(generators):
        for g in generators:
            next(g)

    step(gathers)

    meta_arrive()
    tables = meta[:, 0, :]
    dests, places = tables >> 14, tables & 16383
    owners = jnp.where(tables >= 0, places >> 9, -1)
    onward = (
        jnp.sum(jnp.where(dests == dp, (owners + 1).astype(F32), 0.0), axis=1, keepdims=True) - 1.0
    )
    to_owner = selector(NDP * TOK, widen(onward, NDP * TOK))
    via = jnp.where(owners == dp, dests, -1)
    next_place = (places + 1).astype(F32)
    r, q = iota((32, 128), 0), iota((32, 128), 1)
    found = jnp.zeros((32, 128), F32)
    for d in range(NDP):
        found = jnp.where(
            r == d, jnp.sum(jnp.where(via == d, next_place, 0.0), axis=0, keepdims=True), found
        )
    found = jnp.sum(found, axis=1, keepdims=True)
    live = jnp.where(found > 0.5, 1.0, 0.0)
    live_row = jnp.sum(jnp.where(r == q, live, 0.0), axis=0, keepdims=True)
    rank = jnp.sum(jnp.where(q < r, live_row, 0.0), axis=1, keepdims=True)
    rank = jnp.where(found > 0.5, rank, -1.0)
    rank_row = jnp.sum(jnp.where(r == q, rank, 0.0), axis=0, keepdims=True)
    rank_row = jnp.where(iota((1, 128), 1) < NDP, rank_row, -1.0)
    found_row = jnp.sum(jnp.where(r == q, found, 0.0), axis=0, keepdims=True)
    to_work = selector(NTOK, widen(rank, NDP * TOK))

    base = dp * LM + 1
    r, q = iota((32, NTOK), 0), iota((32, NTOK), 1)
    tok_row = jnp.sum(jnp.where(rank == (q >> 4).astype(F32), found, 0.0), axis=0, keepdims=True)
    tok_row = tok_row.astype(jnp.int32) + (iota((1, NTOK), 1) & 15) - base
    r = iota((NTOK, 128), 0)
    tok_col = jnp.sum(
        jnp.where(rank_row == (r >> 4).astype(F32), found_row, 0.0), axis=1, keepdims=True
    )
    tok_col = tok_col.astype(jnp.int32) + (iota((NTOK, 1), 0) & 15) - base
    fetch = jnp.where(iota((NTOK, LM), 1) == tok_col, 1.0, 0.0).astype(BF)
    place[...] = jnp.where(iota((LM, NTOK), 0) == tok_row, 1.0, 0.0).astype(BF)


    for m, cols in enumerate(chunks):
        hops[0][m][1]()
        part = rv1[:, :, cols].reshape(NDP * TOK, cols.size)
        st2[:, :, cols] = dot(to_owner, part).astype(BF).reshape(NDP, TOK, cols.size)
        hops[1][m][0]()
        rv2[dp, :, cols] = st2[dp, :, cols]
    step(gathers)
    lmg_in.wait()
    up_rows[...] = dot(fetch, lmg[...]).astype(BF)
    core_mail = Mail(pool, 18, co_r, hid2, up_rows, dz, x2)
    core_mail.send(up_rows, up2, 8, sibling, 1)
    all_gain = gain[...].reshape(1, DM)
    for k in range(NZ):
        gains[k] = jnp.concatenate([all_gain[:, 160 * k : 160 * k + 160]] * 4, axis=1)

    low, high, every = pl.ds(0, 128), pl.ds(128, 128), pl.ds(0, 256)
    seven_of = pl.ds(0, 7)
    zx_mail = [
        Mail(pool, 12 + m, zx_r.at[m], xs.at[seven_of, :, cols]) for m, cols in enumerate(chunks)
    ]
    zx = [
        ring_gather(dp, t, xs, ((every, cols), (low, cols), (high, cols)), zx_mail[m])
        for m, cols in enumerate(chunks)
    ]

    def arrive(m):
        cols = chunks[m]
        hops[1][m][1]()
        part = rv2[:, :, cols].reshape(NDP * TOK, cols.size)
        xs[t, :, cols] = dot(to_work, part).astype(BF)

    arrive(0)
    step(zx[:1])
    step(gathers[:2])
    arrive(1)

    seg = iota((NTOK, FEAT), 1) // 160
    square = xs[t].astype(F32)
    square = square * square
    lane = iota((NTOK, 128), 1)
    sums_of = jnp.zeros((NTOK, 128), F32)
    for p in range(4):
        part = jnp.sum(jnp.where(seg == p, square, 0.0), axis=1, keepdims=True)
        sums_of = jnp.where(lane == p, part, sums_of)
    sq[t] = sums_of.T[:8]
    for k in range(1, NZ):
        push(sq.at[t], sq.at[t], sq_s, (dp, lax.rem(t + k, NZ))).start()
    seven = push(sq.at[pl.ds(0, NZ - 1)], sq.at[pl.ds(0, NZ - 1)], sq_s, sibling)
    step(zx[1:])

    step(zx)
    step(gathers[:2])
    step(gathers[2:])
    seven.wait_recv()
    scale = lax.rsqrt(jnp.sum(sq[...], axis=0) * (1.0 / DM) + 1e-06)
    scale = jnp.concatenate([scale] * 16, axis=0).T
    factor[...] = jnp.where(
        seg == 0,
        scale[:, 0:1],
        jnp.where(seg == 1, scale[:, 1:2], jnp.where(seg == 2, scale[:, 2:3], scale[:, 3:4])),
    )

    def normalise(k):
        j = turn(t, k, NZ)
        xn[j] = (xs[j].astype(F32) * factor[...] * gains[j]).astype(BF)

    normalise(0)
    step(zx)
    step(gathers[:2])
    step(gathers[2:])
    normalise(-1)
    normalise(1)
    step(gathers[:2])

    def second_rows(k):
        two = lax.rem(k, 2) * 2
        return f2[lax.div(k, 2), pl.ds(two, 2)].reshape(HID, OUT)

    def back(*ks):
        for k in ks:
            j = turn(t, k, NZ)
            hb[j] = dot(second_rows(j), up_rows[...], 1, 1).astype(BF)

    tokens = (low, high)
    zb_mail = [
        Mail(pool, 14 + m, zb_r.at[m], hb.at[seven_of, :, cut]) for m, cut in enumerate(tokens)
    ]

    def put_back(m):
        def put(total):
            acc[:, 128 * m : 128 * m + 128] = total

        return put

    zb = [
        ring_scatter(dp, t, hb, hb_room, tokens[m], zb_mail[m], put_back(m)) for m in (0, 1)
    ]
    back(4)
    step(zb)
    back(3, -3, 2, -2, 1, -1, 0)

    def first_part(k):
        j = turn(t, k, NZ)
        w = f1[lax.div(j, 2), lax.rem(j, 2)].reshape(FEAT, HID)
        return dot(xn[j], w)

    step(zx)
    normalise(-2)
    normalise(2)
    step(gathers[2:])
    step(zb)
    normalise(-3)
    normalise(3)
    meta_sent()
    seven.wait_send()
    for n in (0, 1):
        for m in (0, 1):
            hops[n][m][2]()
    step(gathers[2:])
    z1 = first_part(0) + first_part(-1) + first_part(1) + first_part(-2)
    z1 = z1 + first_part(2) + first_part(-3) + first_part(3)
    step(zx)
    normalise(4)
    for xx in range(4):
        core_mail.send(xn.at[xx * 2 + 1 - c], x2.at[xx], 10 + xx, sibling, 3)
    z1 = z1 + first_part(4)
    z1 = jnp.concatenate([z1, jnp.zeros((NTOK, HPAD - HID), F32)], axis=1).T[:HID]
    cdf = 0.5 * (1.0 + lax.erf(z1 * 0.7071067811865476))
    hid[t] = (z1 * cdf).astype(BF).reshape(2, 2, 80, NTOK)

    zh_mail = [
        Mail(pool, 16 + m, zh_r.at[m], hid.at[seven_of, :, :, :, cut]) for m, cut in enumerate(tokens)
    ]
    full = slice(None)
    zh = [
        ring_gather(
            dp, t, hid,
            ((full, full, full, cut), (pl.ds(0, 1), full, full, cut), (pl.ds(1, 1), full, full, cut)),
            zh_mail[m],
        )
        for m, cut in enumerate(tokens)
    ]
    order = (0, -1, 1, -2, 2, -3, 3, 4)

    def share(*ks):
        for k in ks:
            j = turn(t, k, NZ)
            core_mail.send(hid.at[j, :, 1 - c], hid2.at[j], order.index(k), sibling)

    def use_hidden(*ks):
        for k in ks:
            j = turn(t, k, NZ)
            mine = dot(hid[j, :, c].reshape(160, NTOK), up_rows[...])
            core_mail.wait(hid2.at[j], order.index(k), sibling)
            term = mine + dot(hid2[j].reshape(160, NTOK), up2[...])
            p2[lax.div(j, 2), pl.ds(lax.rem(j, 2) * 2, 2)] = term.astype(BF).reshape(2, 80, OUT)

    def grad1(xx):
        mine = dot(xn[xx * 2 + c], dz[:, :HID], 0, 0)
        if xx == 0:
            core_mail.wait(dz2, 9, sibling)
        core_mail.wait(x2.at[xx], 10 + xx, sibling)
        p1[xx] = (mine + dot(x2[xx], dz2[:, :HID], 0, 0)).astype(BF).reshape(4, 160, HID)

    rs_mail = []
    for n, hf in enumerate(halves):
        buf = p2 if hf.kind == 2 else p1
        rows, cols = hf.cut(None)
        rs_mail.append(
            Mail(
                pool, 22 + 2 * n, (rs_r if hf.kind == 2 else rs_q).at[hf.h],
                buf.at[:, three, rows, cols], buf.at[0, three, rows, cols],
            )
        )

    def put2(h):
        def put(total):
            g2_out[:, 512 * h : 512 * h + 512] = total

        return put

    def put1(h):
        def put(total):
            g1_out[80 * h : 80 * h + 80, :] = total

        return put

    sums = []
    for n, hf in enumerate(halves):
        h = hf.h
        if hf.kind == 2:
            room = (b_sub.at[h, 0], b_sub.at[h, 1], b_full.at[h],
                    b_lasts.at[h, 0], b_lasts.at[h, 1], b_last.at[h])
            sums.append(ring_sums(hf, p2, room, rs_mail[n], put2(h)))
        else:
            room = (a_sub0.at[h], a_sub1.at[h], a_full.at[h],
                    a_last0.at[h], a_last1.at[h], a_last.at[h])
            sums.append(group_sums(hf, p1, room, rs_mail[n], put1(h)))
    def forward(k):
        return dot(hid[k].reshape(HID, NTOK), second_rows(k), 0, 0)

    step(zh)
    share(0)
    step(zb)
    slope = cdf + z1 * (jnp.exp(-0.5 * z1 * z1) * 0.3989422804014327)
    core_mail.wait(up2, 8, sibling)
    use_hidden(0)
    step(zh)
    share(-1, 1)
    step(zb)
    use_hidden(-1, 1)
    step(zh)
    share(-2, 2)
    step(zb)
    dz_t = acc[...] * slope
    dz[...] = jnp.concatenate([dz_t, jnp.zeros((HPAD - HID, NTOK), F32)], axis=0).T.astype(BF)
    core_mail.send(dz, dz2, 9, sibling, 2)
    use_hidden(-2, 2)
    step(zh)
    share(-3, 3)
    for xx in range(4):
        grad1(xx)
    step(sums[2:])
    use_hidden(-3, 3)
    step(zh)
    share(4)
    step(sums[2:])
    use_hidden(4)
    step(sums[:2])
    step(sums[2:])
    mixed[...] = forward(0) + forward(1) + forward(2) + forward(3)
    step(sums[:2])
    step(sums[2:])
    merged = (mixed[...] + forward(4) + forward(5) + forward(6) + forward(7)).astype(BF)
    step(sums[:2])
    step(sums[2:])
    text_in.wait()
    covered = jnp.max(place[...].astype(F32), axis=1, keepdims=True) > 0.5
    lm_out[...] = jnp.where(covered, dot(place[...], merged), text[...].astype(F32)).astype(BF)
    lm_done.start()
    step(sums[:2])
    step(sums[:2])

    lm_done.wait()
    for m in ag_mail + zx_mail + zb_mail + zh_mail + [core_mail] + rs_mail:
        m.finish(sibling)


def per_device(patches, gain, window_dest, window_pos, fc1, fc2, text_embeds, lm_grad):
    vm = pl.BlockSpec(memory_space=pltpu.VMEM)
    anywhere = pl.BlockSpec(memory_space=pl.ANY)
    sm = pl.BlockSpec(memory_space=pltpu.SMEM)
    V = pltpu.VMEM
    D = pltpu.SemaphoreType.DMA
    scratch = [
        V((LM, OUT), BF),
        V((LM, OUT), BF),
        V((LM, OUT), BF),
        D((3,)),
        V((NZ, 8, NTOK), F32),
        V((NDP, 1, 128), jnp.int32),
        V((NZ, 1, FEAT), F32),
        V((NTOK, FEAT), F32),
        V((NZ, NTOK, FEAT), BF),
        V((2, SRC * WIN, 128), F32),
        V((NDP, TOK, FEAT), BF),
        V((NDP, TOK, FEAT), BF),
        V((NDP, TOK, FEAT), BF),
        V((NDP, TOK, FEAT), BF),
        V((NZ, NTOK, FEAT), BF),
        V((4, 2, 4, 160, HID), BF),
        V((4, 4, 2, 80, OUT), BF),
        V((NTOK, OUT), BF),
        V((LM, NTOK), BF),
        V((HID, NTOK), F32),
        V((NZ, 2, 2, 80, NTOK), BF),
        V((NZ, HID, NTOK), BF),
        V((8, HID, NTOK), BF),
        V((NTOK, HPAD), BF),
        V((NTOK, OUT), F32),
        V((4, 4, 160, HID), BF),
        V((4, 4, 80, OUT), BF),
        V((NZ, 2, 80, NTOK), BF),
        V((NTOK, OUT), BF),
        V((NTOK, HPAD), BF),
        V((4, NTOK, FEAT), BF),
        V((2, 4, 48, HID), BF),
        V((2, 4, 32, HID), BF),
        V((2, 2, 4, 80, HID), BF),
        V((2, 48, HID), BF),
        V((2, 32, HID), BF),
        V((2, 2, 80, HID), BF),
        V((2, 2, 4, 80, 256), BF),
        V((2, 2, 4, 80, 512), BF),
        V((2, 2, 80, 256), BF),
        V((2, 2, 80, 512), BF),
        D((30,)), D((2,)), D((2,)), D((4, 2)),
        D((4, 9)), D((2, 8)), D((2, 8)), D((2, 8)), D((14,)), D((2, 20)), D((2, 8)),
    ]
    return pl.pallas_call(
        body,
        out_shape=(
            pltpu.VMEM((LM, OUT), BF),
            pltpu.VMEM((160, HID), F32),
            pltpu.VMEM((80, OUT), F32),
        ),
        in_specs=[vm, vm, sm, sm, vm, vm, anywhere, anywhere],
        out_specs=(anywhere, vm, vm),
        scratch_shapes=scratch,
        compiler_params=pltpu.CompilerParams(
            collective_id=0, has_side_effects=True, vmem_limit_bytes=60 * 1024 * 1024
        ),
        cost_estimate=pl.CostEstimate(
            flops=6_000_000_000, bytes_accessed=8_000_000, transcendentals=300_000
        ),
    )(patches.T, gain, window_dest, window_pos, fc1, fc2, text_embeds, lm_grad)


def solution(mesh):
    both = P("dp", "tensor")
    return jax.shard_map(
        per_device,
        mesh=mesh,
        in_specs=(both, P(), P("dp"), P("dp"), both, both, both, both),
        out_specs=(both, both, both),
        check_vma=False,
    )
```

```python
import functools

import jax
import jax.numpy as jnp
from jax import lax
from jax.experimental import pallas as pl
from jax.experimental.pallas import tpu as pltpu
from jax.sharding import PartitionSpec as P

MESH = pl.DeviceIdType.MESH
BF = jnp.bfloat16
F32 = jnp.float32
DM = 1280
NDP = 32
NZ = 8
SRC = 24
WORK = 16
TOK = 16
FEAT = 640
WIN = 64
HID = 320
HPAD = 384
LM = 512
OUT = 1024
NTOK = WORK * TOK


def dot(a, b, da=1, db=0):
    return lax.dot_general(a, b, (((da,), (db,)), ((), ())), preferred_element_type=F32)


def iota(shape, axis):
    return lax.broadcasted_iota(jnp.int32, shape, axis)


def turn(v, k, n):
    return lax.rem(v + (k % n), n)


class Half:
    def __init__(self, kind, h, y, x, c, t):
        self.kind, self.h, self.y, self.x, self.c, self.t = kind, h, y, x, c, t
        self.q = x if h == 0 else y
        self.r = y if h == 0 else x

    def dev(self, y, x, c):
        return (y * 8 + x * 2 + c, self.t)

    def first(self, k):
        if self.h == 0:
            return self.dev(self.y, turn(self.x, k, 4), self.c)
        return self.dev(turn(self.y, k, 4), self.x, self.c)

    def second(self, k):
        if self.h == 0:
            return self.dev(turn(self.y, k, 4), self.x, self.c)
        return self.dev(self.y, turn(self.x, k, 4), self.c)

    def sibling(self):
        return self.dev(self.y, self.x, 1 - self.c)

    def cut(self, s):
        if self.kind == 2:
            start = 512 * self.h + (256 if s == 1 else 0)
            return pl.ds(0, 80), pl.ds(start, 512 if s is None else 256)
        start = 80 * self.h + (48 if s == 1 else 0)
        return pl.ds(start, {None: 80, 0: 48, 1: 32}[s]), pl.ds(0, HID)

    def at(self, buf, y, x, c, s):
        rows, cols = self.cut(s)
        if self.kind == 2:
            return buf.at[y, x, c, rows, cols]
        return buf.at[x, c, y, rows, cols]

    def block(self, buf, k, s=None):
        p = turn(self.q, k, 4)
        if self.h == 0:
            return self.at(buf, self.y, p, self.c, s)
        return self.at(buf, p, self.x, self.c, s)

    def cell(self, buf, g, b, s=None):
        y, x = turn(self.r, g, 4), turn(self.q, b, 4)
        if self.h == 1:
            y, x = x, y
        rows, cols = self.cut(s)
        if self.kind == 2:
            return buf.at[y, x, rows, cols]
        return buf.at[x, y, rows, cols]

    def group(self, buf, k, s=None, other=False):
        p = turn(self.r, k, 4)
        c = 1 - self.c if other else self.c
        if self.h == 0:
            return self.at(buf, p, slice(None), c, s)
        return self.at(buf, slice(None), p, c, s)


class Mail:
    def __init__(self, pool, first, recv, *totals):
        self.pool, self.first, self.r, self.totals = pool, first, recv, totals

    def make(self, src, dst, lot, i, device):
        return pltpu.make_async_remote_copy(
            src_ref=src,
            dst_ref=dst,
            send_sem=self.pool.at[self.first + lot],
            recv_sem=self.r.at[i],
            device_id=device,
            device_id_type=MESH,
        )

    def send(self, src, dst, i, device, lot=0):
        self.make(src, dst, lot, i, device).start()

    def wait(self, dst, i, device):
        self.make(dst, dst, 0, i, device).wait_recv()

    def finish(self, device):
        for lot, view in enumerate(self.totals):
            self.make(view, view, lot, 0, device).wait_send()


def plane_gather(hf, buf, mail):
    def send(ref, i, device, lot=0):
        mail.send(ref, ref, i, device, lot)

    def wait(ref, i):
        mail.wait(ref, i, hf.sibling())

    send(hf.block(buf, 0), 0, hf.first(1), 0)
    send(hf.block(buf, 0), 1, hf.first(-1), 0)
    yield
    wait(hf.block(buf, -1), 0)
    send(hf.block(buf, -1, 0), 2, hf.first(1), 0)
    wait(hf.block(buf, 1), 1)
    send(hf.block(buf, 1, 1), 3, hf.first(-1), 0)
    yield
    wait(hf.block(buf, 2, 0), 2)
    wait(hf.block(buf, 2, 1), 3)
    send(hf.group(buf, 0), 4, hf.second(1), 2)
    send(hf.group(buf, 0), 5, hf.second(-1), 2)
    send(hf.group(buf, 0), 6, hf.sibling(), 2)
    yield
    wait(hf.group(buf, -1), 4)
    send(hf.group(buf, -1, 0), 7, hf.second(1), 1)
    send(hf.group(buf, -1), 6, hf.sibling(), 2)
    wait(hf.group(buf, 1), 5)
    send(hf.group(buf, 1, 1), 8, hf.second(-1), 1)
    send(hf.group(buf, 1), 6, hf.sibling(), 2)
    yield
    wait(hf.group(buf, 2, 0), 7)
    wait(hf.group(buf, 2, 1), 8)
    send(hf.group(buf, 2), 6, hf.sibling(), 2)
    yield
    wait(hf.at(buf, slice(None), slice(None), 1 - hf.c, None), 6)
    yield


def ring_sums(hf, buf, room, mail, put):
    sub0, sub1, full, last0, last1, last = room
    order = (2, 1, -1, 0)

    def wait(ref, i):
        mail.wait(ref, i, hf.sibling())

    def plus(mine, *others):
        total = mine[...].astype(F32)
        for o in others:
            total = total + o[...].astype(F32)
        mine[...] = total.astype(BF)

    for n, b in enumerate(order):
        mail.send(hf.cell(buf, 2, b, 0), sub0.at[n], n, hf.second(1))
        mail.send(hf.cell(buf, 2, b, 1), sub1.at[n], 4 + n, hf.second(-1))
    yield
    for n, b in enumerate(order):
        wait(sub0.at[n], n)
        plus(hf.cell(buf, 1, b, 0), sub0.at[n])
        mail.send(hf.cell(buf, 1, b), full.at[0, n], 8 + n, hf.second(1))
        wait(sub1.at[n], 4 + n)
        plus(hf.cell(buf, -1, b, 1), sub1.at[n])
        mail.send(hf.cell(buf, -1, b), full.at[1, n], 12 + n, hf.second(-1))
    yield
    for n in (0, 1, 2):
        wait(full.at[0, n], 8 + n)
        wait(full.at[1, n], 12 + n)
        plus(hf.cell(buf, 0, order[n]), full.at[0, n], full.at[1, n])
        if n == 0:
            mail.send(hf.cell(buf, 0, 2, 0), last0, 16, hf.first(1), 1)
            mail.send(hf.cell(buf, 0, 2, 1), last1, 17, hf.first(-1), 1)
    yield
    wait(last0, 16)
    plus(hf.cell(buf, 0, 1, 0), last0)
    mail.send(hf.cell(buf, 0, 1), last.at[0], 18, hf.first(1), 1)
    wait(last1, 17)
    plus(hf.cell(buf, 0, -1, 1), last1)
    mail.send(hf.cell(buf, 0, -1), last.at[1], 19, hf.first(-1), 1)
    yield
    wait(full.at[0, 3], 11)
    wait(full.at[1, 3], 15)
    wait(last.at[0], 18)
    wait(last.at[1], 19)
    total = hf.cell(buf, 0, 0)[...].astype(F32)
    for part in (full[0, 3], full[1, 3], last[0], last[1]):
        total = total + part.astype(F32)
    put(total)
    yield


def group_sums(hf, buf, room, mail, put):
    sub0, sub1, full, last0, last1, last = room

    def wait(ref, i):
        mail.wait(ref, i, hf.sibling())

    def row(g, s=None):
        rows, cols = hf.cut(s)
        p = turn(hf.r, g, 4)
        if hf.h == 0:
            return buf.at[:, p, rows, cols]
        return buf.at[p, :, rows, cols]

    def plus(mine, *others):
        total = mine[...].astype(F32)
        for o in others:
            total = total + o[...].astype(F32)
        mine[...] = total.astype(BF)

    mail.send(row(2, 0), sub0, 0, hf.second(1))
    mail.send(row(2, 1), sub1, 1, hf.second(-1))
    yield
    wait(sub0, 0)
    plus(row(1, 0), sub0)
    mail.send(row(1), full.at[0], 2, hf.second(1))
    wait(sub1, 1)
    plus(row(-1, 1), sub1)
    mail.send(row(-1), full.at[1], 3, hf.second(-1))
    yield
    wait(full.at[0], 2)
    wait(full.at[1], 3)
    for b in (2, 1, -1):
        q = turn(hf.q, b, 4)
        plus(hf.cell(buf, 0, b), full.at[0, q], full.at[1, q])
        if b == 2:
            mail.send(hf.cell(buf, 0, 2, 0), last0, 4, hf.first(1), 1)
            mail.send(hf.cell(buf, 0, 2, 1), last1, 5, hf.first(-1), 1)
    yield
    wait(last0, 4)
    plus(hf.cell(buf, 0, 1, 0), last0)
    mail.send(hf.cell(buf, 0, 1), last.at[0], 6, hf.first(1), 1)
    wait(last1, 5)
    plus(hf.cell(buf, 0, -1, 1), last1)
    mail.send(hf.cell(buf, 0, -1), last.at[1], 7, hf.first(-1), 1)
    yield
    wait(last.at[0], 6)
    wait(last.at[1], 7)
    total = hf.cell(buf, 0, 0)[...].astype(F32)
    for part in (full[0, hf.q], full[1, hf.q], last[0], last[1]):
        total = total + part.astype(F32)
    put(total)
    yield


def ring_gather(dp, t, buf, cuts, mail):
    up, down = (dp, turn(t, 1, NZ)), (dp, turn(t, -1, NZ))

    def view(k, cut):
        return buf.at[(turn(t, k, NZ),) + cut]

    def send(k, cut, i, device):
        mail.send(view(k, cut), view(k, cut), i, device)

    def wait(k, cut, i):
        mail.wait(view(k, cut), i, up)

    whole, one, two = cuts
    send(0, whole, 0, up)
    send(0, whole, 1, down)
    yield (0,)
    for k in (1, 2):
        wait(-k, whole, 2 * k - 2)
        send(-k, whole, 2 * k, up)
        wait(k, whole, 2 * k - 1)
        send(k, whole, 2 * k + 1, down)
        yield (-k, k)
    wait(-3, whole, 4)
    send(-3, one, 6, up)
    wait(3, whole, 5)
    send(3, two, 7, down)
    yield (-3, 3)
    wait(4, one, 6)
    wait(4, two, 7)
    yield (4,)


def ring_scatter(dp, t, buf, room, cols, mail, put):
    up, down = (dp, turn(t, 1, NZ)), (dp, turn(t, -1, NZ))
    half = HID // 2
    low, high, every = pl.ds(0, half), pl.ds(half, half), pl.ds(0, HID)

    def view(k, cut):
        return buf.at[turn(t, k, NZ), cut, cols]

    def plus(k, cut, other):
        mine = view(k, cut)
        mine[...] = (mine[...].astype(F32) + other[...].astype(F32)).astype(BF)

    mail.send(view(4, low), room.at[0, low, cols], 0, up)
    mail.send(view(4, high), room.at[1, high, cols], 1, down)
    yield
    for n, k in enumerate((3, 2, 1)):
        a, b = (low, high) if n == 0 else (every, every)
        mail.wait(room.at[2 * n, a, cols], 2 * n, up)
        plus(k, a, room.at[2 * n, a, cols])
        mail.send(view(k, every), room.at[2 * n + 2, every, cols], 2 * n + 2, up)
        mail.wait(room.at[2 * n + 1, b, cols], 2 * n + 1, up)
        plus(-k, b, room.at[2 * n + 1, b, cols])
        mail.send(view(-k, every), room.at[2 * n + 3, every, cols], 2 * n + 3, down)
        yield
    mail.wait(room.at[6, every, cols], 6, up)
    mail.wait(room.at[7, every, cols], 7, up)
    put(
        view(0, every)[...].astype(F32)
        + room[6, :, cols].astype(F32)
        + room[7, :, cols].astype(F32)
    )
    yield


def body(
    patches_hbm, gain, dest, pos, fc1, fc2, text_hbm, lmg_hbm,
    lm_hbm, g1_out, g2_out,
    patches_t, text, lmg, lm_out, io_s,
    sq, meta, gains, factor, xn, flat, st1, rv1, st2, rv2, xs, f1, f2, up_rows, place,
    acc, hid, hb, hb_room, dz, mixed, p1, p2, hid2, up2, dz2, x2,
    a_sub0, a_sub1, a_full, a_last0, a_last1, a_last,
    b_sub, b_full, b_lasts, b_last,
    pool, sq_s, meta_s, hop_s, ag_r, zx_r, zh_r, zb_r, co_r, rs_r, rs_q,
):
    dp = lax.axis_index("dp")
    t = lax.axis_index("tensor")
    y, x, c = lax.div(dp, 8), lax.rem(lax.div(dp, 2), 4), lax.rem(dp, 2)
    sibling = (y * 8 + x * 2 + 1 - c, t)

    text_in = pltpu.make_async_copy(text_hbm, text, io_s.at[0])
    lmg_in = pltpu.make_async_copy(lmg_hbm, lmg, io_s.at[1])
    lm_done = pltpu.make_async_copy(lm_out, lm_hbm, io_s.at[2])

    barrier = pltpu.get_barrier_semaphore()

    def greet(k, carry):
        pl.semaphore_signal(
            barrier, inc=1, device_id=(lax.rem(dp + k, NDP), t), device_id_type=MESH
        )
        return carry

    lax.fori_loop(1, NDP, greet, 0)

    def greet_z(k, carry):
        pl.semaphore_signal(
            barrier, inc=1, device_id=(dp, lax.rem(t + k, NZ)), device_id_type=MESH
        )
        return carry

    lax.fori_loop(1, NZ, greet_z, 0)

    patches_in = pltpu.make_async_copy(patches_hbm, patches_t, io_s.at[3])
    fc2_in = pltpu.make_async_copy(fc2, f2.at[y, x, c], io_s.at[4])
    fc1_in = pltpu.make_async_copy(fc1, f1.at[x, c, y], io_s.at[5])
    for copy in (patches_in, fc2_in, fc1_in, lmg_in, text_in):
        copy.start()

    q = iota((1, 128), 1)
    table = jnp.full((1, 128), -1, jnp.int32)
    for s in range(SRC):
        table = jnp.where(q == s, jnp.where(dest[s] >= 0, (dest[s] << 14) + pos[s], -1), table)
    meta[dp] = table

    def selector(count, key):
        n = key.shape[1]
        r, q = iota((count, n), 0), iota((count, n), 1)
        hit = ((r >> 4).astype(F32) == key) & ((r & 15) == (q & 15))
        return jnp.where(hit, 1.0, 0.0).astype(BF)

    def widen(column, n):
        k = column.shape[0]
        return jnp.sum(
            jnp.where(iota((k, n), 0) == (iota((k, n), 1) >> 4), column, 0.0), axis=0, keepdims=True
        )

    patches_in.wait()
    value = patches_t[...].astype(F32)
    flat[0] = value[:128].T
    flat[1] = jnp.concatenate([value[128:], jnp.zeros((96, SRC * WIN), F32)], axis=0).T
    pieces = []
    for p in range(4):
        pieces.append(flat[0, pl.ds(p, SRC * TOK, stride=4), :])
        pieces.append(flat[1, pl.ds(p, SRC * TOK, stride=4), :][:, :32])
    windows = jnp.concatenate(pieces, axis=1).astype(BF)
    slots = jnp.sum(
        jnp.where(iota((32, 128), 0) == iota((32, 128), 1), (table >> 14).astype(F32), 0.0),
        axis=1,
        keepdims=True,
    )
    to_dest = selector(NDP * TOK, widen(slots, SRC * TOK))
    st1[...] = dot(to_dest, windows).astype(BF).reshape(NDP, TOK, FEAT)
    rv1[dp] = st1[dp]

    pl.semaphore_wait(barrier, NDP - 1 + NZ - 1)

    def spread(copy, many):
        def start(k, carry):
            copy(k, lax.rem(dp + k, NDP)).start()
            return carry

        return (
            functools.partial(lax.fori_loop, 1, NDP, start, 0),
            lambda: many().wait_recv(),
            lambda: many().wait_send(),
        )

    def push(src, dst, sems, device):
        return pltpu.make_async_remote_copy(
            src_ref=src, dst_ref=dst, send_sem=sems.at[0], recv_sem=sems.at[1],
            device_id=device, device_id_type=MESH,
        )

    others = pl.ds(0, NDP - 1)
    meta_start, meta_arrive, meta_sent = spread(
        lambda k, j: push(meta.at[dp], meta.at[dp], meta_s, (j, t)),
        lambda: push(meta.at[others], meta.at[others], meta_s, sibling),
    )

    chunks = (pl.ds(0, 256), pl.ds(256, 384))

    def hop(n, m, src, dst):
        cols, sems = chunks[m], hop_s.at[2 * n + m]
        return spread(
            lambda k, j: push(src.at[j, :, cols], dst.at[dp, :, cols], sems, (j, t)),
            lambda: push(src.at[others, :, cols], dst.at[others, :, cols], sems, sibling),
        )

    hops = [
        [hop(n, m, src, dst) for m in (0, 1)]
        for n, (src, dst) in enumerate(((st1, rv1), (st2, rv2)))
    ]

    meta_start()
    hops[0][0][0]()
    hops[0][1][0]()

    halves = [Half(kind, h, y, x, c, t) for kind in (2, 1) for h in (0, 1)]
    fc2_in.wait()
    fc1_in.wait()
    ag_mail = []
    for n, hf in enumerate(halves):
        buf = f2 if hf.kind == 2 else f1
        three, all4 = pl.ds(0, 3), slice(None)
        ag_mail.append(
            Mail(
                pool, 3 * n, ag_r.at[n],
                hf.at(buf, 0, three, 0, None), hf.at(buf, 0, all4, 0, None), hf.at(buf, all4, three, all4, None),
            )
        )
    gathers = [
        plane_gather(hf, f2 if hf.kind == 2 else f1, m) for hf, m in zip(halves, ag_mail)
    ]

    def step(generators):
        for g in generators:
            next(g)

    step(gathers)

    meta_arrive()
    tables = meta[:, 0, :]
    dests, places = tables >> 14, tables & 16383
    owners = jnp.where(tables >= 0, places >> 9, -1)
    onward = (
        jnp.sum(jnp.where(dests == dp, (owners + 1).astype(F32), 0.0), axis=1, keepdims=True) - 1.0
    )
    to_owner = selector(NDP * TOK, widen(onward, NDP * TOK))
    via = jnp.where(owners == dp, dests, -1)
    next_place = (places + 1).astype(F32)
    r, q = iota((32, 128), 0), iota((32, 128), 1)
    found = jnp.zeros((32, 128), F32)
    for d in range(NDP):
        found = jnp.where(
            r == d, jnp.sum(jnp.where(via == d, next_place, 0.0), axis=0, keepdims=True), found
        )
    found = jnp.sum(found, axis=1, keepdims=True)
    live = jnp.where(found > 0.5, 1.0, 0.0)
    live_row = jnp.sum(jnp.where(r == q, live, 0.0), axis=0, keepdims=True)
    rank = jnp.sum(jnp.where(q < r, live_row, 0.0), axis=1, keepdims=True)
    rank = jnp.where(found > 0.5, rank, -1.0)
    rank_row = jnp.sum(jnp.where(r == q, rank, 0.0), axis=0, keepdims=True)
    rank_row = jnp.where(iota((1, 128), 1) < NDP, rank_row, -1.0)
    found_row = jnp.sum(jnp.where(r == q, found, 0.0), axis=0, keepdims=True)
    to_work = selector(NTOK, widen(rank, NDP * TOK))

    base = dp * LM + 1
    r, q = iota((32, NTOK), 0), iota((32, NTOK), 1)
    tok_row = jnp.sum(jnp.where(rank == (q >> 4).astype(F32), found, 0.0), axis=0, keepdims=True)
    tok_row = tok_row.astype(jnp.int32) + (iota((1, NTOK), 1) & 15) - base
    r = iota((NTOK, 128), 0)
    tok_col = jnp.sum(
        jnp.where(rank_row == (r >> 4).astype(F32), found_row, 0.0), axis=1, keepdims=True
    )
    tok_col = tok_col.astype(jnp.int32) + (iota((NTOK, 1), 0) & 15) - base
    fetch = jnp.where(iota((NTOK, LM), 1) == tok_col, 1.0, 0.0).astype(BF)
    place[...] = jnp.where(iota((LM, NTOK), 0) == tok_row, 1.0, 0.0).astype(BF)


    for m, cols in enumerate(chunks):
        hops[0][m][1]()
        part = rv1[:, :, cols].reshape(NDP * TOK, cols.size)
        st2[:, :, cols] = dot(to_owner, part).astype(BF).reshape(NDP, TOK, cols.size)
        hops[1][m][0]()
        rv2[dp, :, cols] = st2[dp, :, cols]
    step(gathers)
    lmg_in.wait()
    up_rows[...] = dot(fetch, lmg[...]).astype(BF)
    core_mail = Mail(pool, 18, co_r, hid2, up_rows, dz, x2)
    core_mail.send(up_rows, up2, 8, sibling, 1)
    all_gain = gain[...].reshape(1, DM)
    for k in range(NZ):
        gains[k] = jnp.concatenate([all_gain[:, 160 * k : 160 * k + 160]] * 4, axis=1)

    low, high, every = pl.ds(0, 128), pl.ds(128, 128), pl.ds(0, 256)
    seven_of = pl.ds(0, 7)
    zx_mail = [
        Mail(pool, 12 + m, zx_r.at[m], xs.at[seven_of, :, cols]) for m, cols in enumerate(chunks)
    ]
    zx = [
        ring_gather(dp, t, xs, ((every, cols), (low, cols), (high, cols)), zx_mail[m])
        for m, cols in enumerate(chunks)
    ]

    def arrive(m):
        cols = chunks[m]
        hops[1][m][1]()
        part = rv2[:, :, cols].reshape(NDP * TOK, cols.size)
        xs[t, :, cols] = dot(to_work, part).astype(BF)

    arrive(0)
    step(zx[:1])
    step(gathers[:2])
    arrive(1)

    seg = iota((NTOK, FEAT), 1) // 160
    square = xs[t].astype(F32)
    square = square * square
    lane = iota((NTOK, 128), 1)
    sums_of = jnp.zeros((NTOK, 128), F32)
    for p in range(4):
        part = jnp.sum(jnp.where(seg == p, square, 0.0), axis=1, keepdims=True)
        sums_of = jnp.where(lane == p, part, sums_of)
    sq[t] = sums_of.T[:8]
    for k in range(1, NZ):
        push(sq.at[t], sq.at[t], sq_s, (dp, lax.rem(t + k, NZ))).start()
    seven = push(sq.at[pl.ds(0, NZ - 1)], sq.at[pl.ds(0, NZ - 1)], sq_s, sibling)
    step(zx[1:])

    step(zx)
    step(gathers[:2])
    step(gathers[2:])
    seven.wait_recv()
    scale = lax.rsqrt(jnp.sum(sq[...], axis=0) * (1.0 / DM) + 1e-06)
    scale = jnp.concatenate([scale] * 16, axis=0).T
    factor[...] = jnp.where(
        seg == 0,
        scale[:, 0:1],
        jnp.where(seg == 1, scale[:, 1:2], jnp.where(seg == 2, scale[:, 2:3], scale[:, 3:4])),
    )

    def normalise(k):
        j = turn(t, k, NZ)
        xn[j] = (xs[j].astype(F32) * factor[...] * gains[j]).astype(BF)

    normalise(0)
    step(zx)
    step(gathers[:2])
    step(gathers[2:])
    normalise(-1)
    normalise(1)
    step(gathers[:2])

    def second_rows(k):
        two = lax.rem(k, 2) * 2
        return f2[lax.div(k, 2), pl.ds(two, 2)].reshape(HID, OUT)

    def back(*ks):
        for k in ks:
            j = turn(t, k, NZ)
            hb[j] = dot(second_rows(j), up_rows[...], 1, 1).astype(BF)

    tokens = (low, high)
    zb_mail = [
        Mail(pool, 14 + m, zb_r.at[m], hb.at[seven_of, :, cut]) for m, cut in enumerate(tokens)
    ]

    def put_back(m):
        def put(total):
            acc[:, 128 * m : 128 * m + 128] = total

        return put

    zb = [
        ring_scatter(dp, t, hb, hb_room, tokens[m], zb_mail[m], put_back(m)) for m in (0, 1)
    ]
    back(4)
    step(zb)
    back(3, -3, 2, -2, 1, -1, 0)

    def first_part(k):
        j = turn(t, k, NZ)
        w = f1[lax.div(j, 2), lax.rem(j, 2)].reshape(FEAT, HID)
        return dot(xn[j], w)

    step(zx)
    normalise(-2)
    normalise(2)
    step(gathers[2:])
    step(zb)
    normalise(-3)
    normalise(3)
    meta_sent()
    seven.wait_send()
    for n in (0, 1):
        for m in (0, 1):
            hops[n][m][2]()
    step(gathers[2:])
    z1 = first_part(0) + first_part(-1) + first_part(1) + first_part(-2)
    z1 = z1 + first_part(2) + first_part(-3) + first_part(3)
    step(zx)
    normalise(4)
    for xx in range(4):
        core_mail.send(xn.at[xx * 2 + 1 - c], x2.at[xx], 10 + xx, sibling, 3)
    z1 = z1 + first_part(4)
    z1 = jnp.concatenate([z1, jnp.zeros((NTOK, HPAD - HID), F32)], axis=1).T[:HID]
    cdf = 0.5 * (1.0 + lax.erf(z1 * 0.7071067811865476))
    hid[t] = (z1 * cdf).astype(BF).reshape(2, 2, 80, NTOK)

    zh_mail = [
        Mail(pool, 16 + m, zh_r.at[m], hid.at[seven_of, :, :, :, cut]) for m, cut in enumerate(tokens)
    ]
    full = slice(None)
    zh = [
        ring_gather(
            dp, t, hid,
            ((full, full, full, cut), (pl.ds(0, 1), full, full, cut), (pl.ds(1, 1), full, full, cut)),
            zh_mail[m],
        )
        for m, cut in enumerate(tokens)
    ]
    order = (0, -1, 1, -2, 2, -3, 3, 4)

    def share(*ks):
        for k in ks:
            j = turn(t, k, NZ)
            core_mail.send(hid.at[j, :, 1 - c], hid2.at[j], order.index(k), sibling)

    def use_hidden(*ks):
        for k in ks:
            j = turn(t, k, NZ)
            mine = dot(hid[j, :, c].reshape(160, NTOK), up_rows[...])
            core_mail.wait(hid2.at[j], order.index(k), sibling)
            term = mine + dot(hid2[j].reshape(160, NTOK), up2[...])
            p2[lax.div(j, 2), pl.ds(lax.rem(j, 2) * 2, 2)] = term.astype(BF).reshape(2, 80, OUT)

    def grad1(xx):
        mine = dot(xn[xx * 2 + c], dz[:, :HID], 0, 0)
        if xx == 0:
            core_mail.wait(dz2, 9, sibling)
        core_mail.wait(x2.at[xx], 10 + xx, sibling)
        p1[xx] = (mine + dot(x2[xx], dz2[:, :HID], 0, 0)).astype(BF).reshape(4, 160, HID)

    rs_mail = []
    for n, hf in enumerate(halves):
        buf = p2 if hf.kind == 2 else p1
        rows, cols = hf.cut(None)
        rs_mail.append(
            Mail(
                pool, 22 + 2 * n, (rs_r if hf.kind == 2 else rs_q).at[hf.h],
                buf.at[:, three, rows, cols], buf.at[0, three, rows, cols],
            )
        )

    def put2(h):
        def put(total):
            g2_out[:, 512 * h : 512 * h + 512] = total

        return put

    def put1(h):
        def put(total):
            g1_out[80 * h : 80 * h + 80, :] = total

        return put

    sums = []
    for n, hf in enumerate(halves):
        h = hf.h
        if hf.kind == 2:
            room = (b_sub.at[h, 0], b_sub.at[h, 1], b_full.at[h],
                    b_lasts.at[h, 0], b_lasts.at[h, 1], b_last.at[h])
            sums.append(ring_sums(hf, p2, room, rs_mail[n], put2(h)))
        else:
            room = (a_sub0.at[h], a_sub1.at[h], a_full.at[h],
                    a_last0.at[h], a_last1.at[h], a_last.at[h])
            sums.append(group_sums(hf, p1, room, rs_mail[n], put1(h)))
    def forward(k):
        return dot(hid[k].reshape(HID, NTOK), second_rows(k), 0, 0)

    step(zh)
    share(0)
    step(zb)
    slope = cdf + z1 * (jnp.exp(-0.5 * z1 * z1) * 0.3989422804014327)
    core_mail.wait(up2, 8, sibling)
    use_hidden(0)
    step(zh)
    share(-1, 1)
    step(zb)
    use_hidden(-1, 1)
    step(zh)
    share(-2, 2)
    step(zb)
    dz_t = acc[...] * slope
    dz[...] = jnp.concatenate([dz_t, jnp.zeros((HPAD - HID, NTOK), F32)], axis=0).T.astype(BF)
    core_mail.send(dz, dz2, 9, sibling, 2)
    use_hidden(-2, 2)
    step(zh)
    share(-3, 3)
    for xx in range(4):
        grad1(xx)
    step(sums[2:])
    use_hidden(-3, 3)
    step(zh)
    share(4)
    use_hidden(4)
    step(sums[:2])
    step(sums[2:])
    mixed[...] = forward(0) + forward(1) + forward(2) + forward(3)
    step(sums[:2])
    step(sums[2:])
    merged = (mixed[...] + forward(4) + forward(5) + forward(6) + forward(7)).astype(BF)
    step(sums[:2])
    step(sums[2:])
    text_in.wait()
    covered = jnp.max(place[...].astype(F32), axis=1, keepdims=True) > 0.5
    lm_out[...] = jnp.where(covered, dot(place[...], merged), text[...].astype(F32)).astype(BF)
    lm_done.start()
    step(sums[:2])
    step(sums[2:])
    step(sums[:2])

    lm_done.wait()
    for m in ag_mail + zx_mail + zb_mail + zh_mail + [core_mail] + rs_mail:
        m.finish(sibling)


def per_device(patches, gain, window_dest, window_pos, fc1, fc2, text_embeds, lm_grad):
    vm = pl.BlockSpec(memory_space=pltpu.VMEM)
    anywhere = pl.BlockSpec(memory_space=pl.ANY)
    sm = pl.BlockSpec(memory_space=pltpu.SMEM)
    V = pltpu.VMEM
    D = pltpu.SemaphoreType.DMA
    scratch = [
        V((160, SRC * WIN), BF),
        V((LM, OUT), BF),
        V((LM, OUT), BF),
        V((LM, OUT), BF),
        D((6,)),
        V((NZ, 8, NTOK), F32),
        V((NDP, 1, 128), jnp.int32),
        V((NZ, 1, FEAT), F32),
        V((NTOK, FEAT), F32),
        V((NZ, NTOK, FEAT), BF),
        V((2, SRC * WIN, 128), F32),
        V((NDP, TOK, FEAT), BF),
        V((NDP, TOK, FEAT), BF),
        V((NDP, TOK, FEAT), BF),
        V((NDP, TOK, FEAT), BF),
        V((NZ, NTOK, FEAT), BF),
        V((4, 2, 4, 160, HID), BF),
        V((4, 4, 2, 80, OUT), BF),
        V((NTOK, OUT), BF),
        V((LM, NTOK), BF),
        V((HID, NTOK), F32),
        V((NZ, 2, 2, 80, NTOK), BF),
        V((NZ, HID, NTOK), BF),
        V((8, HID, NTOK), BF),
        V((NTOK, HPAD), BF),
        V((NTOK, OUT), F32),
        V((4, 4, 160, HID), BF),
        V((4, 4, 80, OUT), BF),
        V((NZ, 2, 80, NTOK), BF),
        V((NTOK, OUT), BF),
        V((NTOK, HPAD), BF),
        V((4, NTOK, FEAT), BF),
        V((2, 4, 48, HID), BF),
        V((2, 4, 32, HID), BF),
        V((2, 2, 4, 80, HID), BF),
        V((2, 48, HID), BF),
        V((2, 32, HID), BF),
        V((2, 2, 80, HID), BF),
        V((2, 2, 4, 80, 256), BF),
        V((2, 2, 4, 80, 512), BF),
        V((2, 2, 80, 256), BF),
        V((2, 2, 80, 512), BF),
        D((30,)), D((2,)), D((2,)), D((4, 2)),
        D((4, 9)), D((2, 8)), D((2, 8)), D((2, 8)), D((14,)), D((2, 20)), D((2, 8)),
    ]
    return pl.pallas_call(
        body,
        out_shape=(
            pltpu.VMEM((LM, OUT), BF),
            pltpu.VMEM((160, HID), F32),
            pltpu.VMEM((80, OUT), F32),
        ),
        in_specs=[anywhere, vm, sm, sm] + [anywhere] * 4,
        out_specs=(anywhere, vm, vm),
        scratch_shapes=scratch,
        compiler_params=pltpu.CompilerParams(
            collective_id=0, has_side_effects=True, vmem_limit_bytes=60 * 1024 * 1024
        ),
        cost_estimate=pl.CostEstimate(
            flops=6_000_000_000, bytes_accessed=8_000_000, transcendentals=300_000
        ),
    )(patches.T, gain, window_dest, window_pos, fc1, fc2, text_embeds, lm_grad)


def solution(mesh):
    both = P("dp", "tensor")
    return jax.shard_map(
        per_device,
        mesh=mesh,
        in_specs=(both, P(), P("dp"), P("dp"), both, both, both, both),
        out_specs=(both, both, both),
        check_vma=False,
    )
```

```python
import functools

import jax
import jax.numpy as jnp
from jax import lax
from jax.experimental import pallas as pl
from jax.experimental.pallas import tpu as pltpu
from jax.sharding import PartitionSpec as P

MESH = pl.DeviceIdType.MESH
BF = jnp.bfloat16
F32 = jnp.float32
DM = 1280
NDP = 32
NZ = 8
SRC = 24
WORK = 16
TOK = 16
FEAT = 640
WIN = 64
HID = 320
HPAD = 384
LM = 512
OUT = 1024
NTOK = WORK * TOK


def dot(a, b, da=1, db=0):
    return lax.dot_general(a, b, (((da,), (db,)), ((), ())), preferred_element_type=F32)


def iota(shape, axis):
    return lax.broadcasted_iota(jnp.int32, shape, axis)


def turn(v, k, n):
    return lax.rem(v + (k % n), n)


class Half:
    def __init__(self, kind, h, y, x, c, t):
        self.kind, self.h, self.y, self.x, self.c, self.t = kind, h, y, x, c, t
        self.q = x if h == 0 else y
        self.r = y if h == 0 else x

    def dev(self, y, x, c):
        return (y * 8 + x * 2 + c, self.t)

    def first(self, k):
        if self.h == 0:
            return self.dev(self.y, turn(self.x, k, 4), self.c)
        return self.dev(turn(self.y, k, 4), self.x, self.c)

    def second(self, k):
        if self.h == 0:
            return self.dev(turn(self.y, k, 4), self.x, self.c)
        return self.dev(self.y, turn(self.x, k, 4), self.c)

    def sibling(self):
        return self.dev(self.y, self.x, 1 - self.c)

    def cut(self, s):
        if self.kind == 2:
            start = 512 * self.h + (256 if s == 1 else 0)
            return pl.ds(0, 80), pl.ds(start, 512 if s is None else 256)
        start = 80 * self.h + (48 if s == 1 else 0)
        return pl.ds(start, {None: 80, 0: 48, 1: 32}[s]), pl.ds(0, HID)

    def at(self, buf, y, x, c, s):
        rows, cols = self.cut(s)
        if self.kind == 2:
            return buf.at[y, x, c, rows, cols]
        return buf.at[x, c, y, rows, cols]

    def block(self, buf, k, s=None):
        p = turn(self.q, k, 4)
        if self.h == 0:
            return self.at(buf, self.y, p, self.c, s)
        return self.at(buf, p, self.x, self.c, s)

    def cell(self, buf, g, b, s=None):
        y, x = turn(self.r, g, 4), turn(self.q, b, 4)
        if self.h == 1:
            y, x = x, y
        rows, cols = self.cut(s)
        if self.kind == 2:
            return buf.at[y, x, rows, cols]
        return buf.at[x, y, rows, cols]

    def group(self, buf, k, s=None, other=False):
        p = turn(self.r, k, 4)
        c = 1 - self.c if other else self.c
        if self.h == 0:
            return self.at(buf, p, slice(None), c, s)
        return self.at(buf, slice(None), p, c, s)


class Mail:
    def __init__(self, pool, first, recv, *totals):
        self.pool, self.first, self.r, self.totals = pool, first, recv, totals

    def make(self, src, dst, lot, i, device):
        return pltpu.make_async_remote_copy(
            src_ref=src,
            dst_ref=dst,
            send_sem=self.pool.at[self.first + lot],
            recv_sem=self.r.at[i],
            device_id=device,
            device_id_type=MESH,
        )

    def send(self, src, dst, i, device, lot=0):
        self.make(src, dst, lot, i, device).start()

    def wait(self, dst, i, device):
        self.make(dst, dst, 0, i, device).wait_recv()

    def finish(self, device):
        for lot, view in enumerate(self.totals):
            self.make(view, view, lot, 0, device).wait_send()


def plane_gather(hf, buf, mail):
    def send(ref, i, device, lot=0):
        mail.send(ref, ref, i, device, lot)

    def wait(ref, i):
        mail.wait(ref, i, hf.sibling())

    send(hf.block(buf, 0), 0, hf.first(1), 0)
    send(hf.block(buf, 0), 1, hf.first(-1), 0)
    yield
    wait(hf.block(buf, -1), 0)
    send(hf.block(buf, -1, 0), 2, hf.first(1), 0)
    wait(hf.block(buf, 1), 1)
    send(hf.block(buf, 1, 1), 3, hf.first(-1), 0)
    yield
    wait(hf.block(buf, 2, 0), 2)
    wait(hf.block(buf, 2, 1), 3)
    send(hf.group(buf, 0), 4, hf.second(1), 2)
    send(hf.group(buf, 0), 5, hf.second(-1), 2)
    send(hf.group(buf, 0), 6, hf.sibling(), 2)
    yield
    wait(hf.group(buf, -1), 4)
    send(hf.group(buf, -1, 0), 7, hf.second(1), 1)
    send(hf.group(buf, -1), 6, hf.sibling(), 2)
    wait(hf.group(buf, 1), 5)
    send(hf.group(buf, 1, 1), 8, hf.second(-1), 1)
    send(hf.group(buf, 1), 6, hf.sibling(), 2)
    yield
    wait(hf.group(buf, 2, 0), 7)
    wait(hf.group(buf, 2, 1), 8)
    send(hf.group(buf, 2), 6, hf.sibling(), 2)
    yield
    wait(hf.at(buf, slice(None), slice(None), 1 - hf.c, None), 6)
    yield


def ring_sums(hf, buf, room, mail, put):
    sub0, sub1, full, last0, last1, last = room
    order = (2, 1, -1, 0)

    def wait(ref, i):
        mail.wait(ref, i, hf.sibling())

    def plus(mine, *others):
        total = mine[...].astype(F32)
        for o in others:
            total = total + o[...].astype(F32)
        mine[...] = total.astype(BF)

    for n, b in enumerate(order):
        mail.send(hf.cell(buf, 2, b, 0), sub0.at[n], n, hf.second(1))
        mail.send(hf.cell(buf, 2, b, 1), sub1.at[n], 4 + n, hf.second(-1))
    yield
    for n, b in enumerate(order):
        wait(sub0.at[n], n)
        plus(hf.cell(buf, 1, b, 0), sub0.at[n])
        mail.send(hf.cell(buf, 1, b), full.at[0, n], 8 + n, hf.second(1))
        wait(sub1.at[n], 4 + n)
        plus(hf.cell(buf, -1, b, 1), sub1.at[n])
        mail.send(hf.cell(buf, -1, b), full.at[1, n], 12 + n, hf.second(-1))
    yield
    for n in (0, 1, 2):
        wait(full.at[0, n], 8 + n)
        wait(full.at[1, n], 12 + n)
        plus(hf.cell(buf, 0, order[n]), full.at[0, n], full.at[1, n])
        if n == 0:
            mail.send(hf.cell(buf, 0, 2, 0), last0, 16, hf.first(1), 1)
            mail.send(hf.cell(buf, 0, 2, 1), last1, 17, hf.first(-1), 1)
    yield
    wait(last0, 16)
    plus(hf.cell(buf, 0, 1, 0), last0)
    mail.send(hf.cell(buf, 0, 1), last.at[0], 18, hf.first(1), 1)
    wait(last1, 17)
    plus(hf.cell(buf, 0, -1, 1), last1)
    mail.send(hf.cell(buf, 0, -1), last.at[1], 19, hf.first(-1), 1)
    yield
    wait(full.at[0, 3], 11)
    wait(full.at[1, 3], 15)
    wait(last.at[0], 18)
    wait(last.at[1], 19)
    total = hf.cell(buf, 0, 0)[...].astype(F32)
    for part in (full[0, 3], full[1, 3], last[0], last[1]):
        total = total + part.astype(F32)
    put(total)
    yield


def group_sums(hf, buf, room, mail, put):
    sub0, sub1, full, last0, last1, last = room

    def wait(ref, i):
        mail.wait(ref, i, hf.sibling())

    def row(g, s=None):
        rows, cols = hf.cut(s)
        p = turn(hf.r, g, 4)
        if hf.h == 0:
            return buf.at[:, p, rows, cols]
        return buf.at[p, :, rows, cols]

    def plus(mine, *others):
        total = mine[...].astype(F32)
        for o in others:
            total = total + o[...].astype(F32)
        mine[...] = total.astype(BF)

    mail.send(row(2, 0), sub0, 0, hf.second(1))
    mail.send(row(2, 1), sub1, 1, hf.second(-1))
    yield
    wait(sub0, 0)
    plus(row(1, 0), sub0)
    mail.send(row(1), full.at[0], 2, hf.second(1))
    wait(sub1, 1)
    plus(row(-1, 1), sub1)
    mail.send(row(-1), full.at[1], 3, hf.second(-1))
    yield
    wait(full.at[0], 2)
    wait(full.at[1], 3)
    for b in (2, 1, -1):
        q = turn(hf.q, b, 4)
        plus(hf.cell(buf, 0, b), full.at[0, q], full.at[1, q])
        if b == 2:
            mail.send(hf.cell(buf, 0, 2, 0), last0, 4, hf.first(1), 1)
            mail.send(hf.cell(buf, 0, 2, 1), last1, 5, hf.first(-1), 1)
    yield
    wait(last0, 4)
    plus(hf.cell(buf, 0, 1, 0), last0)
    mail.send(hf.cell(buf, 0, 1), last.at[0], 6, hf.first(1), 1)
    wait(last1, 5)
    plus(hf.cell(buf, 0, -1, 1), last1)
    mail.send(hf.cell(buf, 0, -1), last.at[1], 7, hf.first(-1), 1)
    yield
    wait(last.at[0], 6)
    wait(last.at[1], 7)
    total = hf.cell(buf, 0, 0)[...].astype(F32)
    for part in (full[0, hf.q], full[1, hf.q], last[0], last[1]):
        total = total + part.astype(F32)
    put(total)
    yield


def ring_gather(dp, t, buf, cuts, mail):
    up, down = (dp, turn(t, 1, NZ)), (dp, turn(t, -1, NZ))

    def view(k, cut):
        return buf.at[(turn(t, k, NZ),) + cut]

    def send(k, cut, i, device):
        mail.send(view(k, cut), view(k, cut), i, device)

    def wait(k, cut, i):
        mail.wait(view(k, cut), i, up)

    whole, one, two = cuts
    send(0, whole, 0, up)
    send(0, whole, 1, down)
    yield (0,)
    for k in (1, 2):
        wait(-k, whole, 2 * k - 2)
        send(-k, whole, 2 * k, up)
        wait(k, whole, 2 * k - 1)
        send(k, whole, 2 * k + 1, down)
        yield (-k, k)
    wait(-3, whole, 4)
    send(-3, one, 6, up)
    wait(3, whole, 5)
    send(3, two, 7, down)
    yield (-3, 3)
    wait(4, one, 6)
    wait(4, two, 7)
    yield (4,)


def ring_scatter(dp, t, buf, room, cols, mail, put):
    up, down = (dp, turn(t, 1, NZ)), (dp, turn(t, -1, NZ))
    half = HID // 2
    low, high, every = pl.ds(0, half), pl.ds(half, half), pl.ds(0, HID)

    def view(k, cut):
        return buf.at[turn(t, k, NZ), cut, cols]

    def plus(k, cut, other):
        mine = view(k, cut)
        mine[...] = (mine[...].astype(F32) + other[...].astype(F32)).astype(BF)

    mail.send(view(4, low), room.at[0, low, cols], 0, up)
    mail.send(view(4, high), room.at[1, high, cols], 1, down)
    yield
    for n, k in enumerate((3, 2, 1)):
        a, b = (low, high) if n == 0 else (every, every)
        mail.wait(room.at[2 * n, a, cols], 2 * n, up)
        plus(k, a, room.at[2 * n, a, cols])
        mail.send(view(k, every), room.at[2 * n + 2, every, cols], 2 * n + 2, up)
        mail.wait(room.at[2 * n + 1, b, cols], 2 * n + 1, up)
        plus(-k, b, room.at[2 * n + 1, b, cols])
        mail.send(view(-k, every), room.at[2 * n + 3, every, cols], 2 * n + 3, down)
        yield
    mail.wait(room.at[6, every, cols], 6, up)
    mail.wait(room.at[7, every, cols], 7, up)
    put(
        view(0, every)[...].astype(F32)
        + room[6, :, cols].astype(F32)
        + room[7, :, cols].astype(F32)
    )
    yield


def body(
    patches_hbm, gain, dest, pos, fc1, fc2, text_hbm, lmg_hbm,
    lm_hbm, g1_out, g2_out,
    patches_t, text, lmg, lm_out, io_s,
    sq, meta, gains, factor, xn, flat, st1, rv1, st2, rv2, xs, f1, f2, up_rows, place,
    acc, hid, hb, hb_room, dz, mixed, p1, p2, hid2, up2, dz2, x2,
    a_sub0, a_sub1, a_full, a_last0, a_last1, a_last,
    b_sub, b_full, b_lasts, b_last,
    pool, sq_s, meta_s, hop_s, ag_r, zx_r, zh_r, zb_r, co_r, rs_r, rs_q,
):
    dp = lax.axis_index("dp")
    t = lax.axis_index("tensor")
    y, x, c = lax.div(dp, 8), lax.rem(lax.div(dp, 2), 4), lax.rem(dp, 2)
    sibling = (y * 8 + x * 2 + 1 - c, t)

    text_in = pltpu.make_async_copy(text_hbm, text, io_s.at[0])
    lmg_in = pltpu.make_async_copy(lmg_hbm, lmg, io_s.at[1])
    lm_done = pltpu.make_async_copy(lm_out, lm_hbm, io_s.at[2])

    barrier = pltpu.get_barrier_semaphore()

    def greet(k, carry):
        pl.semaphore_signal(
            barrier, inc=1, device_id=(lax.rem(dp + k, NDP), t), device_id_type=MESH
        )
        return carry

    lax.fori_loop(1, NDP, greet, 0)

    def greet_z(k, carry):
        pl.semaphore_signal(
            barrier, inc=1, device_id=(dp, lax.rem(t + k, NZ)), device_id_type=MESH
        )
        return carry

    lax.fori_loop(1, NZ, greet_z, 0)

    patches_in = pltpu.make_async_copy(patches_hbm, patches_t, io_s.at[3])
    fc2_in = pltpu.make_async_copy(fc2, f2.at[y, x, c], io_s.at[4])
    fc1_in = pltpu.make_async_copy(fc1, f1.at[x, c, y], io_s.at[5])
    for copy in (patches_in, fc2_in, fc1_in, lmg_in, text_in):
        copy.start()

    q = iota((1, 128), 1)
    table = jnp.full((1, 128), -1, jnp.int32)
    for s in range(SRC):
        table = jnp.where(q == s, jnp.where(dest[s] >= 0, (dest[s] << 14) + pos[s], -1), table)
    meta[dp] = table

    def selector(count, key):
        n = key.shape[1]
        r, q = iota((count, n), 0), iota((count, n), 1)
        hit = ((r >> 4).astype(F32) == key) & ((r & 15) == (q & 15))
        return jnp.where(hit, 1.0, 0.0).astype(BF)

    def widen(column, n):
        k = column.shape[0]
        return jnp.sum(
            jnp.where(iota((k, n), 0) == (iota((k, n), 1) >> 4), column, 0.0), axis=0, keepdims=True
        )

    patches_in.wait()
    value = patches_t[...].astype(F32)
    flat[0] = value[:128].T
    flat[1] = jnp.concatenate([value[128:], jnp.zeros((96, SRC * WIN), F32)], axis=0).T
    pieces = []
    for p in range(4):
        pieces.append(flat[0, pl.ds(p, SRC * TOK, stride=4), :])
        pieces.append(flat[1, pl.ds(p, SRC * TOK, stride=4), :][:, :32])
    windows = jnp.concatenate(pieces, axis=1).astype(BF)
    slots = jnp.sum(
        jnp.where(iota((32, 128), 0) == iota((32, 128), 1), (table >> 14).astype(F32), 0.0),
        axis=1,
        keepdims=True,
    )
    to_dest = selector(NDP * TOK, widen(slots, SRC * TOK))
    st1[...] = dot(to_dest, windows).astype(BF).reshape(NDP, TOK, FEAT)
    rv1[dp] = st1[dp]

    pl.semaphore_wait(barrier, NDP - 1 + NZ - 1)

    def spread(copy, many):
        def start(k, carry):
            copy(k, lax.rem(dp + k, NDP)).start()
            return carry

        return (
            functools.partial(lax.fori_loop, 1, NDP, start, 0),
            lambda: many().wait_recv(),
            lambda: many().wait_send(),
        )

    def push(src, dst, sems, device):
        return pltpu.make_async_remote_copy(
            src_ref=src, dst_ref=dst, send_sem=sems.at[0], recv_sem=sems.at[1],
            device_id=device, device_id_type=MESH,
        )

    others = pl.ds(0, NDP - 1)
    meta_start, meta_arrive, meta_sent = spread(
        lambda k, j: push(meta.at[dp], meta.at[dp], meta_s, (j, t)),
        lambda: push(meta.at[others], meta.at[others], meta_s, sibling),
    )

    chunks = (pl.ds(0, 256), pl.ds(256, 384))

    def hop(n, m, src, dst):
        cols, sems = chunks[m], hop_s.at[2 * n + m]
        return spread(
            lambda k, j: push(src.at[j, :, cols], dst.at[dp, :, cols], sems, (j, t)),
            lambda: push(src.at[others, :, cols], dst.at[others, :, cols], sems, sibling),
        )

    hops = [
        [hop(n, m, src, dst) for m in (0, 1)]
        for n, (src, dst) in enumerate(((st1, rv1), (st2, rv2)))
    ]

    meta_start()
    hops[0][0][0]()
    hops[0][1][0]()

    halves = [Half(kind, h, y, x, c, t) for kind in (2, 1) for h in (0, 1)]
    fc2_in.wait()
    fc1_in.wait()
    ag_mail = []
    for n, hf in enumerate(halves):
        buf = f2 if hf.kind == 2 else f1
        three, all4 = pl.ds(0, 3), slice(None)
        ag_mail.append(
            Mail(
                pool, 3 * n, ag_r.at[n],
                hf.at(buf, 0, three, 0, None), hf.at(buf, 0, all4, 0, None), hf.at(buf, all4, three, all4, None),
            )
        )
    gathers = [
        plane_gather(hf, f2 if hf.kind == 2 else f1, m) for hf, m in zip(halves, ag_mail)
    ]

    def step(generators):
        for g in generators:
            next(g)

    step(gathers)

    meta_arrive()
    tables = meta[:, 0, :]
    dests, places = tables >> 14, tables & 16383
    owners = jnp.where(tables >= 0, places >> 9, -1)
    onward = (
        jnp.sum(jnp.where(dests == dp, (owners + 1).astype(F32), 0.0), axis=1, keepdims=True) - 1.0
    )
    to_owner = selector(NDP * TOK, widen(onward, NDP * TOK))
    via = jnp.where(owners == dp, dests, -1)
    next_place = (places + 1).astype(F32)
    r, q = iota((32, 128), 0), iota((32, 128), 1)
    found = jnp.zeros((32, 128), F32)
    for d in range(NDP):
        found = jnp.where(
            r == d, jnp.sum(jnp.where(via == d, next_place, 0.0), axis=0, keepdims=True), found
        )
    found = jnp.sum(found, axis=1, keepdims=True)
    live = jnp.where(found > 0.5, 1.0, 0.0)
    live_row = jnp.sum(jnp.where(r == q, live, 0.0), axis=0, keepdims=True)
    rank = jnp.sum(jnp.where(q < r, live_row, 0.0), axis=1, keepdims=True)
    rank = jnp.where(found > 0.5, rank, -1.0)
    rank_row = jnp.sum(jnp.where(r == q, rank, 0.0), axis=0, keepdims=True)
    rank_row = jnp.where(iota((1, 128), 1) < NDP, rank_row, -1.0)
    found_row = jnp.sum(jnp.where(r == q, found, 0.0), axis=0, keepdims=True)
    to_work = selector(NTOK, widen(rank, NDP * TOK))

    base = dp * LM + 1
    r, q = iota((32, NTOK), 0), iota((32, NTOK), 1)
    tok_row = jnp.sum(jnp.where(rank == (q >> 4).astype(F32), found, 0.0), axis=0, keepdims=True)
    tok_row = tok_row.astype(jnp.int32) + (iota((1, NTOK), 1) & 15) - base
    r = iota((NTOK, 128), 0)
    tok_col = jnp.sum(
        jnp.where(rank_row == (r >> 4).astype(F32), found_row, 0.0), axis=1, keepdims=True
    )
    tok_col = tok_col.astype(jnp.int32) + (iota((NTOK, 1), 0) & 15) - base
    fetch = jnp.where(iota((NTOK, LM), 1) == tok_col, 1.0, 0.0).astype(BF)
    place[...] = jnp.where(iota((LM, NTOK), 0) == tok_row, 1.0, 0.0).astype(BF)


    for m, cols in enumerate(chunks):
        hops[0][m][1]()
        part = rv1[:, :, cols].reshape(NDP * TOK, cols.size)
        st2[:, :, cols] = dot(to_owner, part).astype(BF).reshape(NDP, TOK, cols.size)
        hops[1][m][0]()
        rv2[dp, :, cols] = st2[dp, :, cols]
    step(gathers)
    lmg_in.wait()
    up_rows[...] = dot(fetch, lmg[...]).astype(BF)
    core_mail = Mail(pool, 18, co_r, hid2, up_rows, dz, x2)
    core_mail.send(up_rows, up2, 8, sibling, 1)
    all_gain = gain[...].reshape(1, DM)
    for k in range(NZ):
        gains[k] = jnp.concatenate([all_gain[:, 160 * k : 160 * k + 160]] * 4, axis=1)

    low, high, every = pl.ds(0, 128), pl.ds(128, 128), pl.ds(0, 256)
    seven_of = pl.ds(0, 7)
    zx_mail = [
        Mail(pool, 12 + m, zx_r.at[m], xs.at[seven_of, :, cols]) for m, cols in enumerate(chunks)
    ]
    zx = [
        ring_gather(dp, t, xs, ((every, cols), (low, cols), (high, cols)), zx_mail[m])
        for m, cols in enumerate(chunks)
    ]

    def arrive(m):
        cols = chunks[m]
        hops[1][m][1]()
        part = rv2[:, :, cols].reshape(NDP * TOK, cols.size)
        xs[t, :, cols] = dot(to_work, part).astype(BF)

    arrive(0)
    step(zx[:1])
    step(gathers[:2])
    arrive(1)

    seg = iota((NTOK, FEAT), 1) // 160
    square = xs[t].astype(F32)
    square = square * square
    lane = iota((NTOK, 128), 1)
    sums_of = jnp.zeros((NTOK, 128), F32)
    for p in range(4):
        part = jnp.sum(jnp.where(seg == p, square, 0.0), axis=1, keepdims=True)
        sums_of = jnp.where(lane == p, part, sums_of)
    sq[t] = sums_of.T[:8]
    for k in range(1, NZ):
        push(sq.at[t], sq.at[t], sq_s, (dp, lax.rem(t + k, NZ))).start()
    seven = push(sq.at[pl.ds(0, NZ - 1)], sq.at[pl.ds(0, NZ - 1)], sq_s, sibling)
    step(zx[1:])

    step(zx)
    step(gathers[:2])
    step(gathers[2:])
    seven.wait_recv()
    scale = lax.rsqrt(jnp.sum(sq[...], axis=0) * (1.0 / DM) + 1e-06)
    scale = jnp.concatenate([scale] * 16, axis=0).T
    factor[...] = jnp.where(
        seg == 0,
        scale[:, 0:1],
        jnp.where(seg == 1, scale[:, 1:2], jnp.where(seg == 2, scale[:, 2:3], scale[:, 3:4])),
    )

    def normalise(k):
        j = turn(t, k, NZ)
        xn[j] = (xs[j].astype(F32) * factor[...] * gains[j]).astype(BF)

    normalise(0)
    step(zx)
    step(gathers[:2])
    step(gathers[2:])
    normalise(-1)
    normalise(1)
    step(gathers[:2])

    def second_rows(k):
        two = lax.rem(k, 2) * 2
        return f2[lax.div(k, 2), pl.ds(two, 2)].reshape(HID, OUT)

    def back(*ks):
        for k in ks:
            j = turn(t, k, NZ)
            hb[j] = dot(second_rows(j), up_rows[...], 1, 1).astype(BF)

    tokens = (low, high)
    zb_mail = [
        Mail(pool, 14 + m, zb_r.at[m], hb.at[seven_of, :, cut]) for m, cut in enumerate(tokens)
    ]

    def put_back(m):
        def put(total):
            acc[:, 128 * m : 128 * m + 128] = total

        return put

    zb = [
        ring_scatter(dp, t, hb, hb_room, tokens[m], zb_mail[m], put_back(m)) for m in (0, 1)
    ]
    back(4)
    step(zb)
    back(3, -3, 2, -2, 1, -1, 0)

    def first_part(k):
        j = turn(t, k, NZ)
        w = f1[lax.div(j, 2), lax.rem(j, 2)].reshape(FEAT, HID)
        return dot(xn[j], w)

    step(zx)
    normalise(-2)
    normalise(2)
    step(gathers[2:])
    step(zb)
    normalise(-3)
    normalise(3)
    meta_sent()
    seven.wait_send()
    for n in (0, 1):
        for m in (0, 1):
            hops[n][m][2]()
    step(gathers[2:])
    z1 = first_part(0) + first_part(-1) + first_part(1) + first_part(-2)
    z1 = z1 + first_part(2) + first_part(-3) + first_part(3)
    step(zx)
    normalise(4)
    for xx in range(4):
        core_mail.send(xn.at[xx * 2 + 1 - c], x2.at[xx], 10 + xx, sibling, 3)
    z1 = z1 + first_part(4)
    z1 = jnp.concatenate([z1, jnp.zeros((NTOK, HPAD - HID), F32)], axis=1).T[:HID]
    cdf = 0.5 * (1.0 + lax.erf(z1 * 0.7071067811865476))
    hid[t] = (z1 * cdf).astype(BF).reshape(2, 2, 80, NTOK)

    zh_mail = [
        Mail(pool, 16 + m, zh_r.at[m], hid.at[seven_of, :, :, :, cut]) for m, cut in enumerate(tokens)
    ]
    full = slice(None)
    zh = [
        ring_gather(
            dp, t, hid,
            ((full, full, full, cut), (pl.ds(0, 1), full, full, cut), (pl.ds(1, 1), full, full, cut)),
            zh_mail[m],
        )
        for m, cut in enumerate(tokens)
    ]
    order = (0, -1, 1, -2, 2, -3, 3, 4)

    def share(*ks):
        for k in ks:
            j = turn(t, k, NZ)
            core_mail.send(hid.at[j, :, 1 - c], hid2.at[j], order.index(k), sibling)

    def use_hidden(*ks):
        js = [turn(t, k, NZ) for k in ks]
        mine = jnp.concatenate([hid[j, :, c].reshape(160, NTOK) for j in js], axis=0)
        term = dot(mine, up_rows[...])
        for k, j in zip(ks, js):
            core_mail.wait(hid2.at[j], order.index(k), sibling)
        theirs = jnp.concatenate([hid2[j].reshape(160, NTOK) for j in js], axis=0)
        term = (term + dot(theirs, up2[...])).astype(BF)
        for n, j in enumerate(js):
            part = term[160 * n : 160 * n + 160].reshape(2, 80, OUT)
            p2[lax.div(j, 2), pl.ds(lax.rem(j, 2) * 2, 2)] = part

    def grad1(xx):
        mine = dot(xn[xx * 2 + c], dz[:, :HID], 0, 0)
        if xx == 0:
            core_mail.wait(dz2, 9, sibling)
        core_mail.wait(x2.at[xx], 10 + xx, sibling)
        p1[xx] = (mine + dot(x2[xx], dz2[:, :HID], 0, 0)).astype(BF).reshape(4, 160, HID)

    rs_mail = []
    for n, hf in enumerate(halves):
        buf = p2 if hf.kind == 2 else p1
        rows, cols = hf.cut(None)
        rs_mail.append(
            Mail(
                pool, 22 + 2 * n, (rs_r if hf.kind == 2 else rs_q).at[hf.h],
                buf.at[:, three, rows, cols], buf.at[0, three, rows, cols],
            )
        )

    def put2(h):
        def put(total):
            g2_out[:, 512 * h : 512 * h + 512] = total

        return put

    def put1(h):
        def put(total):
            g1_out[80 * h : 80 * h + 80, :] = total

        return put

    sums = []
    for n, hf in enumerate(halves):
        h = hf.h
        if hf.kind == 2:
            room = (b_sub.at[h, 0], b_sub.at[h, 1], b_full.at[h],
                    b_lasts.at[h, 0], b_lasts.at[h, 1], b_last.at[h])
            sums.append(ring_sums(hf, p2, room, rs_mail[n], put2(h)))
        else:
            room = (a_sub0.at[h], a_sub1.at[h], a_full.at[h],
                    a_last0.at[h], a_last1.at[h], a_last.at[h])
            sums.append(group_sums(hf, p1, room, rs_mail[n], put1(h)))
    def forward(k):
        return dot(hid[k].reshape(HID, NTOK), second_rows(k), 0, 0)

    step(zh)
    share(0)
    step(zb)
    slope = cdf + z1 * (jnp.exp(-0.5 * z1 * z1) * 0.3989422804014327)
    core_mail.wait(up2, 8, sibling)
    use_hidden(0)
    step(zh)
    share(-1, 1)
    step(zb)
    use_hidden(-1, 1)
    step(zh)
    share(-2, 2)
    step(zb)
    dz_t = acc[...] * slope
    dz[...] = jnp.concatenate([dz_t, jnp.zeros((HPAD - HID, NTOK), F32)], axis=0).T.astype(BF)
    core_mail.send(dz, dz2, 9, sibling, 2)
    use_hidden(-2, 2)
    step(zh)
    share(-3, 3)
    for xx in range(4):
        grad1(xx)
    step(sums[2:])
    use_hidden(-3, 3)
    step(zh)
    share(4)
    use_hidden(4)
    step(sums[:2])
    step(sums[2:])
    mixed[...] = forward(0) + forward(1) + forward(2) + forward(3)
    step(sums[:2])
    step(sums[2:])
    merged = (mixed[...] + forward(4) + forward(5) + forward(6) + forward(7)).astype(BF)
    step(sums[:2])
    step(sums[2:])
    text_in.wait()
    covered = jnp.max(place[...].astype(F32), axis=1, keepdims=True) > 0.5
    lm_out[...] = jnp.where(covered, dot(place[...], merged), text[...].astype(F32)).astype(BF)
    lm_done.start()
    step(sums[:2])
    step(sums[2:])
    step(sums[:2])

    lm_done.wait()
    for m in ag_mail + zx_mail + zb_mail + zh_mail + [core_mail] + rs_mail:
        m.finish(sibling)


def per_device(patches, gain, window_dest, window_pos, fc1, fc2, text_embeds, lm_grad):
    vm = pl.BlockSpec(memory_space=pltpu.VMEM)
    anywhere = pl.BlockSpec(memory_space=pl.ANY)
    sm = pl.BlockSpec(memory_space=pltpu.SMEM)
    V = pltpu.VMEM
    D = pltpu.SemaphoreType.DMA
    scratch = [
        V((160, SRC * WIN), BF),
        V((LM, OUT), BF),
        V((LM, OUT), BF),
        V((LM, OUT), BF),
        D((6,)),
        V((NZ, 8, NTOK), F32),
        V((NDP, 1, 128), jnp.int32),
        V((NZ, 1, FEAT), F32),
        V((NTOK, FEAT), F32),
        V((NZ, NTOK, FEAT), BF),
        V((2, SRC * WIN, 128), F32),
        V((NDP, TOK, FEAT), BF),
        V((NDP, TOK, FEAT), BF),
        V((NDP, TOK, FEAT), BF),
        V((NDP, TOK, FEAT), BF),
        V((NZ, NTOK, FEAT), BF),
        V((4, 2, 4, 160, HID), BF),
        V((4, 4, 2, 80, OUT), BF),
        V((NTOK, OUT), BF),
        V((LM, NTOK), BF),
        V((HID, NTOK), F32),
        V((NZ, 2, 2, 80, NTOK), BF),
        V((NZ, HID, NTOK), BF),
        V((8, HID, NTOK), BF),
        V((NTOK, HPAD), BF),
        V((NTOK, OUT), F32),
        V((4, 4, 160, HID), BF),
        V((4, 4, 80, OUT), BF),
        V((NZ, 2, 80, NTOK), BF),
        V((NTOK, OUT), BF),
        V((NTOK, HPAD), BF),
        V((4, NTOK, FEAT), BF),
        V((2, 4, 48, HID), BF),
        V((2, 4, 32, HID), BF),
        V((2, 2, 4, 80, HID), BF),
        V((2, 48, HID), BF),
        V((2, 32, HID), BF),
        V((2, 2, 80, HID), BF),
        V((2, 2, 4, 80, 256), BF),
        V((2, 2, 4, 80, 512), BF),
        V((2, 2, 80, 256), BF),
        V((2, 2, 80, 512), BF),
        D((30,)), D((2,)), D((2,)), D((4, 2)),
        D((4, 9)), D((2, 8)), D((2, 8)), D((2, 8)), D((14,)), D((2, 20)), D((2, 8)),
    ]
    return pl.pallas_call(
        body,
        out_shape=(
            pltpu.VMEM((LM, OUT), BF),
            pltpu.VMEM((160, HID), F32),
            pltpu.VMEM((80, OUT), F32),
        ),
        in_specs=[anywhere, vm, sm, sm] + [anywhere] * 4,
        out_specs=(anywhere, vm, vm),
        scratch_shapes=scratch,
        compiler_params=pltpu.CompilerParams(
            collective_id=0, has_side_effects=True, vmem_limit_bytes=60 * 1024 * 1024
        ),
        cost_estimate=pl.CostEstimate(
            flops=6_000_000_000, bytes_accessed=8_000_000, transcendentals=300_000
        ),
    )(patches.T, gain, window_dest, window_pos, fc1, fc2, text_embeds, lm_grad)


def solution(mesh):
    both = P("dp", "tensor")
    return jax.shard_map(
        per_device,
        mesh=mesh,
        in_specs=(both, P(), P("dp"), P("dp"), both, both, both, both),
        out_specs=(both, both, both),
        check_vma=False,
    )
```
